32 devices in a mesh: lat: 4 (over y, x), lon: 8 (over z, core).
Axes of the slice: x: 2, y: 2, z: 4, core: 2. Of those that a mesh axis runs over, the one named last changes fastest.
Arguments:
- queries: bfloat16 [32, 128, 1024], P('lat', 'lon'), may hold values from -108 to 108
- keys_values: bfloat16 [2, 32, 128, 1024], P(None, 'lat', 'lon'), may hold values from -6 to 6
- out_weight: bfloat16 [1024, 1024], replicated, may hold values from -0.1875 to 0.1875
Outputs:
- mixed: bfloat16 [32, 128, 1024], P('lat', 'lon')
The draws below stay inside these ranges and needn't reach their ends.
All inputs are finite; a program needn't handle non-finite values.
Results may differ from the reference program's by a relative error of at most 0.0059.
Values may be sent and summed in bfloat16 or wider, within the bound.
No kernel may reach another device: no remote copies, remote signals or barrier semaphores. Data moves between devices by JAX's collectives and lax.ppermute only.
A program may use at most 64 MiB of HBM per device.

```python
import math
import jax
import jax.numpy as jnp
from jax import lax

D = 1024
HEADS = 8
HEAD_DIM = 128
TILE = 8
LEVELS = 2
CLAT = 8
CLON = 16
NLAT = 32
NLON = 128
N_LAT = 4
N_LON = 8


def shared_pair(key):
    base = jax.random.fold_in(key, 7)
    rough = jax.random.truncated_normal(jax.random.fold_in(base, 1), -4.0, 4.0, (2, NLAT, NLON, D), jnp.float32)
    tiled = jax.random.truncated_normal(jax.random.fold_in(base, 2), -4.0, 4.0, (2, NLAT // TILE, NLON // TILE, D), jnp.float32)
    tiled = jnp.repeat(jnp.repeat(tiled, TILE, axis=1), TILE, axis=2)
    return 0.5 * rough + tiled


def draw_keys_values(key, part):
    return shared_pair(key).astype(jnp.bfloat16)


def draw_queries(key, part):
    noise = jax.random.truncated_normal(jax.random.fold_in(key, 11), -4.0, 4.0, (NLAT, NLON, D), jnp.float32)
    return noise.astype(jnp.bfloat16)


def gaussian(key, extent, spread, most, kind=jnp.bfloat16):
    return jnp.clip(spread * jax.random.normal(key, extent, jnp.float32), -most, most).astype(kind)


def setup_inputs(seed: int = 0) -> dict:
    key_of = jax.random.split(jax.random.key(seed), 4)
    queries = draw_queries(jax.random.fold_in(key_of[3], 71), 0)
    keys_values = draw_keys_values(jax.random.fold_in(key_of[3], 71), 0)
    out_weight = gaussian(key_of[2], (D, D), D ** -0.5, 0.1875)
    return dict(queries=queries, keys_values=keys_values, out_weight=out_weight)


def pool_pairs(grid, factor):
    two, rows, cols, width = grid.shape
    shaped = grid.reshape(two, rows // factor, factor, cols // factor, factor, width)
    return lax.optimization_barrier(jnp.mean(shaped.astype(jnp.float32), axis=(2, 4))).astype(jnp.bfloat16)

def attend(queries, ext, valid, coarse_keys, coarse_vals, bias, out_weight):
    rows, cols, width = queries.shape
    tall, wide = (rows // TILE, cols // TILE)
    q_tiles = queries.astype(jnp.float32).reshape(tall, TILE, wide, TILE, HEADS, HEAD_DIM)
    k_tiles = ext[0].astype(jnp.float32).reshape(tall + 2, TILE, wide + 2, TILE, HEADS, HEAD_DIM)
    v_tiles = ext[1].astype(jnp.float32).reshape(tall + 2, TILE, wide + 2, TILE, HEADS, HEAD_DIM)
    row_mask = valid.reshape(tall + 2, TILE)
    scale = 1.0 / math.sqrt(HEAD_DIM)
    parts = []
    offsets = [(da, db) for da in range(3) for db in range(3)]
    for da, db in offsets:
        keys_near = k_tiles[da:da + tall, :, db:db + wide]
        block = jnp.einsum('aibjhe,akblhe->abhijkl', q_tiles, keys_near) * scale
        keep = row_mask[da:da + tall][:, None, None, None, None, :, None]
        block = jnp.where(keep, block, jnp.float32(-1e+30))
        parts.append(block.reshape(tall, wide, HEADS, TILE * TILE, TILE * TILE))
    ckeys = coarse_keys.astype(jnp.float32).reshape(-1, HEADS, HEAD_DIM)
    cvals = coarse_vals.astype(jnp.float32).reshape(-1, HEADS, HEAD_DIM)
    far = jnp.einsum('aibjhe,nhe->abhijn', q_tiles, ckeys) * scale + bias
    parts.append(far.reshape(tall, wide, HEADS, TILE * TILE, -1))
    scores = jnp.concatenate(parts, axis=-1)
    top = lax.optimization_barrier(jnp.max(scores, axis=-1, keepdims=True))
    expo = jnp.exp(scores - top)
    weights = (expo / lax.optimization_barrier(jnp.sum(expo, axis=-1, keepdims=True))).astype(jnp.bfloat16)
    weights = weights.astype(jnp.float32)
    total = jnp.zeros((tall, TILE, wide, TILE, HEADS, HEAD_DIM), jnp.float32)
    span = TILE * TILE
    for index, (da, db) in enumerate(offsets):
        piece = weights[..., index * span:(index + 1) * span].reshape(tall, wide, HEADS, TILE, TILE, TILE, TILE)
        total = total + jnp.einsum('abhijkl,akblhe->aibjhe', piece, v_tiles[da:da + tall, :, db:db + wide])
    piece = weights[..., 9 * span:].reshape(tall, wide, HEADS, TILE, TILE, -1)
    total = total + jnp.einsum('abhijn,nhe->aibjhe', piece, cvals)
    attended = total.reshape(rows * cols, width).astype(jnp.bfloat16)
    mixed = jnp.dot(attended, out_weight, preferred_element_type=jnp.float32)
    return mixed.astype(jnp.bfloat16).reshape(rows, cols, width)

def reference(queries, keys_values, out_weight):
    tall, wide = (CLAT // TILE, CLON // TILE)

    def pool_row(index):
        strip = lax.dynamic_slice_in_dim(keys_values, index * TILE, TILE, 1)
        return pool_pairs(strip, TILE)[:, 0]
    summary = lax.map(pool_row, jnp.arange(NLAT // TILE, dtype=jnp.int32))
    summary = jnp.transpose(summary, (1, 0, 2, 3))
    summaries = [summary]
    for level in range(1, LEVELS):
        summaries.append(pool_pairs(summaries[-1], 2))
    wrapped = jnp.concatenate([keys_values[:, :, NLON - TILE:], keys_values, keys_values[:, :, :TILE]], axis=2)
    padded = jnp.pad(wrapped, ((0, 0), (TILE, TILE), (0, 0), (0, 0)))
    zero = jnp.zeros((), jnp.int32)

    def one_block(device):
        row_blk = device // N_LON
        col_blk = device % N_LON
        block_q = lax.dynamic_slice(queries, (row_blk * CLAT, col_blk * CLON, zero), (CLAT, CLON, D))
        ext = lax.dynamic_slice(padded, (zero, row_blk * CLAT, col_blk * CLON, zero), (2, CLAT + 2 * TILE, CLON + 2 * TILE, D))
        rows = row_blk * CLAT - TILE + jnp.arange(CLAT + 2 * TILE, dtype=jnp.int32)
        valid = (rows >= 0) & (rows < NLAT)
        pieces = []
        biases = []
        for level in range(LEVELS):
            group_r = row_blk >> level
            group_c = col_blk >> level
            for rr, cc in ((group_r ^ 1, group_c), (group_r, group_c ^ 1), (group_r ^ 1, group_c ^ 1)):
                piece = lax.dynamic_slice(summaries[level], (zero, rr * tall, cc * wide, zero), (2, tall, wide, D))
                pieces.append(piece.reshape(2, tall * wide, D))
            biases.append(jnp.full((3 * tall * wide,), math.log(TILE * TILE * 4 ** level), jnp.float32))
        coarse = jnp.concatenate(pieces, axis=1)
        bias = jnp.concatenate(biases)
        return attend(block_q, ext, valid, coarse[0], coarse[1], bias, out_weight)
    blocks = lax.map(one_block, jnp.arange(N_LAT * N_LON, dtype=jnp.int32))
    blocks = blocks.reshape(N_LAT, N_LON, CLAT, CLON, D)
    return jnp.transpose(blocks, (0, 2, 1, 3, 4)).reshape(NLAT, NLON, D)
```

```python
import functools
import math

import jax
import jax.numpy as jnp
from jax import lax
from jax.experimental import pallas as pl
from jax.experimental.pallas import tpu as pltpu
from jax.sharding import PartitionSpec as P

HEADS = 8
HEAD_DIM = 128
TILE = 8
SPAN = TILE * TILE
SCALE = 1.0 / math.sqrt(HEAD_DIM)
NEG = -1e30
F32 = jnp.float32
BF16 = jnp.bfloat16
VMEM = pl.BlockSpec(memory_space=pltpu.VMEM)


def call(kernel, outs, name, flops, *args):
    moved = sum(a.size * a.dtype.itemsize for a in args)
    moved += sum(math.prod(o.shape) * o.dtype.itemsize for o in outs)
    return pl.pallas_call(
        kernel,
        out_shape=outs,
        in_specs=[VMEM] * len(args),
        out_specs=[VMEM] * len(outs),
        name=name,
        compiler_params=pltpu.CompilerParams(vmem_limit_bytes=16 * 1024 * 1024),
        cost_estimate=pl.CostEstimate(flops=flops, bytes_accessed=moved, transcendentals=0),
    )(*args)


def odd_column():
    return lax.rem(lax.axis_index("lon"), 2) == 1


def far_exists(n_lat):
    row = lax.axis_index("lat")
    return jnp.where(lax.rem(row, 2) == 1, row < n_lat - 1, row > 0)


def split_tiles(x, odd):
    cut = x.reshape(TILE, 2, TILE, x.shape[-1])
    left = cut[:, 0].reshape(SPAN, x.shape[-1])
    right = cut[:, 1].reshape(SPAN, x.shape[-1])
    return jnp.where(odd, right, left), jnp.where(odd, left, right)


def split_kernel(q_ref, kv_ref, qe_ref, qi_ref, kve_ref, kvi_ref, pool_ref):
    odd = odd_column()
    edge, inner = split_tiles(q_ref[...].astype(F32), odd)
    qe_ref[...] = edge.astype(BF16)
    qi_ref[...] = inner.astype(BF16)
    pooled = []
    for half in range(2):
        edge, inner = split_tiles(kv_ref[half].astype(F32), odd)
        kve_ref[half] = edge.astype(BF16)
        kvi_ref[half] = inner.astype(BF16)
        for tile in (edge, inner):
            pooled.append(jnp.sum(tile, axis=0, keepdims=True) * (1.0 / SPAN))
    pool_ref[...] = jnp.concatenate(pooled, axis=0).astype(BF16)


def logits(q, k):
    return lax.dot_general(q, k, (((1,), (1,)), ((), ())), preferred_element_type=F32) * SCALE


def partial_kernel(n_lat, q_ref, own_ref, pair_ref, far_ref, out_ref):
    far = far_exists(n_lat)
    lane = lax.broadcasted_iota(jnp.int32, (SPAN, 3 * SPAN), 1)
    keep = jnp.logical_or(lane < 2 * SPAN, far)
    column = lax.broadcasted_iota(jnp.int32, (SPAN, HEAD_DIM), 1)
    stats = jnp.zeros((SPAN, HEAD_DIM), F32)
    for h in range(HEADS):
        cols = slice(h * HEAD_DIM, (h + 1) * HEAD_DIM)
        k = jnp.concatenate([r[0, :, cols] for r in (own_ref, pair_ref, far_ref)], axis=0)
        v = jnp.concatenate([r[1, :, cols] for r in (own_ref, pair_ref, far_ref)], axis=0)
        s = jnp.where(keep, logits(q_ref[:, cols], k), NEG)
        top = jnp.max(s, axis=-1, keepdims=True)
        expo = jnp.exp(s - top)
        total = jnp.sum(expo, axis=-1, keepdims=True)
        part = jnp.dot(expo.astype(BF16), v, preferred_element_type=F32)
        out_ref[:, cols] = (part / total).astype(BF16)
        lse = top + jnp.log(total)
        high = lse.astype(BF16).astype(F32)
        mid = (lse - high).astype(BF16).astype(F32)
        low = lse - high - mid
        stats = jnp.where(column == h, high, stats)
        stats = jnp.where(column == HEADS + h, mid, stats)
        stats = jnp.where(column == 2 * HEADS + h, low, stats)
    out_ref[:, HEADS * HEAD_DIM :] = stats.astype(BF16)


def own_kernel(n_lat, count, qe_ref, qi_ref, *refs):
    tiles, (coarse_ref, out_ref, lse_ref) = refs[:6], refs[6:]
    rows = 2 * SPAN
    far = far_exists(n_lat)
    lane = lax.broadcasted_iota(jnp.int32, (rows, 6 * SPAN), 1)
    keep = jnp.logical_or(lane < 4 * SPAN, far)
    entry = lax.broadcasted_iota(jnp.int32, (rows, 2 * count), 1)
    bias = jnp.where(entry < count, math.log(SPAN), math.log(4 * SPAN)).astype(F32)
    column = lax.broadcasted_iota(jnp.int32, (rows, HEAD_DIM), 1)
    stats = jnp.zeros((rows, HEAD_DIM), F32)
    for h in range(HEADS):
        cols = slice(h * HEAD_DIM, (h + 1) * HEAD_DIM)
        q = jnp.concatenate([qe_ref[:, cols], qi_ref[:, cols]], axis=0)
        k = jnp.concatenate([r[0, :, cols] for r in tiles], axis=0)
        v = jnp.concatenate([r[1, :, cols] for r in tiles], axis=0)
        near = jnp.where(keep, logits(q, k), NEG)
        coarse = logits(q, coarse_ref[0, :, cols])[:, : 2 * count] + bias
        top = jnp.maximum(
            jnp.max(near, axis=-1, keepdims=True), jnp.max(coarse, axis=-1, keepdims=True)
        )
        near = jnp.exp(near - top)
        coarse = jnp.exp(coarse - top)
        total = jnp.sum(near, axis=-1, keepdims=True) + jnp.sum(coarse, axis=-1, keepdims=True)
        part = jnp.dot(near.astype(BF16), v, preferred_element_type=F32)
        part += jnp.dot(
            coarse.astype(BF16), coarse_ref[1, : 2 * count, cols], preferred_element_type=F32
        )
        out_ref[:, cols] = part / total
        stats = jnp.where(column == h, top + jnp.log(total), stats)
    lse_ref[...] = stats


def merge_kernel(own_ref, lse_ref, edge_ref, inner_ref, weight_ref, out_ref):
    width = HEADS * HEAD_DIM
    odd = odd_column()
    merged = []
    for index, back_ref in enumerate((edge_ref, inner_ref)):
        rows = slice(index * SPAN, (index + 1) * SPAN)
        stats = back_ref[:, width:].astype(F32)
        pieces = []
        for h in range(HEADS):
            cols = slice(h * HEAD_DIM, (h + 1) * HEAD_DIM)
            here = lse_ref[rows, h : h + 1]
            there = stats[:, h : h + 1] + stats[:, HEADS + h : HEADS + h + 1]
            there = there + stats[:, 2 * HEADS + h : 2 * HEADS + h + 1]
            share = 1.0 / (1.0 + jnp.exp(jnp.minimum(there - here, 80.0)))
            own = own_ref[rows, cols]
            pieces.append(own * share + back_ref[:, cols].astype(F32) * (1.0 - share))
        merged.append(jnp.concatenate(pieces, axis=1).reshape(TILE, TILE, width))
    edge, inner = merged
    left = jnp.where(odd, inner, edge)
    right = jnp.where(odd, edge, inner)
    attended = jnp.stack([left, right], axis=1).reshape(2 * SPAN, width).astype(BF16)
    mixed = jnp.dot(attended, weight_ref[...], preferred_element_type=F32)
    out_ref[...] = mixed.reshape(TILE, 2 * TILE, width).astype(BF16)


def swap(x, axis, distance):
    count = lax.axis_size(axis)
    return lax.ppermute(x, axis, [(i, i ^ distance) for i in range(count)])


def outward(x, axis):
    count = lax.axis_size(axis)
    return lax.ppermute(x, axis, [(i, (i + (1 if i % 2 else -1)) % count) for i in range(count)])


def onward(x, axis):
    count = lax.axis_size(axis)
    route = [(i, i + (-2 if i % 2 else 2)) for i in range(count)]
    return lax.ppermute(x, axis, [(s, t) for s, t in route if 0 <= t < count])


def mean_entries(*entries):
    total = sum(e.astype(F32) for e in entries)
    return (total * (1.0 / len(entries))).astype(BF16)


def shards(queries, keys_values, out_weight):
    n_lat = lax.axis_size("lat")
    width = queries.shape[-1]
    tile = jax.ShapeDtypeStruct((SPAN, width), BF16)
    pair = jax.ShapeDtypeStruct((2, SPAN, width), BF16)
    q_edge, q_inner, edge_own, inner_own, pooled = call(
        split_kernel,
        [tile, tile, pair, pair, jax.ShapeDtypeStruct((4, width), BF16)],
        "split",
        0,
        queries,
        keys_values,
    )
    edge_pair = swap(edge_own, "lat", 1)
    far_q_edge = outward(q_edge, "lon")
    far_q_inner = swap(q_inner, "lon", 1)
    level0 = pooled.reshape(2, 2, width)
    level0_lat = swap(level0, "lat", 1)
    inner_pair = swap(inner_own, "lat", 1)
    edge_far = onward(edge_pair, "lat")
    inner_far = onward(inner_pair, "lat")
    mine = mean_entries(level0[:, 0:1], level0[:, 1:2], level0_lat[:, 0:1], level0_lat[:, 1:2])
    beside = swap(jnp.concatenate([level0, level0_lat, mine], axis=1), "lon", 1)
    group = jnp.concatenate([mine, beside[:, 4:5]], axis=1)
    group_lon = swap(group, "lon", 2)
    group_lat = swap(jnp.concatenate([group, group_lon], axis=1), "lat", 2)
    coarse = jnp.concatenate([level0_lat, beside[:, 0:4], group_lon, group_lat], axis=1)
    count = coarse.shape[1] // 2
    coarse = jnp.pad(coarse, ((0, 0), (0, 16 - 2 * count), (0, 0)))

    back = jax.ShapeDtypeStruct((SPAN, width + HEAD_DIM), BF16)
    flops = 4 * SPAN * 3 * SPAN * width
    edge_part = call(
        functools.partial(partial_kernel, n_lat),
        [back],
        "edge_part",
        flops,
        far_q_edge,
        edge_own,
        edge_pair,
        edge_far,
    )[0]
    edge_back = outward(edge_part, "lon")
    inner_part = call(
        functools.partial(partial_kernel, n_lat),
        [back],
        "inner_part",
        flops,
        far_q_inner,
        inner_own,
        inner_pair,
        inner_far,
    )[0]
    inner_back = swap(inner_part, "lon", 1)
    own, lse = call(
        functools.partial(own_kernel, n_lat, count),
        [
            jax.ShapeDtypeStruct((2 * SPAN, width), F32),
            jax.ShapeDtypeStruct((2 * SPAN, HEAD_DIM), F32),
        ],
        "own_part",
        4 * flops,
        q_edge,
        q_inner,
        edge_own,
        inner_own,
        edge_pair,
        inner_pair,
        edge_far,
        inner_far,
        coarse,
    )
    return call(
        merge_kernel,
        [jax.ShapeDtypeStruct(queries.shape, BF16)],
        "merge",
        4 * SPAN * width * width,
        own,
        lse,
        edge_back,
        inner_back,
        out_weight,
    )[0]


def solution(mesh):
    return jax.shard_map(
        shards,
        mesh=mesh,
        in_specs=(P("lat", "lon", None), P(None, "lat", "lon", None), P()),
        out_specs=P("lat", "lon", None),
        check_vma=False,
    )
```

```python
import functools
import math

import jax
import jax.numpy as jnp
from jax import lax
from jax.experimental import pallas as pl
from jax.experimental.pallas import tpu as pltpu
from jax.sharding import PartitionSpec as P

HEADS = 8
HEAD_DIM = 128
TILE = 8
SPAN = TILE * TILE
SCALE = 1.0 / math.sqrt(HEAD_DIM)
NEG = -1e30
LIMIT = 16 * 1024 * 1024
F32 = jnp.float32
BF16 = jnp.bfloat16
VMEM = pl.BlockSpec(memory_space=pltpu.VMEM)


def call(kernel, outs, name, flops, *args):
    moved = sum(a.size * a.dtype.itemsize for a in args)
    moved += sum(math.prod(o.shape) * o.dtype.itemsize for o in outs)
    return pl.pallas_call(
        kernel,
        out_shape=outs,
        in_specs=[VMEM] * len(args),
        out_specs=[VMEM] * len(outs),
        name=name,
        compiler_params=pltpu.CompilerParams(vmem_limit_bytes=LIMIT),
        cost_estimate=pl.CostEstimate(flops=flops, bytes_accessed=moved, transcendentals=0),
    )(*args)


def odd_column():
    return lax.rem(lax.axis_index("lon"), 2) == 1


def far_exists(n_lat):
    row = lax.axis_index("lat")
    return jnp.where(lax.rem(row, 2) == 1, row < n_lat - 1, row > 0)


def split_tiles(x, odd):
    cut = x.reshape(TILE, 2, TILE, x.shape[-1])
    left = cut[:, 0].reshape(SPAN, x.shape[-1])
    right = cut[:, 1].reshape(SPAN, x.shape[-1])
    return jnp.where(odd, right, left), jnp.where(odd, left, right)


def split_kernel(q_hbm, kv_hbm, qe_ref, qi_ref, edge_ref, inner_ref, pool_ref, q_ref, kv_ref, sems):
    copies = [pltpu.make_async_copy(kv_hbm.at[i], kv_ref.at[i], sems.at[i]) for i in range(2)]
    copies.append(pltpu.make_async_copy(q_hbm, q_ref, sems.at[2]))
    for copy in copies:
        copy.start()
    odd = odd_column()
    pooled = []
    for half in range(2):
        copies[half].wait()
        edge, inner = split_tiles(kv_ref[half].astype(F32), odd)
        rows = slice(half * SPAN, (half + 1) * SPAN)
        edge_ref[rows] = edge.astype(BF16)
        inner_ref[rows] = inner.astype(BF16)
        for tile in (edge, inner):
            pooled.append(jnp.sum(tile, axis=0, keepdims=True) * (1.0 / SPAN))
    pooled = jnp.concatenate(pooled, axis=0).astype(BF16)
    pool_ref[...] = pooled
    edge_ref[2 * SPAN :] = pooled
    copies[2].wait()
    edge, inner = split_tiles(q_ref[...].astype(F32), odd)
    qe_ref[...] = edge.astype(BF16)
    qi_ref[...] = inner.astype(BF16)


def logits(q, k):
    return lax.dot_general(q, k, (((1,), (1,)), ((), ())), preferred_element_type=F32) * SCALE


def heads():
    return [slice(h * HEAD_DIM, (h + 1) * HEAD_DIM) for h in range(HEADS)]


def stacked(refs, half, cols):
    return jnp.concatenate([r[half * SPAN : (half + 1) * SPAN, cols] for r in refs], axis=0)


def partial_kernel(n_lat, q_ref, own_ref, pair_ref, far_ref, out_ref):
    tiles = (own_ref, pair_ref, far_ref)
    far = far_exists(n_lat)
    lane = lax.broadcasted_iota(jnp.int32, (SPAN, 3 * SPAN), 1)
    keep = jnp.logical_or(lane < 2 * SPAN, far)
    column = lax.broadcasted_iota(jnp.int32, (SPAN, HEAD_DIM), 1)
    scores = [
        jnp.where(keep, logits(q_ref[:, cols], stacked(tiles, 0, cols)), NEG) for cols in heads()
    ]
    tops = [jnp.max(s, axis=-1, keepdims=True) for s in scores]
    expos = [jnp.exp(s - top) for s, top in zip(scores, tops)]
    totals = [jnp.sum(e, axis=-1, keepdims=True) for e in expos]
    parts = [
        jnp.dot(e.astype(BF16), stacked(tiles, 1, cols), preferred_element_type=F32)
        for e, cols in zip(expos, heads())
    ]
    stats = jnp.zeros((SPAN, HEAD_DIM), F32)
    for h in range(HEADS):
        lse = tops[h] + jnp.log(totals[h])
        high = lse.astype(BF16).astype(F32)
        mid = (lse - high).astype(BF16).astype(F32)
        low = lse - high - mid
        stats = jnp.where(column == h, high, stats)
        stats = jnp.where(column == HEADS + h, mid, stats)
        stats = jnp.where(column == 2 * HEADS + h, low, stats)
    for h, cols in enumerate(heads()):
        out_ref[:, cols] = (parts[h] * (1.0 / totals[h])).astype(BF16)
    out_ref[:, HEADS * HEAD_DIM :] = stats.astype(BF16)


def own_kernel(n_lat, count, qe_ref, qi_ref, *refs):
    tiles, (coarse_ref, out_ref, lse_ref) = refs[:6], refs[6:]
    rows = 2 * SPAN
    far = far_exists(n_lat)
    lane = lax.broadcasted_iota(jnp.int32, (rows, 6 * SPAN), 1)
    keep = jnp.logical_or(lane < 4 * SPAN, far)
    entry = lax.broadcasted_iota(jnp.int32, (rows, 2 * count), 1)
    bias = jnp.where(entry < count, math.log(SPAN), math.log(4 * SPAN)).astype(F32)
    column = lax.broadcasted_iota(jnp.int32, (rows, HEAD_DIM), 1)
    stats = jnp.zeros((rows, HEAD_DIM), F32)
    for group in range(0, HEADS, 4):
        near, coarse = [], []
        for cols in heads()[group : group + 4]:
            q = jnp.concatenate([qe_ref[:, cols], qi_ref[:, cols]], axis=0)
            near.append(jnp.where(keep, logits(q, stacked(tiles, 0, cols)), NEG))
            coarse.append(logits(q, coarse_ref[0, :, cols])[:, : 2 * count] + bias)
        tops = [
            jnp.maximum(jnp.max(n, axis=-1, keepdims=True), jnp.max(c, axis=-1, keepdims=True))
            for n, c in zip(near, coarse)
        ]
        near = [jnp.exp(n - top) for n, top in zip(near, tops)]
        coarse = [jnp.exp(c - top) for c, top in zip(coarse, tops)]
        totals = [
            jnp.sum(n, axis=-1, keepdims=True) + jnp.sum(c, axis=-1, keepdims=True)
            for n, c in zip(near, coarse)
        ]
        for i, cols in enumerate(heads()[group : group + 4]):
            part = jnp.dot(
                near[i].astype(BF16), stacked(tiles, 1, cols), preferred_element_type=F32
            )
            part += jnp.dot(
                coarse[i].astype(BF16), coarse_ref[1, : 2 * count, cols], preferred_element_type=F32
            )
            out_ref[:, cols] = part * (1.0 / totals[i])
            stats = jnp.where(column == group + i, tops[i] + jnp.log(totals[i]), stats)
    lse_ref[...] = stats


def merge_kernel(own_ref, lse_ref, edge_ref, inner_ref, weight_ref, out_ref):
    width = HEADS * HEAD_DIM
    odd = odd_column()
    merged = []
    for index, back_ref in enumerate((edge_ref, inner_ref)):
        rows = slice(index * SPAN, (index + 1) * SPAN)
        stats = back_ref[:, width:].astype(F32)
        pieces = []
        for h in range(HEADS):
            cols = slice(h * HEAD_DIM, (h + 1) * HEAD_DIM)
            here = lse_ref[rows, h : h + 1]
            there = stats[:, h : h + 1] + stats[:, HEADS + h : HEADS + h + 1]
            there = there + stats[:, 2 * HEADS + h : 2 * HEADS + h + 1]
            share = 1.0 / (1.0 + jnp.exp(jnp.minimum(there - here, 80.0)))
            own = own_ref[rows, cols]
            pieces.append(own * share + back_ref[:, cols].astype(F32) * (1.0 - share))
        merged.append(jnp.concatenate(pieces, axis=1).reshape(TILE, TILE, width))
    edge, inner = merged
    left = jnp.where(odd, inner, edge)
    right = jnp.where(odd, edge, inner)
    attended = jnp.stack([left, right], axis=1).reshape(2 * SPAN, width).astype(BF16)
    mixed = jnp.dot(attended, weight_ref[...], preferred_element_type=F32)
    out_ref[...] = mixed.reshape(TILE, 2 * TILE, width).astype(BF16)


def swap(x, axis, distance):
    count = lax.axis_size(axis)
    return lax.ppermute(x, axis, [(i, i ^ distance) for i in range(count)])


def outward(x, axis):
    count = lax.axis_size(axis)
    return lax.ppermute(x, axis, [(i, (i + (1 if i % 2 else -1)) % count) for i in range(count)])


def stride(x, axis, step):
    count = lax.axis_size(axis)
    route = [(i, (i + (-step if i % 2 else step)) % count) for i in range(count)]
    return lax.ppermute(x, axis, route)


def after_kernel(*refs):
    pass


def after(x, *tokens):
    return pl.pallas_call(
        after_kernel,
        out_shape=jax.ShapeDtypeStruct(x.shape, x.dtype),
        in_specs=[pl.BlockSpec(memory_space=pl.ANY)] * (1 + len(tokens)),
        out_specs=pl.BlockSpec(memory_space=pl.ANY),
        input_output_aliases={0: 0},
        name="after",
    )(x, *tokens)


def mean_entries(*entries):
    total = sum(e.astype(F32) for e in entries)
    return (total * (1.0 / len(entries))).astype(BF16)


def shards(queries, keys_values, out_weight):
    n_lat = lax.axis_size("lat")
    width = queries.shape[-1]
    def like(*shape):
        return jax.ShapeDtypeStruct(shape, BF16)

    pack = 2 * SPAN + 4
    q_edge, q_inner, edge_own, inner_own, pooled = pl.pallas_call(
        split_kernel,
        out_shape=[
            like(SPAN, width),
            like(SPAN, width),
            like(pack, width),
            like(2 * SPAN, width),
            like(4, width),
        ],
        in_specs=[pl.BlockSpec(memory_space=pltpu.HBM)] * 2,
        out_specs=[VMEM] * 5,
        scratch_shapes=[
            pltpu.VMEM(queries.shape, BF16),
            pltpu.VMEM(keys_values.shape, BF16),
            pltpu.SemaphoreType.DMA((3,)),
        ],
        name="split",
        compiler_params=pltpu.CompilerParams(vmem_limit_bytes=LIMIT),
        cost_estimate=pl.CostEstimate(flops=0, bytes_accessed=2 << 20, transcendentals=0),
    )(*(pltpu.with_memory_space_constraint(x, pltpu.HBM) for x in (queries, keys_values)))
    edge_pair = swap(edge_own, "lat", 1)
    far_q_edge = outward(q_edge, "lon")
    far_q_inner = swap(q_inner, "lon", 1)
    inner_pair = swap(inner_own, "lat", 1)
    edge_pair = after(edge_pair, far_q_edge, far_q_inner)
    edge_far = stride(edge_pair, "lat", 2)
    level0 = pooled.reshape(2, 2, width)
    level0_lat = edge_pair[2 * SPAN :].reshape(2, 2, width)
    mine = mean_entries(level0[:, 0:1], level0[:, 1:2], level0_lat[:, 0:1], level0_lat[:, 1:2])
    beside = swap(jnp.concatenate([level0, level0_lat, mine], axis=1), "lon", 1)
    group = jnp.concatenate([mine, beside[:, 4:5]], axis=1)
    group_lon = swap(group, "lon", 2)
    inner_pair = after(inner_pair, group_lon)
    inner_far = stride(inner_pair, "lat", 2)
    group_lat = swap(jnp.concatenate([group, group_lon], axis=1), "lat", 2)
    coarse = jnp.concatenate([level0_lat, beside[:, 0:4], group_lon, group_lat], axis=1)
    count = coarse.shape[1] // 2
    coarse = jnp.pad(coarse, ((0, 0), (0, 16 - 2 * count), (0, 0)))

    back = jax.ShapeDtypeStruct((SPAN, width + HEAD_DIM), BF16)
    flops = 4 * SPAN * 3 * SPAN * width
    edge_part = call(
        functools.partial(partial_kernel, n_lat),
        [back],
        "edge_part",
        flops,
        far_q_edge,
        edge_own,
        edge_pair,
        edge_far,
    )[0]
    edge_back = outward(edge_part, "lon")
    inner_far = after(inner_far, edge_part)
    inner_part = call(
        functools.partial(partial_kernel, n_lat),
        [back],
        "inner_part",
        flops,
        far_q_inner,
        inner_own,
        inner_pair,
        inner_far,
    )[0]
    inner_back = swap(inner_part, "lon", 1)
    coarse = after(coarse, inner_part)
    own, lse = call(
        functools.partial(own_kernel, n_lat, count),
        [
            jax.ShapeDtypeStruct((2 * SPAN, width), F32),
            jax.ShapeDtypeStruct((2 * SPAN, HEAD_DIM), F32),
        ],
        "own_part",
        4 * flops,
        q_edge,
        q_inner,
        edge_own,
        inner_own,
        edge_pair,
        inner_pair,
        edge_far,
        inner_far,
        coarse,
    )
    return call(
        merge_kernel,
        [jax.ShapeDtypeStruct(queries.shape, BF16)],
        "merge",
        4 * SPAN * width * width,
        own,
        lse,
        edge_back,
        inner_back,
        out_weight,
    )[0]


def solution(mesh):
    return jax.shard_map(
        shards,
        mesh=mesh,
        in_specs=(P("lat", "lon", None), P(None, "lat", "lon", None), P()),
        out_specs=P("lat", "lon", None),
        check_vma=False,
    )
```

```python
import functools
import math

import jax
import jax.numpy as jnp
from jax import lax
from jax.experimental import pallas as pl
from jax.experimental.pallas import tpu as pltpu
from jax.sharding import PartitionSpec as P

HEADS = 8
HEAD_DIM = 128
TILE = 8
SPAN = TILE * TILE
SCALE = 1.0 / math.sqrt(HEAD_DIM)
NEG = -1e30
LIMIT = 16 * 1024 * 1024
F32 = jnp.float32
BF16 = jnp.bfloat16
VMEM = pl.BlockSpec(memory_space=pltpu.VMEM)


def call(kernel, outs, name, flops, *args):
    moved = sum(a.size * a.dtype.itemsize for a in args)
    moved += sum(math.prod(o.shape) * o.dtype.itemsize for o in outs)
    return pl.pallas_call(
        kernel,
        out_shape=outs,
        in_specs=[VMEM] * len(args),
        out_specs=[VMEM] * len(outs),
        name=name,
        compiler_params=pltpu.CompilerParams(vmem_limit_bytes=LIMIT),
        cost_estimate=pl.CostEstimate(flops=flops, bytes_accessed=moved, transcendentals=0),
    )(*args)


def odd_column():
    return lax.rem(lax.axis_index("lon"), 2) == 1


def far_exists(n_lat):
    row = lax.axis_index("lat")
    return jnp.where(lax.rem(row, 2) == 1, row < n_lat - 1, row > 0)


def split_tiles(x, odd):
    cut = x.reshape(TILE, 2, TILE, x.shape[-1])
    left = cut[:, 0].reshape(SPAN, x.shape[-1])
    right = cut[:, 1].reshape(SPAN, x.shape[-1])
    return jnp.where(odd, right, left), jnp.where(odd, left, right)


def split_kernel(q_hbm, kv_hbm, qe_ref, qi_ref, edge_ref, inner_ref, pool_ref, q_ref, kv_ref, sems):
    copies = [pltpu.make_async_copy(kv_hbm.at[i], kv_ref.at[i], sems.at[i]) for i in range(2)]
    copies.append(pltpu.make_async_copy(q_hbm, q_ref, sems.at[2]))
    for copy in copies:
        copy.start()
    odd = odd_column()
    pooled = []
    for half in range(2):
        copies[half].wait()
        edge, inner = split_tiles(kv_ref[half].astype(F32), odd)
        rows = slice(half * SPAN, (half + 1) * SPAN)
        edge_ref[rows] = edge.astype(BF16)
        inner_ref[rows] = inner.astype(BF16)
        for tile in (edge, inner):
            pooled.append(jnp.sum(tile, axis=0, keepdims=True) * (1.0 / SPAN))
    pooled = jnp.concatenate(pooled, axis=0).astype(BF16)
    pool_ref[...] = pooled
    edge_ref[2 * SPAN :] = pooled
    copies[2].wait()
    edge, inner = split_tiles(q_ref[...].astype(F32), odd)
    qe_ref[...] = edge.astype(BF16)
    qi_ref[...] = inner.astype(BF16)


def logits(q, k):
    return lax.dot_general(q, k, (((1,), (1,)), ((), ())), preferred_element_type=F32) * SCALE


def heads():
    return [slice(h * HEAD_DIM, (h + 1) * HEAD_DIM) for h in range(HEADS)]


def stacked(refs, half, cols):
    return jnp.concatenate([r[half * SPAN : (half + 1) * SPAN, cols] for r in refs], axis=0)


def partial_kernel(n_lat, q_ref, own_ref, pair_ref, far_ref, out_ref):
    tiles = (own_ref, pair_ref, far_ref)
    far = far_exists(n_lat)
    lane = lax.broadcasted_iota(jnp.int32, (SPAN, 3 * SPAN), 1)
    keep = jnp.logical_or(lane < 2 * SPAN, far)
    column = lax.broadcasted_iota(jnp.int32, (SPAN, HEAD_DIM), 1)
    scores = [
        jnp.where(keep, logits(q_ref[:, cols], stacked(tiles, 0, cols)), NEG) for cols in heads()
    ]
    tops = [jnp.max(s, axis=-1, keepdims=True) for s in scores]
    expos = [jnp.exp(s - top) for s, top in zip(scores, tops)]
    totals = [jnp.sum(e, axis=-1, keepdims=True) for e in expos]
    parts = [
        jnp.dot(e.astype(BF16), stacked(tiles, 1, cols), preferred_element_type=F32)
        for e, cols in zip(expos, heads())
    ]
    stats = jnp.zeros((SPAN, HEAD_DIM), F32)
    for h in range(HEADS):
        lse = tops[h] + jnp.log(totals[h])
        high = lse.astype(BF16).astype(F32)
        mid = (lse - high).astype(BF16).astype(F32)
        low = lse - high - mid
        stats = jnp.where(column == h, high, stats)
        stats = jnp.where(column == HEADS + h, mid, stats)
        stats = jnp.where(column == 2 * HEADS + h, low, stats)
    for h, cols in enumerate(heads()):
        out_ref[:, cols] = (parts[h] * (1.0 / totals[h])).astype(BF16)
    out_ref[:, HEADS * HEAD_DIM :] = stats.astype(BF16)


def own_kernel(n_lat, count, qe_ref, qi_ref, *refs):
    tiles, (coarse_ref, out_ref, lse_ref) = refs[:6], refs[6:]
    rows = 2 * SPAN
    far = far_exists(n_lat)
    lane = lax.broadcasted_iota(jnp.int32, (rows, 6 * SPAN), 1)
    keep = jnp.logical_or(lane < 4 * SPAN, far)
    entry = lax.broadcasted_iota(jnp.int32, (rows, 2 * count), 1)
    bias = jnp.where(entry < count, math.log(SPAN), math.log(4 * SPAN)).astype(F32)
    column = lax.broadcasted_iota(jnp.int32, (rows, HEAD_DIM), 1)
    stats = jnp.zeros((rows, HEAD_DIM), F32)
    for group in range(0, HEADS, 4):
        near, coarse = [], []
        for cols in heads()[group : group + 4]:
            q = jnp.concatenate([qe_ref[:, cols], qi_ref[:, cols]], axis=0)
            near.append(jnp.where(keep, logits(q, stacked(tiles, 0, cols)), NEG))
            coarse.append(logits(q, coarse_ref[0, :, cols])[:, : 2 * count] + bias)
        tops = [
            jnp.maximum(jnp.max(n, axis=-1, keepdims=True), jnp.max(c, axis=-1, keepdims=True))
            for n, c in zip(near, coarse)
        ]
        near = [jnp.exp(n - top) for n, top in zip(near, tops)]
        coarse = [jnp.exp(c - top) for c, top in zip(coarse, tops)]
        totals = [
            jnp.sum(n, axis=-1, keepdims=True) + jnp.sum(c, axis=-1, keepdims=True)
            for n, c in zip(near, coarse)
        ]
        for i, cols in enumerate(heads()[group : group + 4]):
            part = jnp.dot(
                near[i].astype(BF16), stacked(tiles, 1, cols), preferred_element_type=F32
            )
            part += jnp.dot(
                coarse[i].astype(BF16), coarse_ref[1, : 2 * count, cols], preferred_element_type=F32
            )
            out_ref[:, cols] = part * (1.0 / totals[i])
            stats = jnp.where(column == group + i, tops[i] + jnp.log(totals[i]), stats)
    lse_ref[...] = stats


def merge_kernel(own_ref, lse_ref, edge_ref, inner_ref, weight_ref, out_ref):
    width = HEADS * HEAD_DIM
    odd = odd_column()
    merged = []
    for index, back_ref in enumerate((edge_ref, inner_ref)):
        rows = slice(index * SPAN, (index + 1) * SPAN)
        stats = back_ref[:, width:].astype(F32)
        pieces = []
        for h in range(HEADS):
            cols = slice(h * HEAD_DIM, (h + 1) * HEAD_DIM)
            here = lse_ref[rows, h : h + 1]
            there = stats[:, h : h + 1] + stats[:, HEADS + h : HEADS + h + 1]
            there = there + stats[:, 2 * HEADS + h : 2 * HEADS + h + 1]
            share = 1.0 / (1.0 + jnp.exp(jnp.minimum(there - here, 80.0)))
            own = own_ref[rows, cols]
            pieces.append(own * share + back_ref[:, cols].astype(F32) * (1.0 - share))
        merged.append(jnp.concatenate(pieces, axis=1).reshape(TILE, TILE, width))
    edge, inner = merged
    left = jnp.where(odd, inner, edge)
    right = jnp.where(odd, edge, inner)
    attended = jnp.stack([left, right], axis=1).reshape(2 * SPAN, width).astype(BF16)
    mixed = jnp.dot(attended, weight_ref[...], preferred_element_type=F32)
    out_ref[...] = mixed.reshape(TILE, 2 * TILE, width).astype(BF16)


def swap(x, axis, distance):
    count = lax.axis_size(axis)
    return lax.ppermute(x, axis, [(i, i ^ distance) for i in range(count)])


def outward(x, axis):
    count = lax.axis_size(axis)
    return lax.ppermute(x, axis, [(i, (i + (1 if i % 2 else -1)) % count) for i in range(count)])


def stride(x, axis, step):
    count = lax.axis_size(axis)
    route = [(i, (i + (-step if i % 2 else step)) % count) for i in range(count)]
    return lax.ppermute(x, axis, route)


def after_kernel(*refs):
    pass


def after(x, *tokens):
    return pl.pallas_call(
        after_kernel,
        out_shape=jax.ShapeDtypeStruct(x.shape, x.dtype),
        in_specs=[pl.BlockSpec(memory_space=pl.ANY)] * (1 + len(tokens)),
        out_specs=pl.BlockSpec(memory_space=pl.ANY),
        input_output_aliases={0: 0},
        name="after",
        compiler_params=pltpu.CompilerParams(vmem_limit_bytes=1024 * 1024),
    )(x, *tokens)


def mean_entries(*entries):
    total = sum(e.astype(F32) for e in entries)
    return (total * (1.0 / len(entries))).astype(BF16)


def shards(queries, keys_values, out_weight):
    n_lat = lax.axis_size("lat")
    width = queries.shape[-1]
    def like(*shape):
        return jax.ShapeDtypeStruct(shape, BF16)

    pack = 2 * SPAN + 4
    q_edge, q_inner, edge_own, inner_own, pooled = pl.pallas_call(
        split_kernel,
        out_shape=[
            like(SPAN, width),
            like(SPAN, width),
            like(pack, width),
            like(2 * SPAN, width),
            like(4, width),
        ],
        in_specs=[pl.BlockSpec(memory_space=pltpu.HBM)] * 2,
        out_specs=[VMEM] * 5,
        scratch_shapes=[
            pltpu.VMEM(queries.shape, BF16),
            pltpu.VMEM(keys_values.shape, BF16),
            pltpu.SemaphoreType.DMA((3,)),
        ],
        name="split",
        compiler_params=pltpu.CompilerParams(vmem_limit_bytes=LIMIT),
        cost_estimate=pl.CostEstimate(flops=0, bytes_accessed=2 << 20, transcendentals=0),
    )(*(pltpu.with_memory_space_constraint(x, pltpu.HBM) for x in (queries, keys_values)))
    edge_pair = swap(edge_own, "lat", 1)
    far_q_edge = outward(q_edge, "lon")
    far_q_inner = swap(q_inner, "lon", 1)
    inner_pair = swap(inner_own, "lat", 1)
    edge_pair = after(edge_pair, far_q_edge, far_q_inner)
    edge_far = stride(edge_pair, "lat", 2)
    level0 = pooled.reshape(2, 2, width)
    level0_lat = edge_pair[2 * SPAN :].reshape(2, 2, width)
    mine = mean_entries(level0[:, 0:1], level0[:, 1:2], level0_lat[:, 0:1], level0_lat[:, 1:2])
    beside = swap(jnp.concatenate([level0, level0_lat, mine], axis=1), "lon", 1)
    group = jnp.concatenate([mine, beside[:, 4:5]], axis=1)
    group_lon = swap(group, "lon", 2)
    inner_pair = after(inner_pair, group_lon)
    inner_far = stride(inner_pair, "lat", 2)
    group_lat = swap(jnp.concatenate([group, group_lon], axis=1), "lat", 2)
    coarse = jnp.concatenate([level0_lat, beside[:, 0:4], group_lon, group_lat], axis=1)
    count = coarse.shape[1] // 2
    coarse = jnp.pad(coarse, ((0, 0), (0, 16 - 2 * count), (0, 0)))

    back = jax.ShapeDtypeStruct((SPAN, width + HEAD_DIM), BF16)
    flops = 4 * SPAN * 3 * SPAN * width
    edge_part = call(
        functools.partial(partial_kernel, n_lat),
        [back],
        "edge_part",
        flops,
        far_q_edge,
        edge_own,
        edge_pair,
        edge_far,
    )[0]
    edge_back = outward(edge_part, "lon")
    inner_far = after(inner_far, edge_part)
    inner_part = call(
        functools.partial(partial_kernel, n_lat),
        [back],
        "inner_part",
        flops,
        far_q_inner,
        inner_own,
        inner_pair,
        inner_far,
    )[0]
    inner_back = swap(inner_part, "lon", 1)
    coarse = after(coarse, inner_part)
    own, lse = call(
        functools.partial(own_kernel, n_lat, count),
        [
            jax.ShapeDtypeStruct((2 * SPAN, width), F32),
            jax.ShapeDtypeStruct((2 * SPAN, HEAD_DIM), F32),
        ],
        "own_part",
        4 * flops,
        q_edge,
        q_inner,
        edge_own,
        inner_own,
        edge_pair,
        inner_pair,
        edge_far,
        inner_far,
        coarse,
    )
    return call(
        merge_kernel,
        [jax.ShapeDtypeStruct(queries.shape, BF16)],
        "merge",
        4 * SPAN * width * width,
        own,
        lse,
        edge_back,
        inner_back,
        out_weight,
    )[0]


def solution(mesh):
    return jax.shard_map(
        shards,
        mesh=mesh,
        in_specs=(P("lat", "lon", None), P(None, "lat", "lon", None), P()),
        out_specs=P("lat", "lon", None),
        check_vma=False,
    )
```

```python
import functools
import math

import jax
import jax.numpy as jnp
from jax import lax
from jax.experimental import pallas as pl
from jax.experimental.pallas import tpu as pltpu
from jax.sharding import PartitionSpec as P

HEADS = 8
HEAD_DIM = 128
TILE = 8
SPAN = TILE * TILE
SCALE = 1.0 / math.sqrt(HEAD_DIM)
NEG = -1e30
WEIGHT = 2 * 10**8
LIMIT = 16 * 1024 * 1024
F32 = jnp.float32
BF16 = jnp.bfloat16
VMEM = pl.BlockSpec(memory_space=pltpu.VMEM)


def call(kernel, outs, name, flops, *args):
    moved = sum(a.size * a.dtype.itemsize for a in args)
    moved += sum(math.prod(o.shape) * o.dtype.itemsize for o in outs)
    return pl.pallas_call(
        kernel,
        out_shape=outs,
        in_specs=[VMEM] * len(args),
        out_specs=[VMEM] * len(outs),
        name=name,
        compiler_params=pltpu.CompilerParams(vmem_limit_bytes=LIMIT),
        cost_estimate=pl.CostEstimate(flops=flops, bytes_accessed=moved, transcendentals=0),
    )(*args)


def odd_column():
    return lax.rem(lax.axis_index("lon"), 2) == 1


def far_exists(n_lat):
    row = lax.axis_index("lat")
    return jnp.where(lax.rem(row, 2) == 1, row < n_lat - 1, row > 0)


def split_tiles(x, odd):
    cut = x.reshape(TILE, 2, TILE, x.shape[-1])
    left = cut[:, 0].reshape(SPAN, x.shape[-1])
    right = cut[:, 1].reshape(SPAN, x.shape[-1])
    return jnp.where(odd, right, left), jnp.where(odd, left, right)


def split_kernel(q_hbm, kv_hbm, qe_ref, qi_ref, edge_ref, inner_ref, pool_ref, q_ref, kv_ref, sems):
    copies = [pltpu.make_async_copy(kv_hbm.at[i], kv_ref.at[i], sems.at[i]) for i in range(2)]
    copies.append(pltpu.make_async_copy(q_hbm, q_ref, sems.at[2]))
    for copy in copies:
        copy.start()
    odd = odd_column()
    pooled = []
    for half in range(2):
        copies[half].wait()
        edge, inner = split_tiles(kv_ref[half].astype(F32), odd)
        rows = slice(half * SPAN, (half + 1) * SPAN)
        edge_ref[rows] = edge.astype(BF16)
        inner_ref[rows] = inner.astype(BF16)
        for tile in (edge, inner):
            pooled.append(jnp.sum(tile, axis=0, keepdims=True) * (1.0 / SPAN))
    pooled = jnp.concatenate(pooled, axis=0).astype(BF16)
    pool_ref[...] = pooled
    edge_ref[2 * SPAN :] = pooled
    copies[2].wait()
    edge, inner = split_tiles(q_ref[...].astype(F32), odd)
    qe_ref[...] = edge.astype(BF16)
    qi_ref[...] = inner.astype(BF16)


def logits(q, k):
    return lax.dot_general(q, k, (((1,), (1,)), ((), ())), preferred_element_type=F32) * SCALE


def heads():
    return [slice(h * HEAD_DIM, (h + 1) * HEAD_DIM) for h in range(HEADS)]


def stacked(refs, half, cols):
    return jnp.concatenate([r[half * SPAN : (half + 1) * SPAN, cols] for r in refs], axis=0)


def partial_kernel(n_lat, q_ref, own_ref, pair_ref, far_ref, out_ref):
    tiles = (own_ref, pair_ref, far_ref)
    far = far_exists(n_lat)
    lane = lax.broadcasted_iota(jnp.int32, (SPAN, 3 * SPAN), 1)
    keep = jnp.logical_or(lane < 2 * SPAN, far)
    column = lax.broadcasted_iota(jnp.int32, (SPAN, HEAD_DIM), 1)
    scores = [
        jnp.where(keep, logits(q_ref[:, cols], stacked(tiles, 0, cols)), NEG) for cols in heads()
    ]
    tops = [jnp.max(s, axis=-1, keepdims=True) for s in scores]
    expos = [jnp.exp(s - top) for s, top in zip(scores, tops)]
    totals = [jnp.sum(e, axis=-1, keepdims=True) for e in expos]
    parts = [
        jnp.dot(e.astype(BF16), stacked(tiles, 1, cols), preferred_element_type=F32)
        for e, cols in zip(expos, heads())
    ]
    stats = jnp.zeros((SPAN, HEAD_DIM), F32)
    for h in range(HEADS):
        lse = tops[h] + jnp.log(totals[h])
        high = lse.astype(BF16).astype(F32)
        mid = (lse - high).astype(BF16).astype(F32)
        low = lse - high - mid
        stats = jnp.where(column == h, high, stats)
        stats = jnp.where(column == HEADS + h, mid, stats)
        stats = jnp.where(column == 2 * HEADS + h, low, stats)
    for h, cols in enumerate(heads()):
        out_ref[:, cols] = (parts[h] * (1.0 / totals[h])).astype(BF16)
    out_ref[:, HEADS * HEAD_DIM :] = stats.astype(BF16)


def own_kernel(n_lat, count, *refs):
    tiles, (qi_ref, qe_ref, coarse_ref, out_ref, lse_ref) = refs[:6], refs[6:]
    rows = 2 * SPAN
    far = far_exists(n_lat)
    lane = lax.broadcasted_iota(jnp.int32, (rows, 6 * SPAN), 1)
    keep = jnp.logical_or(lane < 4 * SPAN, far)
    entry = lax.broadcasted_iota(jnp.int32, (rows, 2 * count), 1)
    bias = jnp.where(entry < count, math.log(SPAN), math.log(4 * SPAN)).astype(F32)
    column = lax.broadcasted_iota(jnp.int32, (rows, HEAD_DIM), 1)
    stats = jnp.zeros((rows, HEAD_DIM), F32)
    for group in range(0, HEADS, 4):
        near, coarse = [], []
        for cols in heads()[group : group + 4]:
            q = jnp.concatenate([qe_ref[:, cols], qi_ref[:, cols]], axis=0)
            near.append(jnp.where(keep, logits(q, stacked(tiles, 0, cols)), NEG))
            coarse.append(logits(q, coarse_ref[0, :, cols])[:, : 2 * count] + bias)
        tops = [
            jnp.maximum(jnp.max(n, axis=-1, keepdims=True), jnp.max(c, axis=-1, keepdims=True))
            for n, c in zip(near, coarse)
        ]
        near = [jnp.exp(n - top) for n, top in zip(near, tops)]
        coarse = [jnp.exp(c - top) for c, top in zip(coarse, tops)]
        totals = [
            jnp.sum(n, axis=-1, keepdims=True) + jnp.sum(c, axis=-1, keepdims=True)
            for n, c in zip(near, coarse)
        ]
        for i, cols in enumerate(heads()[group : group + 4]):
            part = jnp.dot(
                near[i].astype(BF16), stacked(tiles, 1, cols), preferred_element_type=F32
            )
            part += jnp.dot(
                coarse[i].astype(BF16), coarse_ref[1, : 2 * count, cols], preferred_element_type=F32
            )
            out_ref[:, cols] = part * (1.0 / totals[i])
            stats = jnp.where(column == group + i, tops[i] + jnp.log(totals[i]), stats)
    lse_ref[...] = stats


def merge_kernel(own_ref, lse_ref, edge_ref, inner_ref, weight_ref, out_ref):
    width = HEADS * HEAD_DIM
    odd = odd_column()
    merged = []
    for index, back_ref in enumerate((edge_ref, inner_ref)):
        rows = slice(index * SPAN, (index + 1) * SPAN)
        stats = back_ref[:, width:].astype(F32)
        pieces = []
        for h in range(HEADS):
            cols = slice(h * HEAD_DIM, (h + 1) * HEAD_DIM)
            here = lse_ref[rows, h : h + 1]
            there = stats[:, h : h + 1] + stats[:, HEADS + h : HEADS + h + 1]
            there = there + stats[:, 2 * HEADS + h : 2 * HEADS + h + 1]
            share = 1.0 / (1.0 + jnp.exp(jnp.minimum(there - here, 80.0)))
            own = own_ref[rows, cols]
            pieces.append(own * share + back_ref[:, cols].astype(F32) * (1.0 - share))
        merged.append(jnp.concatenate(pieces, axis=1).reshape(TILE, TILE, width))
    edge, inner = merged
    left = jnp.where(odd, inner, edge)
    right = jnp.where(odd, edge, inner)
    attended = jnp.stack([left, right], axis=1).reshape(2 * SPAN, width).astype(BF16)
    mixed = jnp.dot(attended, weight_ref[...], preferred_element_type=F32)
    out_ref[...] = mixed.reshape(TILE, 2 * TILE, width).astype(BF16)


def swap(x, axis, distance):
    count = lax.axis_size(axis)
    return lax.ppermute(x, axis, [(i, i ^ distance) for i in range(count)])


def outward(x, axis):
    count = lax.axis_size(axis)
    return lax.ppermute(x, axis, [(i, (i + (1 if i % 2 else -1)) % count) for i in range(count)])


def stride(x, axis, step):
    count = lax.axis_size(axis)
    route = [(i, (i + (-step if i % 2 else step)) % count) for i in range(count)]
    return lax.ppermute(x, axis, route)


def after_kernel(*refs):
    pass


def after(x, *tokens, weight=0):
    return pl.pallas_call(
        after_kernel,
        out_shape=jax.ShapeDtypeStruct(x.shape, x.dtype),
        in_specs=[pl.BlockSpec(memory_space=pl.ANY)] * (1 + len(tokens)),
        out_specs=pl.BlockSpec(memory_space=pl.ANY),
        input_output_aliases={0: 0},
        name="after",
        compiler_params=pltpu.CompilerParams(vmem_limit_bytes=1024 * 1024),
        cost_estimate=pl.CostEstimate(flops=weight, bytes_accessed=0, transcendentals=0),
    )(x, *tokens)


def mean_entries(*entries):
    total = sum(e.astype(F32) for e in entries)
    return (total * (1.0 / len(entries))).astype(BF16)


def shards(queries, keys_values, out_weight):
    n_lat = lax.axis_size("lat")
    width = queries.shape[-1]
    def like(*shape):
        return jax.ShapeDtypeStruct(shape, BF16)

    pack = 2 * SPAN + 4
    q_edge, q_inner, edge_own, inner_own, pooled = pl.pallas_call(
        split_kernel,
        out_shape=[
            like(SPAN, width),
            like(SPAN, width),
            like(pack, width),
            like(2 * SPAN, width),
            like(4, width),
        ],
        in_specs=[pl.BlockSpec(memory_space=pltpu.HBM)] * 2,
        out_specs=[VMEM] * 5,
        scratch_shapes=[
            pltpu.VMEM(queries.shape, BF16),
            pltpu.VMEM(keys_values.shape, BF16),
            pltpu.SemaphoreType.DMA((3,)),
        ],
        name="split",
        compiler_params=pltpu.CompilerParams(vmem_limit_bytes=LIMIT),
        cost_estimate=pl.CostEstimate(flops=0, bytes_accessed=2 << 20, transcendentals=0),
    )(*(pltpu.with_memory_space_constraint(x, pltpu.HBM) for x in (queries, keys_values)))
    edge_pair = swap(edge_own, "lat", 1)
    far_q_edge = outward(q_edge, "lon")
    far_q_inner = swap(q_inner, "lon", 1)
    inner_pair = swap(inner_own, "lat", 1)
    inner_hop = stride(inner_own, "lat", -2)
    pooled = after(pooled, weight=4 * WEIGHT)
    edge_pair = after(edge_pair, pooled, far_q_edge, far_q_inner, inner_hop)
    edge_far = stride(edge_pair, "lat", 2)
    inner_far = swap(inner_hop, "lat", 1)
    level0 = pooled.reshape(2, 2, width)
    level0_lat = edge_pair[2 * SPAN :].reshape(2, 2, width)
    mine = mean_entries(level0[:, 0:1], level0[:, 1:2], level0_lat[:, 0:1], level0_lat[:, 1:2])
    beside = swap(jnp.concatenate([level0, level0_lat, mine], axis=1), "lon", 1)
    group = jnp.concatenate([mine, beside[:, 4:5]], axis=1)
    group_lon = swap(group, "lon", 2)
    group_both = jnp.concatenate([group, group_lon], axis=1)
    group_lat = swap(after(group_both, inner_pair), "lat", 2)
    coarse = jnp.concatenate([level0_lat, beside[:, 0:4], group_lon, group_lat], axis=1)
    count = coarse.shape[1] // 2
    coarse = jnp.pad(coarse, ((0, 0), (0, 16 - 2 * count), (0, 0)))

    back = jax.ShapeDtypeStruct((SPAN, width + HEAD_DIM), BF16)
    flops = 4 * SPAN * 3 * SPAN * width
    edge_part = call(
        functools.partial(partial_kernel, n_lat),
        [back],
        "edge_part",
        flops,
        far_q_edge,
        edge_own,
        edge_pair,
        edge_far,
    )[0]
    edge_back = outward(edge_part, "lon")
    inner_far = after(inner_far, edge_part)
    inner_part = call(
        functools.partial(partial_kernel, n_lat),
        [back],
        "inner_part",
        flops,
        far_q_inner,
        inner_own,
        inner_pair,
        inner_far,
    )[0]
    inner_back = swap(inner_part, "lon", 1)
    coarse = after(coarse, inner_part)
    own, lse = call(
        functools.partial(own_kernel, n_lat, count),
        [
            jax.ShapeDtypeStruct((2 * SPAN, width), F32),
            jax.ShapeDtypeStruct((2 * SPAN, HEAD_DIM), F32),
        ],
        "own_part",
        4 * flops,
        edge_own,
        inner_own,
        edge_pair,
        inner_pair,
        edge_far,
        inner_far,
        q_inner,
        q_edge,
        coarse,
    )
    edge_back = after(edge_back, own, weight=WEIGHT)
    return call(
        merge_kernel,
        [jax.ShapeDtypeStruct(queries.shape, BF16)],
        "merge",
        4 * SPAN * width * width,
        own,
        lse,
        edge_back,
        inner_back,
        out_weight,
    )[0]


def solution(mesh):
    return jax.shard_map(
        shards,
        mesh=mesh,
        in_specs=(P("lat", "lon", None), P(None, "lat", "lon", None), P()),
        out_specs=P("lat", "lon", None),
        check_vma=False,
    )
```

```python
import functools
import math

import jax
import jax.numpy as jnp
from jax import lax
from jax.experimental import pallas as pl
from jax.experimental.pallas import tpu as pltpu
from jax.sharding import PartitionSpec as P

HEADS = 8
HEAD_DIM = 128
TILE = 8
SPAN = TILE * TILE
SCALE = 1.0 / math.sqrt(HEAD_DIM)
NEG = -1e30
WEIGHT = 2 * 10**8
LIMIT = 16 * 1024 * 1024
F32 = jnp.float32
BF16 = jnp.bfloat16
VMEM = pl.BlockSpec(memory_space=pltpu.VMEM)


def call(kernel, outs, name, flops, *args):
    moved = sum(a.size * a.dtype.itemsize for a in args)
    moved += sum(math.prod(o.shape) * o.dtype.itemsize for o in outs)
    return pl.pallas_call(
        kernel,
        out_shape=outs,
        in_specs=[VMEM] * len(args),
        out_specs=[VMEM] * len(outs),
        name=name,
        compiler_params=pltpu.CompilerParams(vmem_limit_bytes=LIMIT),
        cost_estimate=pl.CostEstimate(flops=flops, bytes_accessed=moved, transcendentals=0),
    )(*args)


def odd_column():
    return lax.rem(lax.axis_index("lon"), 2) == 1


def far_exists(n_lat):
    row = lax.axis_index("lat")
    return jnp.where(lax.rem(row, 2) == 1, row < n_lat - 1, row > 0)


def split_tiles(x, odd):
    cut = x.reshape(TILE, 2, TILE, x.shape[-1])
    left = cut[:, 0].reshape(SPAN, x.shape[-1])
    right = cut[:, 1].reshape(SPAN, x.shape[-1])
    return jnp.where(odd, right, left), jnp.where(odd, left, right)


def split_kernel(q_hbm, kv_hbm, *refs):
    ke_ref, ve_ref, ki_ref, vi_ref, qi_ref, qe_ref, pool_ref, q_ref, kv_ref, sems = refs
    copies = [pltpu.make_async_copy(kv_hbm.at[i], kv_ref.at[i], sems.at[i]) for i in range(2)]
    copies.append(pltpu.make_async_copy(q_hbm, q_ref, sems.at[2]))
    for copy in copies:
        copy.start()
    odd = odd_column()
    pooled = []
    for half, edge_ref, inner_ref in ((0, ke_ref, ki_ref), (1, ve_ref, vi_ref)):
        copies[half].wait()
        edge, inner = split_tiles(kv_ref[half].astype(F32), odd)
        edge_ref[:SPAN] = edge.astype(BF16)
        inner_ref[...] = inner.astype(BF16)
        for tile in (edge, inner):
            pooled.append(jnp.sum(tile, axis=0, keepdims=True) * (1.0 / SPAN))
    pooled = jnp.concatenate(pooled, axis=0).astype(BF16)
    pool_ref[...] = pooled
    ke_ref[SPAN:] = pooled
    copies[2].wait()
    edge, inner = split_tiles(q_ref[...].astype(F32), odd)
    qe_ref[...] = edge.astype(BF16)
    qi_ref[...] = inner.astype(BF16)


def logits(q, k):
    return lax.dot_general(q, k, (((1,), (1,)), ((), ())), preferred_element_type=F32) * SCALE


def heads():
    return [slice(h * HEAD_DIM, (h + 1) * HEAD_DIM) for h in range(HEADS)]


def stacked(refs, cols):
    return jnp.concatenate([r[:SPAN, cols] for r in refs], axis=0)


def partial_kernel(n_lat, q_ref, *refs):
    keys, values, out_ref = refs[:3], refs[3:6], refs[6]
    far = far_exists(n_lat)
    lane = lax.broadcasted_iota(jnp.int32, (SPAN, 3 * SPAN), 1)
    keep = jnp.logical_or(lane < 2 * SPAN, far)
    column = lax.broadcasted_iota(jnp.int32, (SPAN, HEAD_DIM), 1)
    scores = [
        jnp.where(keep, logits(q_ref[:, cols], stacked(keys, cols)), NEG) for cols in heads()
    ]
    tops = [jnp.max(s, axis=-1, keepdims=True) for s in scores]
    expos = [jnp.exp(s - top) for s, top in zip(scores, tops)]
    totals = [jnp.sum(e, axis=-1, keepdims=True) for e in expos]
    parts = [
        jnp.dot(e.astype(BF16), stacked(values, cols), preferred_element_type=F32)
        for e, cols in zip(expos, heads())
    ]
    stats = jnp.zeros((SPAN, HEAD_DIM), F32)
    for h in range(HEADS):
        lse = tops[h] + jnp.log(totals[h])
        high = lse.astype(BF16).astype(F32)
        mid = (lse - high).astype(BF16).astype(F32)
        low = lse - high - mid
        stats = jnp.where(column == h, high, stats)
        stats = jnp.where(column == HEADS + h, mid, stats)
        stats = jnp.where(column == 2 * HEADS + h, low, stats)
    for h, cols in enumerate(heads()):
        out_ref[:, cols] = (parts[h] * (1.0 / totals[h])).astype(BF16)
    out_ref[:, HEADS * HEAD_DIM :] = stats.astype(BF16)


def own_kernel(n_lat, count, *refs):
    keys, values = refs[0:12:2], refs[1:12:2]
    qi_ref, qe_ref, coarse_ref, out_ref, lse_ref = refs[12:]
    rows = 2 * SPAN
    far = far_exists(n_lat)
    lane = lax.broadcasted_iota(jnp.int32, (rows, 6 * SPAN), 1)
    keep = jnp.logical_or(lane < 4 * SPAN, far)
    entry = lax.broadcasted_iota(jnp.int32, (rows, 2 * count), 1)
    bias = jnp.where(entry < count, math.log(SPAN), math.log(4 * SPAN)).astype(F32)
    column = lax.broadcasted_iota(jnp.int32, (rows, HEAD_DIM), 1)
    stats = jnp.zeros((rows, HEAD_DIM), F32)
    for group in range(0, HEADS, 4):
        near, coarse = [], []
        for cols in heads()[group : group + 4]:
            q = jnp.concatenate([qe_ref[:, cols], qi_ref[:, cols]], axis=0)
            near.append(jnp.where(keep, logits(q, stacked(keys, cols)), NEG))
            coarse.append(logits(q, coarse_ref[0, :, cols])[:, : 2 * count] + bias)
        tops = [
            jnp.maximum(jnp.max(n, axis=-1, keepdims=True), jnp.max(c, axis=-1, keepdims=True))
            for n, c in zip(near, coarse)
        ]
        near = [jnp.exp(n - top) for n, top in zip(near, tops)]
        coarse = [jnp.exp(c - top) for c, top in zip(coarse, tops)]
        totals = [
            jnp.sum(n, axis=-1, keepdims=True) + jnp.sum(c, axis=-1, keepdims=True)
            for n, c in zip(near, coarse)
        ]
        for i, cols in enumerate(heads()[group : group + 4]):
            part = jnp.dot(
                near[i].astype(BF16), stacked(values, cols), preferred_element_type=F32
            )
            part += jnp.dot(
                coarse[i].astype(BF16), coarse_ref[1, : 2 * count, cols], preferred_element_type=F32
            )
            out_ref[:, cols] = part * (1.0 / totals[i])
            stats = jnp.where(column == group + i, tops[i] + jnp.log(totals[i]), stats)
    lse_ref[...] = stats


def merge_kernel(own_ref, lse_ref, edge_ref, inner_ref, weight_ref, out_ref):
    width = HEADS * HEAD_DIM
    odd = odd_column()
    merged = []
    for index, back_ref in enumerate((edge_ref, inner_ref)):
        rows = slice(index * SPAN, (index + 1) * SPAN)
        stats = back_ref[:, width:].astype(F32)
        pieces = []
        for h in range(HEADS):
            cols = slice(h * HEAD_DIM, (h + 1) * HEAD_DIM)
            here = lse_ref[rows, h : h + 1]
            there = stats[:, h : h + 1] + stats[:, HEADS + h : HEADS + h + 1]
            there = there + stats[:, 2 * HEADS + h : 2 * HEADS + h + 1]
            share = 1.0 / (1.0 + jnp.exp(jnp.minimum(there - here, 80.0)))
            own = own_ref[rows, cols]
            pieces.append(own * share + back_ref[:, cols].astype(F32) * (1.0 - share))
        merged.append(jnp.concatenate(pieces, axis=1).reshape(TILE, TILE, width))
    edge, inner = merged
    left = jnp.where(odd, inner, edge)
    right = jnp.where(odd, edge, inner)
    attended = jnp.stack([left, right], axis=1).reshape(2 * SPAN, width).astype(BF16)
    mixed = jnp.dot(attended, weight_ref[...], preferred_element_type=F32)
    out_ref[...] = mixed.reshape(TILE, 2 * TILE, width).astype(BF16)


def swap(x, axis, distance):
    count = lax.axis_size(axis)
    return lax.ppermute(x, axis, [(i, i ^ distance) for i in range(count)])


def outward(x, axis):
    count = lax.axis_size(axis)
    return lax.ppermute(x, axis, [(i, (i + (1 if i % 2 else -1)) % count) for i in range(count)])


def stride(x, axis, step):
    count = lax.axis_size(axis)
    route = [(i, (i + (-step if i % 2 else step)) % count) for i in range(count)]
    return lax.ppermute(x, axis, route)


def after_kernel(*refs):
    pass


def after(x, *tokens, weight=0):
    return pl.pallas_call(
        after_kernel,
        out_shape=jax.ShapeDtypeStruct(x.shape, x.dtype),
        in_specs=[pl.BlockSpec(memory_space=pl.ANY)] * (1 + len(tokens)),
        out_specs=pl.BlockSpec(memory_space=pl.ANY),
        input_output_aliases={0: 0},
        name="after",
        compiler_params=pltpu.CompilerParams(vmem_limit_bytes=1024 * 1024),
        cost_estimate=pl.CostEstimate(flops=weight, bytes_accessed=0, transcendentals=0),
    )(x, *tokens)


def mean_entries(*entries):
    total = sum(e.astype(F32) for e in entries)
    return (total * (1.0 / len(entries))).astype(BF16)


def shards(queries, keys_values, out_weight):
    n_lat = lax.axis_size("lat")
    width = queries.shape[-1]
    def like(*shape):
        return jax.ShapeDtypeStruct(shape, BF16)

    tile = like(SPAN, width)
    ke_own, ve_own, ki_own, vi_own, q_inner, q_edge, pooled = pl.pallas_call(
        split_kernel,
        out_shape=[like(SPAN + 4, width), *[tile] * 5, like(4, width)],
        in_specs=[pl.BlockSpec(memory_space=pltpu.HBM)] * 2,
        out_specs=[VMEM] * 7,
        scratch_shapes=[
            pltpu.VMEM(queries.shape, BF16),
            pltpu.VMEM(keys_values.shape, BF16),
            pltpu.SemaphoreType.DMA((3,)),
        ],
        name="split",
        compiler_params=pltpu.CompilerParams(vmem_limit_bytes=LIMIT),
        cost_estimate=pl.CostEstimate(flops=0, bytes_accessed=2 << 20, transcendentals=0),
    )(*(pltpu.with_memory_space_constraint(x, pltpu.HBM) for x in (queries, keys_values)))
    ke_pair = swap(ke_own, "lat", 1)
    ve_pair = swap(ve_own, "lat", 1)
    vi_hop = stride(vi_own, "lat", -2)
    ki_pair = swap(ki_own, "lat", 1)
    vi_pair = swap(vi_own, "lat", 1)
    far_q_edge = outward(q_edge, "lon")
    far_q_inner = swap(q_inner, "lon", 1)
    pooled = after(pooled, weight=4 * WEIGHT)
    ke_pair = after(ke_pair, pooled, far_q_inner, vi_hop)
    ke_far = stride(ke_pair, "lat", 2)
    ki_far = stride(ki_pair, "lat", 2)
    vi_far = swap(vi_hop, "lat", 1)
    level0 = pooled.reshape(2, 2, width)
    level0_lat = ke_pair[SPAN:].reshape(2, 2, width)
    mine = mean_entries(level0[:, 0:1], level0[:, 1:2], level0_lat[:, 0:1], level0_lat[:, 1:2])
    three = jnp.concatenate([level0, level0_lat, mine], axis=1)
    beside = swap(three, "lon", 1)
    ve_pair = after(ve_pair, far_q_edge, beside)
    ve_far = stride(ve_pair, "lat", 2)
    group = jnp.concatenate([mine, beside[:, 4:5]], axis=1)
    group_lon = swap(group, "lon", 2)
    both = jnp.concatenate([group, group_lon], axis=1)
    both = after(both, ki_pair)
    group_lat = swap(both, "lat", 2)
    coarse = jnp.concatenate([level0_lat, beside[:, 0:4], group_lon, group_lat], axis=1)
    count = coarse.shape[1] // 2
    coarse = jnp.pad(coarse, ((0, 0), (0, 16 - 2 * count), (0, 0)))

    back = like(SPAN, width + HEAD_DIM)
    flops = 4 * SPAN * 3 * SPAN * width
    part = functools.partial(partial_kernel, n_lat)
    edge = (ke_own, ke_pair, ke_far, ve_own, ve_pair, ve_far)
    edge_part = call(part, [back], "edge_part", flops, far_q_edge, *edge)[0]
    edge_back = outward(edge_part, "lon")
    vi_far = after(vi_far, edge_part)
    inner = (ki_own, ki_pair, ki_far, vi_own, vi_pair, vi_far)
    inner_part = call(part, [back], "inner_part", flops, far_q_inner, *inner)[0]
    inner_back = swap(inner_part, "lon", 1)
    coarse = after(coarse, inner_part)
    own_tiles = (ke_own, ve_own, ki_own, vi_own)
    pair_tiles = (ke_pair, ve_pair, ki_pair, vi_pair)
    far_tiles = (ke_far, ve_far, ki_far, vi_far)
    own, lse = call(
        functools.partial(own_kernel, n_lat, count),
        [
            jax.ShapeDtypeStruct((2 * SPAN, width), F32),
            jax.ShapeDtypeStruct((2 * SPAN, HEAD_DIM), F32),
        ],
        "own_part",
        4 * flops,
        *own_tiles,
        *pair_tiles,
        *far_tiles,
        q_inner,
        q_edge,
        coarse,
    )
    edge_back = after(edge_back, own, weight=WEIGHT)
    return call(
        merge_kernel,
        [jax.ShapeDtypeStruct(queries.shape, BF16)],
        "merge",
        4 * SPAN * width * width,
        own,
        lse,
        edge_back,
        inner_back,
        out_weight,
    )[0]


def solution(mesh):
    return jax.shard_map(
        shards,
        mesh=mesh,
        in_specs=(P("lat", "lon", None), P(None, "lat", "lon", None), P()),
        out_specs=P("lat", "lon", None),
        check_vma=False,
    )
```

```python
import functools
import math

import jax
import jax.numpy as jnp
from jax import lax
from jax.experimental import pallas as pl
from jax.experimental.pallas import tpu as pltpu
from jax.sharding import PartitionSpec as P

HEADS = 8
HEAD_DIM = 128
TILE = 8
SPAN = TILE * TILE
SCALE = 1.0 / math.sqrt(HEAD_DIM)
NEG = -1e30
WEIGHT = 2 * 10**8
LIMIT = 16 * 1024 * 1024
F32 = jnp.float32
BF16 = jnp.bfloat16
VMEM = pl.BlockSpec(memory_space=pltpu.VMEM)


def call(kernel, outs, name, flops, *args):
    moved = sum(a.size * a.dtype.itemsize for a in args)
    moved += sum(math.prod(o.shape) * o.dtype.itemsize for o in outs)
    return pl.pallas_call(
        kernel,
        out_shape=outs,
        in_specs=[VMEM] * len(args),
        out_specs=[VMEM] * len(outs),
        name=name,
        compiler_params=pltpu.CompilerParams(vmem_limit_bytes=LIMIT),
        cost_estimate=pl.CostEstimate(flops=flops, bytes_accessed=moved, transcendentals=0),
    )(*args)


def odd_column():
    return lax.rem(lax.axis_index("lon"), 2) == 1


def far_exists(n_lat):
    row = lax.axis_index("lat")
    return jnp.where(lax.rem(row, 2) == 1, row < n_lat - 1, row > 0)


def split_tiles(x, odd):
    cut = x.reshape(TILE, 2, TILE, x.shape[-1])
    left = cut[:, 0].reshape(SPAN, x.shape[-1])
    right = cut[:, 1].reshape(SPAN, x.shape[-1])
    return jnp.where(odd, right, left), jnp.where(odd, left, right)


def split_kernel(q_hbm, kv_hbm, *refs):
    ke_ref, ve_ref, ki_ref, vi_ref, qi_ref, qe_ref, pool_ref, q_ref, kv_ref, sems = refs
    copies = [pltpu.make_async_copy(kv_hbm.at[i], kv_ref.at[i], sems.at[i]) for i in range(2)]
    copies.append(pltpu.make_async_copy(q_hbm, q_ref, sems.at[2]))
    for copy in copies:
        copy.start()
    odd = odd_column()
    pooled = []
    for half, edge_ref, inner_ref in ((0, ke_ref, ki_ref), (1, ve_ref, vi_ref)):
        copies[half].wait()
        edge, inner = split_tiles(kv_ref[half].astype(F32), odd)
        edge_ref[:SPAN] = edge.astype(BF16)
        inner_ref[...] = inner.astype(BF16)
        for tile in (edge, inner):
            pooled.append(jnp.sum(tile, axis=0, keepdims=True) * (1.0 / SPAN))
    pooled = jnp.concatenate(pooled, axis=0).astype(BF16)
    pool_ref[...] = pooled
    ke_ref[SPAN:] = pooled
    copies[2].wait()
    edge, inner = split_tiles(q_ref[...].astype(F32), odd)
    qe_ref[...] = edge.astype(BF16)
    qi_ref[...] = inner.astype(BF16)


def logits(q, k):
    return lax.dot_general(q, k, (((1,), (1,)), ((), ())), preferred_element_type=F32) * SCALE


def heads():
    return [slice(h * HEAD_DIM, (h + 1) * HEAD_DIM) for h in range(HEADS)]


def stacked(refs, cols):
    return jnp.concatenate([r[:SPAN, cols] for r in refs], axis=0)


def partial_kernel(n_lat, q_ref, *refs):
    keys, values, out_ref = refs[:3], refs[3:6], refs[6]
    far = far_exists(n_lat)
    lane = lax.broadcasted_iota(jnp.int32, (SPAN, 3 * SPAN), 1)
    keep = jnp.logical_or(lane < 2 * SPAN, far)
    column = lax.broadcasted_iota(jnp.int32, (SPAN, HEAD_DIM), 1)
    scores = [
        jnp.where(keep, logits(q_ref[:, cols], stacked(keys, cols)), NEG) for cols in heads()
    ]
    tops = [jnp.max(s, axis=-1, keepdims=True) for s in scores]
    expos = [jnp.exp(s - top) for s, top in zip(scores, tops)]
    totals = [jnp.sum(e, axis=-1, keepdims=True) for e in expos]
    parts = [
        jnp.dot(e.astype(BF16), stacked(values, cols), preferred_element_type=F32)
        for e, cols in zip(expos, heads())
    ]
    stats = jnp.zeros((SPAN, HEAD_DIM), F32)
    for h in range(HEADS):
        lse = tops[h] + jnp.log(totals[h])
        high = lse.astype(BF16).astype(F32)
        mid = (lse - high).astype(BF16).astype(F32)
        low = lse - high - mid
        stats = jnp.where(column == h, high, stats)
        stats = jnp.where(column == HEADS + h, mid, stats)
        stats = jnp.where(column == 2 * HEADS + h, low, stats)
    for h, cols in enumerate(heads()):
        out_ref[:, cols] = (parts[h] * (1.0 / totals[h])).astype(BF16)
    out_ref[:, HEADS * HEAD_DIM :] = stats.astype(BF16)


def own_kernel(n_lat, count, *refs):
    keys, values = refs[0:12:2], refs[1:12:2]
    qi_ref, qe_ref, coarse_ref, out_ref, lse_ref = refs[12:]
    rows = 2 * SPAN
    far = far_exists(n_lat)
    lane = lax.broadcasted_iota(jnp.int32, (rows, 6 * SPAN), 1)
    keep = jnp.logical_or(lane < 4 * SPAN, far)
    entry = lax.broadcasted_iota(jnp.int32, (rows, 2 * count), 1)
    bias = jnp.where(entry < count, math.log(SPAN), math.log(4 * SPAN)).astype(F32)
    column = lax.broadcasted_iota(jnp.int32, (rows, HEAD_DIM), 1)
    stats = jnp.zeros((rows, HEAD_DIM), F32)
    for group in range(0, HEADS, 4):
        near, coarse = [], []
        for cols in heads()[group : group + 4]:
            q = jnp.concatenate([qe_ref[:, cols], qi_ref[:, cols]], axis=0)
            near.append(jnp.where(keep, logits(q, stacked(keys, cols)), NEG))
            coarse.append(logits(q, coarse_ref[0, :, cols])[:, : 2 * count] + bias)
        tops = [
            jnp.maximum(jnp.max(n, axis=-1, keepdims=True), jnp.max(c, axis=-1, keepdims=True))
            for n, c in zip(near, coarse)
        ]
        near = [jnp.exp(n - top) for n, top in zip(near, tops)]
        coarse = [jnp.exp(c - top) for c, top in zip(coarse, tops)]
        totals = [
            jnp.sum(n, axis=-1, keepdims=True) + jnp.sum(c, axis=-1, keepdims=True)
            for n, c in zip(near, coarse)
        ]
        for i, cols in enumerate(heads()[group : group + 4]):
            part = jnp.dot(
                near[i].astype(BF16), stacked(values, cols), preferred_element_type=F32
            )
            part += jnp.dot(
                coarse[i].astype(BF16), coarse_ref[1, : 2 * count, cols], preferred_element_type=F32
            )
            out_ref[:, cols] = part * (1.0 / totals[i])
            stats = jnp.where(column == group + i, tops[i] + jnp.log(totals[i]), stats)
    lse_ref[...] = stats


def merge_kernel(own_ref, lse_ref, edge_ref, inner_ref, weight_ref, out_ref):
    width = HEADS * HEAD_DIM
    odd = odd_column()
    merged = []
    for index, back_ref in enumerate((edge_ref, inner_ref)):
        rows = slice(index * SPAN, (index + 1) * SPAN)
        stats = back_ref[:, width:].astype(F32)
        pieces = []
        for h in range(HEADS):
            cols = slice(h * HEAD_DIM, (h + 1) * HEAD_DIM)
            here = lse_ref[rows, h : h + 1]
            there = stats[:, h : h + 1] + stats[:, HEADS + h : HEADS + h + 1]
            there = there + stats[:, 2 * HEADS + h : 2 * HEADS + h + 1]
            share = 1.0 / (1.0 + jnp.exp(jnp.minimum(there - here, 80.0)))
            own = own_ref[rows, cols]
            pieces.append(own * share + back_ref[:, cols].astype(F32) * (1.0 - share))
        merged.append(jnp.concatenate(pieces, axis=1).reshape(TILE, TILE, width))
    edge, inner = merged
    left = jnp.where(odd, inner, edge)
    right = jnp.where(odd, edge, inner)
    attended = jnp.stack([left, right], axis=1).reshape(2 * SPAN, width).astype(BF16)
    mixed = jnp.dot(attended, weight_ref[...], preferred_element_type=F32)
    out_ref[...] = mixed.reshape(TILE, 2 * TILE, width).astype(BF16)


def swap(x, axis, distance):
    count = lax.axis_size(axis)
    return lax.ppermute(x, axis, [(i, i ^ distance) for i in range(count)])


def outward(x, axis):
    count = lax.axis_size(axis)
    return lax.ppermute(x, axis, [(i, (i + (1 if i % 2 else -1)) % count) for i in range(count)])


def stride(x, axis, step):
    count = lax.axis_size(axis)
    route = [(i, (i + (-step if i % 2 else step)) % count) for i in range(count)]
    return lax.ppermute(x, axis, route)


def after_kernel(*refs):
    pass


def after(x, *tokens, weight=0):
    return pl.pallas_call(
        after_kernel,
        out_shape=jax.ShapeDtypeStruct(x.shape, x.dtype),
        in_specs=[pl.BlockSpec(memory_space=pl.ANY)] * (1 + len(tokens)),
        out_specs=pl.BlockSpec(memory_space=pl.ANY),
        input_output_aliases={0: 0},
        name="after",
        compiler_params=pltpu.CompilerParams(vmem_limit_bytes=1024 * 1024),
        cost_estimate=pl.CostEstimate(flops=weight, bytes_accessed=0, transcendentals=0),
    )(x, *tokens)


def mean_entries(*entries):
    total = sum(e.astype(F32) for e in entries)
    return (total * (1.0 / len(entries))).astype(BF16)


def shards(queries, keys_values, out_weight):
    n_lat = lax.axis_size("lat")
    width = queries.shape[-1]
    def like(*shape):
        return jax.ShapeDtypeStruct(shape, BF16)

    tile = like(SPAN, width)
    ke_own, ve_own, ki_own, vi_own, q_inner, q_edge, pooled = pl.pallas_call(
        split_kernel,
        out_shape=[like(SPAN + 4, width), *[tile] * 5, like(4, width)],
        in_specs=[pl.BlockSpec(memory_space=pltpu.HBM)] * 2,
        out_specs=[VMEM] * 7,
        scratch_shapes=[
            pltpu.VMEM(queries.shape, BF16),
            pltpu.VMEM(keys_values.shape, BF16),
            pltpu.SemaphoreType.DMA((3,)),
        ],
        name="split",
        compiler_params=pltpu.CompilerParams(vmem_limit_bytes=LIMIT),
        cost_estimate=pl.CostEstimate(flops=0, bytes_accessed=2 << 20, transcendentals=0),
    )(*(pltpu.with_memory_space_constraint(x, pltpu.HBM) for x in (queries, keys_values)))
    ke_pair = swap(ke_own, "lat", 1)
    ve_pair = swap(ve_own, "lat", 1)
    ki_pair = swap(ki_own, "lat", 1)
    vi_pair = swap(vi_own, "lat", 1)
    far_q_edge = outward(q_edge, "lon")
    far_q_inner = swap(q_inner, "lon", 1)
    pooled = after(pooled, weight=4 * WEIGHT)
    ke_pair = after(ke_pair, pooled, far_q_inner)
    ke_far = stride(ke_pair, "lat", 2)
    ki_far = stride(ki_pair, "lat", 2)
    vi_pair = after(vi_pair, ke_far)
    vi_far = stride(vi_pair, "lat", 2)
    level0 = pooled.reshape(2, 2, width)
    level0_lat = ke_pair[SPAN:].reshape(2, 2, width)
    mine = mean_entries(level0[:, 0:1], level0[:, 1:2], level0_lat[:, 0:1], level0_lat[:, 1:2])
    three = jnp.concatenate([level0, level0_lat, mine], axis=1)
    beside = swap(three, "lon", 1)
    ve_pair = after(ve_pair, far_q_edge, beside)
    ve_far = stride(ve_pair, "lat", 2)
    group = jnp.concatenate([mine, beside[:, 4:5]], axis=1)
    group_lon = swap(group, "lon", 2)
    both = jnp.concatenate([group, group_lon], axis=1)
    group_lat = swap(both, "lat", 2)
    coarse = jnp.concatenate([level0_lat, beside[:, 0:4], group_lon, group_lat], axis=1)
    count = coarse.shape[1] // 2
    coarse = jnp.pad(coarse, ((0, 0), (0, 16 - 2 * count), (0, 0)))

    back = like(SPAN, width + HEAD_DIM)
    flops = 4 * SPAN * 3 * SPAN * width
    part = functools.partial(partial_kernel, n_lat)
    edge = (ke_own, ke_pair, ke_far, ve_own, ve_pair, ve_far)
    edge_part = call(part, [back], "edge_part", flops, far_q_edge, *edge)[0]
    edge_back = outward(edge_part, "lon")
    vi_far = after(vi_far, edge_part)
    inner = (ki_own, ki_pair, ki_far, vi_own, vi_pair, vi_far)
    inner_part = call(part, [back], "inner_part", flops, far_q_inner, *inner)[0]
    inner_back = swap(inner_part, "lon", 1)
    coarse = after(coarse, inner_part)
    own_tiles = (ke_own, ve_own, ki_own, vi_own)
    pair_tiles = (ke_pair, ve_pair, ki_pair, vi_pair)
    far_tiles = (ke_far, ve_far, ki_far, vi_far)
    own, lse = call(
        functools.partial(own_kernel, n_lat, count),
        [
            jax.ShapeDtypeStruct((2 * SPAN, width), F32),
            jax.ShapeDtypeStruct((2 * SPAN, HEAD_DIM), F32),
        ],
        "own_part",
        4 * flops,
        *own_tiles,
        *pair_tiles,
        *far_tiles,
        q_inner,
        q_edge,
        coarse,
    )
    edge_back = after(edge_back, own, weight=WEIGHT)
    return call(
        merge_kernel,
        [jax.ShapeDtypeStruct(queries.shape, BF16)],
        "merge",
        4 * SPAN * width * width,
        own,
        lse,
        edge_back,
        inner_back,
        out_weight,
    )[0]


def solution(mesh):
    return jax.shard_map(
        shards,
        mesh=mesh,
        in_specs=(P("lat", "lon", None), P(None, "lat", "lon", None), P()),
        out_specs=P("lat", "lon", None),
        check_vma=False,
    )
```

```python
import functools
import math

import jax
import jax.numpy as jnp
from jax import lax
from jax.experimental import pallas as pl
from jax.experimental.pallas import tpu as pltpu
from jax.sharding import PartitionSpec as P

HEADS = 8
HEAD_DIM = 128
TILE = 8
SPAN = TILE * TILE
SCALE = 1.0 / math.sqrt(HEAD_DIM)
NEG = -1e30
WEIGHT = 2 * 10**8
LIMIT = 16 * 1024 * 1024
F32 = jnp.float32
BF16 = jnp.bfloat16
VMEM = pl.BlockSpec(memory_space=pltpu.VMEM)


def call(kernel, outs, name, flops, *args):
    moved = sum(a.size * a.dtype.itemsize for a in args)
    moved += sum(math.prod(o.shape) * o.dtype.itemsize for o in outs)
    return pl.pallas_call(
        kernel,
        out_shape=outs,
        in_specs=[VMEM] * len(args),
        out_specs=[VMEM] * len(outs),
        name=name,
        compiler_params=pltpu.CompilerParams(vmem_limit_bytes=LIMIT),
        cost_estimate=pl.CostEstimate(flops=flops, bytes_accessed=moved, transcendentals=0),
    )(*args)


def odd_column():
    return lax.rem(lax.axis_index("lon"), 2) == 1


def far_exists(n_lat):
    row = lax.axis_index("lat")
    return jnp.where(lax.rem(row, 2) == 1, row < n_lat - 1, row > 0)


def split_tiles(x, odd):
    cut = x.reshape(TILE, 2, TILE, x.shape[-1])
    left = cut[:, 0].reshape(SPAN, x.shape[-1])
    right = cut[:, 1].reshape(SPAN, x.shape[-1])
    return jnp.where(odd, right, left), jnp.where(odd, left, right)


def split_kernel(q_hbm, kv_hbm, qe_ref, qi_ref, edge_ref, inner_ref, pool_ref, q_ref, kv_ref, sems):
    copies = [pltpu.make_async_copy(kv_hbm.at[i], kv_ref.at[i], sems.at[i]) for i in range(2)]
    copies.append(pltpu.make_async_copy(q_hbm, q_ref, sems.at[2]))
    for copy in copies:
        copy.start()
    odd = odd_column()
    pooled = []
    for half in range(2):
        copies[half].wait()
        edge, inner = split_tiles(kv_ref[half].astype(F32), odd)
        rows = slice(half * SPAN, (half + 1) * SPAN)
        edge_ref[rows] = edge.astype(BF16)
        inner_ref[rows] = inner.astype(BF16)
        for tile in (edge, inner):
            pooled.append(jnp.sum(tile, axis=0, keepdims=True) * (1.0 / SPAN))
    pooled = jnp.concatenate(pooled, axis=0).astype(BF16)
    pool_ref[...] = pooled
    edge_ref[2 * SPAN :] = pooled
    copies[2].wait()
    edge, inner = split_tiles(q_ref[...].astype(F32), odd)
    qe_ref[...] = edge.astype(BF16)
    qi_ref[...] = inner.astype(BF16)


def logits(q, k):
    return lax.dot_general(q, k, (((1,), (1,)), ((), ())), preferred_element_type=F32) * SCALE


def heads():
    return [slice(h * HEAD_DIM, (h + 1) * HEAD_DIM) for h in range(HEADS)]


def stacked(refs, half, cols):
    return jnp.concatenate([r[half * SPAN : (half + 1) * SPAN, cols] for r in refs], axis=0)


def partial_kernel(n_lat, q_ref, own_ref, pair_ref, far_ref, out_ref):
    tiles = (own_ref, pair_ref, far_ref)
    far = far_exists(n_lat)
    lane = lax.broadcasted_iota(jnp.int32, (SPAN, 3 * SPAN), 1)
    keep = jnp.logical_or(lane < 2 * SPAN, far)
    column = lax.broadcasted_iota(jnp.int32, (SPAN, HEAD_DIM), 1)
    scores = [
        jnp.where(keep, logits(q_ref[:, cols], stacked(tiles, 0, cols)), NEG) for cols in heads()
    ]
    tops = [jnp.max(s, axis=-1, keepdims=True) for s in scores]
    expos = [jnp.exp(s - top) for s, top in zip(scores, tops)]
    totals = [jnp.sum(e, axis=-1, keepdims=True) for e in expos]
    parts = [
        jnp.dot(e.astype(BF16), stacked(tiles, 1, cols), preferred_element_type=F32)
        for e, cols in zip(expos, heads())
    ]
    stats = jnp.zeros((SPAN, HEAD_DIM), F32)
    for h in range(HEADS):
        lse = tops[h] + jnp.log(totals[h])
        high = lse.astype(BF16).astype(F32)
        mid = (lse - high).astype(BF16).astype(F32)
        low = lse - high - mid
        stats = jnp.where(column == h, high, stats)
        stats = jnp.where(column == HEADS + h, mid, stats)
        stats = jnp.where(column == 2 * HEADS + h, low, stats)
    for h, cols in enumerate(heads()):
        out_ref[:, cols] = (parts[h] * (1.0 / totals[h])).astype(BF16)
    out_ref[:, HEADS * HEAD_DIM :] = stats.astype(BF16)


def own_kernel(n_lat, count, *refs):
    tiles, (qi_ref, qe_ref, coarse_ref, out_ref, lse_ref) = refs[:6], refs[6:]
    rows = 2 * SPAN
    far = far_exists(n_lat)
    lane = lax.broadcasted_iota(jnp.int32, (rows, 6 * SPAN), 1)
    keep = jnp.logical_or(lane < 4 * SPAN, far)
    entry = lax.broadcasted_iota(jnp.int32, (rows, 2 * count), 1)
    bias = jnp.where(entry < count, math.log(SPAN), math.log(4 * SPAN)).astype(F32)
    column = lax.broadcasted_iota(jnp.int32, (rows, HEAD_DIM), 1)
    stats = jnp.zeros((rows, HEAD_DIM), F32)
    for group in range(0, HEADS, 4):
        near, coarse = [], []
        for cols in heads()[group : group + 4]:
            q = jnp.concatenate([qe_ref[:, cols], qi_ref[:, cols]], axis=0)
            near.append(jnp.where(keep, logits(q, stacked(tiles, 0, cols)), NEG))
            coarse.append(logits(q, coarse_ref[0, :, cols])[:, : 2 * count] + bias)
        tops = [
            jnp.maximum(jnp.max(n, axis=-1, keepdims=True), jnp.max(c, axis=-1, keepdims=True))
            for n, c in zip(near, coarse)
        ]
        near = [jnp.exp(n - top) for n, top in zip(near, tops)]
        coarse = [jnp.exp(c - top) for c, top in zip(coarse, tops)]
        totals = [
            jnp.sum(n, axis=-1, keepdims=True) + jnp.sum(c, axis=-1, keepdims=True)
            for n, c in zip(near, coarse)
        ]
        for i, cols in enumerate(heads()[group : group + 4]):
            part = jnp.dot(
                near[i].astype(BF16), stacked(tiles, 1, cols), preferred_element_type=F32
            )
            part += jnp.dot(
                coarse[i].astype(BF16), coarse_ref[1, : 2 * count, cols], preferred_element_type=F32
            )
            out_ref[:, cols] = part * (1.0 / totals[i])
            stats = jnp.where(column == group + i, tops[i] + jnp.log(totals[i]), stats)
    lse_ref[...] = stats


def merge_kernel(own_ref, lse_ref, edge_ref, inner_ref, weight_ref, out_ref):
    width = HEADS * HEAD_DIM
    odd = odd_column()
    merged = []
    for index, back_ref in enumerate((edge_ref, inner_ref)):
        rows = slice(index * SPAN, (index + 1) * SPAN)
        stats = back_ref[:, width:].astype(F32)
        pieces = []
        for h in range(HEADS):
            cols = slice(h * HEAD_DIM, (h + 1) * HEAD_DIM)
            here = lse_ref[rows, h : h + 1]
            there = stats[:, h : h + 1] + stats[:, HEADS + h : HEADS + h + 1]
            there = there + stats[:, 2 * HEADS + h : 2 * HEADS + h + 1]
            share = 1.0 / (1.0 + jnp.exp(jnp.minimum(there - here, 80.0)))
            own = own_ref[rows, cols]
            pieces.append(own * share + back_ref[:, cols].astype(F32) * (1.0 - share))
        merged.append(jnp.concatenate(pieces, axis=1).reshape(TILE, TILE, width))
    edge, inner = merged
    left = jnp.where(odd, inner, edge)
    right = jnp.where(odd, edge, inner)
    attended = jnp.stack([left, right], axis=1).reshape(2 * SPAN, width).astype(BF16)
    mixed = jnp.dot(attended, weight_ref[...], preferred_element_type=F32)
    out_ref[...] = mixed.reshape(TILE, 2 * TILE, width).astype(BF16)


def swap(x, axis, distance):
    count = lax.axis_size(axis)
    return lax.ppermute(x, axis, [(i, i ^ distance) for i in range(count)])


def outward(x, axis):
    count = lax.axis_size(axis)
    return lax.ppermute(x, axis, [(i, (i + (1 if i % 2 else -1)) % count) for i in range(count)])


def stride(x, axis, step):
    count = lax.axis_size(axis)
    route = [(i, i + (-step if i % 2 else step)) for i in range(count)]
    return lax.ppermute(x, axis, [(s, t) for s, t in route if 0 <= t < count])


def after_kernel(*refs):
    pass


def after(x, *tokens, weight=0):
    return pl.pallas_call(
        after_kernel,
        out_shape=jax.ShapeDtypeStruct(x.shape, x.dtype),
        in_specs=[pl.BlockSpec(memory_space=pl.ANY)] * (1 + len(tokens)),
        out_specs=pl.BlockSpec(memory_space=pl.ANY),
        input_output_aliases={0: 0},
        name="after",
        compiler_params=pltpu.CompilerParams(vmem_limit_bytes=1024 * 1024),
        cost_estimate=pl.CostEstimate(flops=weight, bytes_accessed=0, transcendentals=0),
    )(x, *tokens)


def mean_entries(*entries):
    total = sum(e.astype(F32) for e in entries)
    return (total * (1.0 / len(entries))).astype(BF16)


def shards(queries, keys_values, out_weight):
    n_lat = lax.axis_size("lat")
    width = queries.shape[-1]
    def like(*shape):
        return jax.ShapeDtypeStruct(shape, BF16)

    pack = 2 * SPAN + 4
    q_edge, q_inner, edge_own, inner_own, pooled = pl.pallas_call(
        split_kernel,
        out_shape=[
            like(SPAN, width),
            like(SPAN, width),
            like(pack, width),
            like(2 * SPAN, width),
            like(4, width),
        ],
        in_specs=[pl.BlockSpec(memory_space=pltpu.HBM)] * 2,
        out_specs=[VMEM] * 5,
        scratch_shapes=[
            pltpu.VMEM(queries.shape, BF16),
            pltpu.VMEM(keys_values.shape, BF16),
            pltpu.SemaphoreType.DMA((3,)),
        ],
        name="split",
        compiler_params=pltpu.CompilerParams(vmem_limit_bytes=LIMIT),
        cost_estimate=pl.CostEstimate(flops=0, bytes_accessed=2 << 20, transcendentals=0),
    )(*(pltpu.with_memory_space_constraint(x, pltpu.HBM) for x in (queries, keys_values)))
    edge_pair = swap(edge_own, "lat", 1)
    far_q_edge = outward(q_edge, "lon")
    far_q_inner = swap(q_inner, "lon", 1)
    inner_pair = swap(inner_own, "lat", 1)
    inner_hop = stride(inner_own, "lat", -2)
    pooled = after(pooled, weight=4 * WEIGHT)
    edge_pair = after(edge_pair, pooled, far_q_edge, far_q_inner, inner_hop)
    edge_far = stride(edge_pair, "lat", 2)
    inner_far = swap(inner_hop, "lat", 1)
    level0 = pooled.reshape(2, 2, width)
    level0_lat = edge_pair[2 * SPAN :].reshape(2, 2, width)
    mine = mean_entries(level0[:, 0:1], level0[:, 1:2], level0_lat[:, 0:1], level0_lat[:, 1:2])
    beside = swap(jnp.concatenate([level0, level0_lat, mine], axis=1), "lon", 1)
    group = jnp.concatenate([mine, beside[:, 4:5]], axis=1)
    group_lon = swap(group, "lon", 2)
    group_both = jnp.concatenate([group, group_lon], axis=1)
    group_lat = swap(after(group_both, inner_pair), "lat", 2)
    coarse = jnp.concatenate([level0_lat, beside[:, 0:4], group_lon, group_lat], axis=1)
    count = coarse.shape[1] // 2
    coarse = jnp.pad(coarse, ((0, 0), (0, 16 - 2 * count), (0, 0)))

    back = jax.ShapeDtypeStruct((SPAN, width + HEAD_DIM), BF16)
    flops = 4 * SPAN * 3 * SPAN * width
    edge_part = call(
        functools.partial(partial_kernel, n_lat),
        [back],
        "edge_part",
        flops,
        far_q_edge,
        edge_own,
        edge_pair,
        edge_far,
    )[0]
    edge_back = outward(edge_part, "lon")
    inner_far = after(inner_far, edge_part)
    inner_part = call(
        functools.partial(partial_kernel, n_lat),
        [back],
        "inner_part",
        flops,
        far_q_inner,
        inner_own,
        inner_pair,
        inner_far,
    )[0]
    inner_back = swap(inner_part, "lon", 1)
    coarse = after(coarse, inner_part)
    own, lse = call(
        functools.partial(own_kernel, n_lat, count),
        [
            jax.ShapeDtypeStruct((2 * SPAN, width), F32),
            jax.ShapeDtypeStruct((2 * SPAN, HEAD_DIM), F32),
        ],
        "own_part",
        4 * flops,
        edge_own,
        inner_own,
        edge_pair,
        inner_pair,
        edge_far,
        inner_far,
        q_inner,
        q_edge,
        coarse,
    )
    edge_back = after(edge_back, own, weight=WEIGHT)
    return call(
        merge_kernel,
        [jax.ShapeDtypeStruct(queries.shape, BF16)],
        "merge",
        4 * SPAN * width * width,
        own,
        lse,
        edge_back,
        inner_back,
        out_weight,
    )[0]


def solution(mesh):
    return jax.shard_map(
        shards,
        mesh=mesh,
        in_specs=(P("lat", "lon", None), P(None, "lat", "lon", None), P()),
        out_specs=P("lat", "lon", None),
        check_vma=False,
    )
```

```python
import functools
import math

import jax
import jax.numpy as jnp
from jax import lax
from jax.experimental import pallas as pl
from jax.experimental.pallas import tpu as pltpu
from jax.sharding import PartitionSpec as P

HEADS = 8
HEAD_DIM = 128
TILE = 8
SPAN = TILE * TILE
SCALE = 1.0 / math.sqrt(HEAD_DIM)
NEG = -1e30
WEIGHT = 2 * 10**8
LIMIT = 16 * 1024 * 1024
F32 = jnp.float32
BF16 = jnp.bfloat16
VMEM = pl.BlockSpec(memory_space=pltpu.VMEM)


def call(kernel, outs, name, flops, *args):
    moved = sum(a.size * a.dtype.itemsize for a in args)
    moved += sum(math.prod(o.shape) * o.dtype.itemsize for o in outs)
    return pl.pallas_call(
        kernel,
        out_shape=outs,
        in_specs=[VMEM] * len(args),
        out_specs=[VMEM] * len(outs),
        name=name,
        compiler_params=pltpu.CompilerParams(vmem_limit_bytes=LIMIT),
        cost_estimate=pl.CostEstimate(flops=flops, bytes_accessed=moved, transcendentals=0),
    )(*args)


def odd_column():
    return lax.rem(lax.axis_index("lon"), 2) == 1


def far_exists(n_lat):
    row = lax.axis_index("lat")
    return jnp.where(lax.rem(row, 2) == 1, row < n_lat - 1, row > 0)


def split_tiles(x, odd):
    cut = x.reshape(TILE, 2, TILE, x.shape[-1])
    left = cut[:, 0].reshape(SPAN, x.shape[-1])
    right = cut[:, 1].reshape(SPAN, x.shape[-1])
    return jnp.where(odd, right, left), jnp.where(odd, left, right)


def split_kernel(q_hbm, kv_hbm, *refs):
    ke_ref, ve_ref, inner_ref, qi_ref, qe_ref, pool_ref, q_ref, kv_ref, sems = refs
    copies = [pltpu.make_async_copy(kv_hbm.at[i], kv_ref.at[i], sems.at[i]) for i in range(2)]
    copies.append(pltpu.make_async_copy(q_hbm, q_ref, sems.at[2]))
    for copy in copies:
        copy.start()
    odd = odd_column()
    pooled = []
    for half, edge_ref in enumerate((ke_ref, ve_ref)):
        copies[half].wait()
        edge, inner = split_tiles(kv_ref[half].astype(F32), odd)
        edge_ref[:SPAN] = edge.astype(BF16)
        inner_ref[half * SPAN : (half + 1) * SPAN] = inner.astype(BF16)
        for tile in (edge, inner):
            pooled.append(jnp.sum(tile, axis=0, keepdims=True) * (1.0 / SPAN))
    pooled = jnp.concatenate(pooled, axis=0).astype(BF16)
    pool_ref[...] = pooled
    ke_ref[SPAN:] = pooled
    copies[2].wait()
    edge, inner = split_tiles(q_ref[...].astype(F32), odd)
    qe_ref[...] = edge.astype(BF16)
    qi_ref[...] = inner.astype(BF16)


def logits(q, k):
    return lax.dot_general(q, k, (((1,), (1,)), ((), ())), preferred_element_type=F32) * SCALE


def heads():
    return [slice(h * HEAD_DIM, (h + 1) * HEAD_DIM) for h in range(HEADS)]


def stacked(places, cols):
    return jnp.concatenate([r[row : row + SPAN, cols] for r, row in places], axis=0)


def halves(refs, apart):
    if apart:
        return [(r, 0) for r in refs[0::2]], [(r, 0) for r in refs[1::2]]
    return [(r, 0) for r in refs], [(r, SPAN) for r in refs]


def partial_kernel(n_lat, apart, q_ref, *refs):
    keys, values = halves(refs[:-1], apart)
    out_ref = refs[-1]
    far = far_exists(n_lat)
    lane = lax.broadcasted_iota(jnp.int32, (SPAN, 3 * SPAN), 1)
    keep = jnp.logical_or(lane < 2 * SPAN, far)
    column = lax.broadcasted_iota(jnp.int32, (SPAN, HEAD_DIM), 1)
    scores = [
        jnp.where(keep, logits(q_ref[:, cols], stacked(keys, cols)), NEG) for cols in heads()
    ]
    tops = [jnp.max(s, axis=-1, keepdims=True) for s in scores]
    expos = [jnp.exp(s - top) for s, top in zip(scores, tops)]
    totals = [jnp.sum(e, axis=-1, keepdims=True) for e in expos]
    parts = [
        jnp.dot(e.astype(BF16), stacked(values, cols), preferred_element_type=F32)
        for e, cols in zip(expos, heads())
    ]
    stats = jnp.zeros((SPAN, HEAD_DIM), F32)
    for h in range(HEADS):
        lse = tops[h] + jnp.log(totals[h])
        high = lse.astype(BF16).astype(F32)
        mid = (lse - high).astype(BF16).astype(F32)
        low = lse - high - mid
        stats = jnp.where(column == h, high, stats)
        stats = jnp.where(column == HEADS + h, mid, stats)
        stats = jnp.where(column == 2 * HEADS + h, low, stats)
    for h, cols in enumerate(heads()):
        out_ref[:, cols] = (parts[h] * (1.0 / totals[h])).astype(BF16)
    out_ref[:, HEADS * HEAD_DIM :] = stats.astype(BF16)


def own_kernel(n_lat, count, *refs):
    edge_keys, edge_values = halves(refs[:6], True)
    inner_keys, inner_values = halves(refs[6:9], False)
    keys = [k for pair in zip(edge_keys, inner_keys) for k in pair]
    values = [v for pair in zip(edge_values, inner_values) for v in pair]
    qi_ref, qe_ref, coarse_ref, out_ref, lse_ref = refs[9:]
    rows = 2 * SPAN
    far = far_exists(n_lat)
    lane = lax.broadcasted_iota(jnp.int32, (rows, 6 * SPAN), 1)
    keep = jnp.logical_or(lane < 4 * SPAN, far)
    entry = lax.broadcasted_iota(jnp.int32, (rows, 2 * count), 1)
    bias = jnp.where(entry < count, math.log(SPAN), math.log(4 * SPAN)).astype(F32)
    column = lax.broadcasted_iota(jnp.int32, (rows, HEAD_DIM), 1)
    stats = jnp.zeros((rows, HEAD_DIM), F32)
    for group in range(0, HEADS, 4):
        near, coarse = [], []
        for cols in heads()[group : group + 4]:
            q = jnp.concatenate([qe_ref[:, cols], qi_ref[:, cols]], axis=0)
            near.append(jnp.where(keep, logits(q, stacked(keys, cols)), NEG))
            coarse.append(logits(q, coarse_ref[0, :, cols])[:, : 2 * count] + bias)
        tops = [
            jnp.maximum(jnp.max(n, axis=-1, keepdims=True), jnp.max(c, axis=-1, keepdims=True))
            for n, c in zip(near, coarse)
        ]
        near = [jnp.exp(n - top) for n, top in zip(near, tops)]
        coarse = [jnp.exp(c - top) for c, top in zip(coarse, tops)]
        totals = [
            jnp.sum(n, axis=-1, keepdims=True) + jnp.sum(c, axis=-1, keepdims=True)
            for n, c in zip(near, coarse)
        ]
        for i, cols in enumerate(heads()[group : group + 4]):
            part = jnp.dot(
                near[i].astype(BF16), stacked(values, cols), preferred_element_type=F32
            )
            part += jnp.dot(
                coarse[i].astype(BF16), coarse_ref[1, : 2 * count, cols], preferred_element_type=F32
            )
            out_ref[:, cols] = part * (1.0 / totals[i])
            stats = jnp.where(column == group + i, tops[i] + jnp.log(totals[i]), stats)
    lse_ref[...] = stats


def merge_kernel(own_ref, lse_ref, edge_ref, inner_ref, weight_ref, out_ref):
    width = HEADS * HEAD_DIM
    odd = odd_column()
    merged = []
    for index, back_ref in enumerate((edge_ref, inner_ref)):
        rows = slice(index * SPAN, (index + 1) * SPAN)
        stats = back_ref[:, width:].astype(F32)
        pieces = []
        for h in range(HEADS):
            cols = slice(h * HEAD_DIM, (h + 1) * HEAD_DIM)
            here = lse_ref[rows, h : h + 1]
            there = stats[:, h : h + 1] + stats[:, HEADS + h : HEADS + h + 1]
            there = there + stats[:, 2 * HEADS + h : 2 * HEADS + h + 1]
            share = 1.0 / (1.0 + jnp.exp(jnp.minimum(there - here, 80.0)))
            own = own_ref[rows, cols]
            pieces.append(own * share + back_ref[:, cols].astype(F32) * (1.0 - share))
        merged.append(jnp.concatenate(pieces, axis=1).reshape(TILE, TILE, width))
    edge, inner = merged
    left = jnp.where(odd, inner, edge)
    right = jnp.where(odd, edge, inner)
    attended = jnp.stack([left, right], axis=1).reshape(2 * SPAN, width).astype(BF16)
    mixed = jnp.dot(attended, weight_ref[...], preferred_element_type=F32)
    out_ref[...] = mixed.reshape(TILE, 2 * TILE, width).astype(BF16)


def swap(x, axis, distance):
    count = lax.axis_size(axis)
    return lax.ppermute(x, axis, [(i, i ^ distance) for i in range(count)])


def outward(x, axis):
    count = lax.axis_size(axis)
    return lax.ppermute(x, axis, [(i, (i + (1 if i % 2 else -1)) % count) for i in range(count)])


def stride(x, axis, step):
    count = lax.axis_size(axis)
    route = [(i, (i + (-step if i % 2 else step)) % count) for i in range(count)]
    return lax.ppermute(x, axis, route)


def after_kernel(*refs):
    pass


def after(x, *tokens, weight=0):
    return pl.pallas_call(
        after_kernel,
        out_shape=jax.ShapeDtypeStruct(x.shape, x.dtype),
        in_specs=[pl.BlockSpec(memory_space=pl.ANY)] * (1 + len(tokens)),
        out_specs=pl.BlockSpec(memory_space=pl.ANY),
        input_output_aliases={0: 0},
        name="after",
        compiler_params=pltpu.CompilerParams(vmem_limit_bytes=1024 * 1024),
        cost_estimate=pl.CostEstimate(flops=weight, bytes_accessed=0, transcendentals=0),
    )(x, *tokens)


def mean_entries(*entries):
    total = sum(e.astype(F32) for e in entries)
    return (total * (1.0 / len(entries))).astype(BF16)


def shards(queries, keys_values, out_weight):
    n_lat = lax.axis_size("lat")
    width = queries.shape[-1]
    def like(*shape):
        return jax.ShapeDtypeStruct(shape, BF16)

    tile = like(SPAN, width)
    ke_own, ve_own, inner_own, q_inner, q_edge, pooled = pl.pallas_call(
        split_kernel,
        out_shape=[
            like(SPAN + 4, width),
            tile,
            like(2 * SPAN, width),
            tile,
            tile,
            like(4, width),
        ],
        in_specs=[pl.BlockSpec(memory_space=pltpu.HBM)] * 2,
        out_specs=[VMEM] * 6,
        scratch_shapes=[
            pltpu.VMEM(queries.shape, BF16),
            pltpu.VMEM(keys_values.shape, BF16),
            pltpu.SemaphoreType.DMA((3,)),
        ],
        name="split",
        compiler_params=pltpu.CompilerParams(vmem_limit_bytes=LIMIT),
        cost_estimate=pl.CostEstimate(flops=0, bytes_accessed=2 << 20, transcendentals=0),
    )(*(pltpu.with_memory_space_constraint(x, pltpu.HBM) for x in (queries, keys_values)))
    ke_pair = swap(ke_own, "lat", 1)
    ve_pair = swap(ve_own, "lat", 1)
    inner_pair = swap(inner_own, "lat", 1)
    far_q_edge = outward(q_edge, "lon")
    far_q_inner = swap(q_inner, "lon", 1)
    pooled = after(pooled, weight=4 * WEIGHT)
    ke_pair = after(ke_pair, pooled, far_q_inner)
    ke_far = stride(ke_pair, "lat", 2)
    level0 = pooled.reshape(2, 2, width)
    level0_lat = ke_pair[SPAN:].reshape(2, 2, width)
    mine = mean_entries(level0[:, 0:1], level0[:, 1:2], level0_lat[:, 0:1], level0_lat[:, 1:2])
    three = jnp.concatenate([level0, level0_lat, mine], axis=1)
    beside = swap(three, "lon", 1)
    ve_pair = after(ve_pair, far_q_edge, beside)
    ve_far = stride(ve_pair, "lat", 2)
    group = jnp.concatenate([mine, beside[:, 4:5]], axis=1)
    group_lon = swap(group, "lon", 2)
    both = jnp.concatenate([group, group_lon], axis=1)
    group_lat = swap(both, "lat", 2)
    inner_pair = after(inner_pair, ke_far, ve_far, group_lon)
    inner_far = stride(inner_pair, "lat", 2)
    coarse = jnp.concatenate([level0_lat, beside[:, 0:4], group_lon, group_lat], axis=1)
    count = coarse.shape[1] // 2
    coarse = jnp.pad(coarse, ((0, 0), (0, 16 - 2 * count), (0, 0)))

    back = like(SPAN, width + HEAD_DIM)
    flops = 4 * SPAN * 3 * SPAN * width
    edge = (ke_own, ve_own, ke_pair, ve_pair, ke_far, ve_far)
    part = functools.partial(partial_kernel, n_lat, True)
    edge_part = call(part, [back], "edge_part", flops, far_q_edge, *edge)[0]
    edge_back = outward(edge_part, "lon")
    inner_far = after(inner_far, edge_part)
    inner = (inner_own, inner_pair, inner_far)
    part = functools.partial(partial_kernel, n_lat, False)
    inner_part = call(part, [back], "inner_part", flops, far_q_inner, *inner)[0]
    inner_back = swap(inner_part, "lon", 1)
    coarse = after(coarse, inner_part)
    own, lse = call(
        functools.partial(own_kernel, n_lat, count),
        [
            jax.ShapeDtypeStruct((2 * SPAN, width), F32),
            jax.ShapeDtypeStruct((2 * SPAN, HEAD_DIM), F32),
        ],
        "own_part",
        4 * flops,
        *edge,
        *inner,
        q_inner,
        q_edge,
        coarse,
    )
    edge_back = after(edge_back, own, weight=WEIGHT)
    return call(
        merge_kernel,
        [jax.ShapeDtypeStruct(queries.shape, BF16)],
        "merge",
        4 * SPAN * width * width,
        own,
        lse,
        edge_back,
        inner_back,
        out_weight,
    )[0]


def solution(mesh):
    return jax.shard_map(
        shards,
        mesh=mesh,
        in_specs=(P("lat", "lon", None), P(None, "lat", "lon", None), P()),
        out_specs=P("lat", "lon", None),
        check_vma=False,
    )
```

```python
import functools
import math

import jax
import jax.numpy as jnp
from jax import lax
from jax.experimental import pallas as pl
from jax.experimental.pallas import tpu as pltpu
from jax.sharding import PartitionSpec as P

HEADS = 8
HEAD_DIM = 128
TILE = 8
SPAN = TILE * TILE
SCALE = 1.0 / math.sqrt(HEAD_DIM)
NEG = -1e30
WEIGHT = 2 * 10**8
LIMIT = 16 * 1024 * 1024
F32 = jnp.float32
BF16 = jnp.bfloat16
VMEM = pl.BlockSpec(memory_space=pltpu.VMEM)


def call(kernel, outs, name, flops, *args):
    moved = sum(a.size * a.dtype.itemsize for a in args)
    moved += sum(math.prod(o.shape) * o.dtype.itemsize for o in outs)
    return pl.pallas_call(
        kernel,
        out_shape=outs,
        in_specs=[VMEM] * len(args),
        out_specs=[VMEM] * len(outs),
        name=name,
        compiler_params=pltpu.CompilerParams(vmem_limit_bytes=LIMIT),
        cost_estimate=pl.CostEstimate(flops=flops, bytes_accessed=moved, transcendentals=0),
    )(*args)


def odd_column():
    return lax.rem(lax.axis_index("lon"), 2) == 1


def far_exists(n_lat):
    row = lax.axis_index("lat")
    return jnp.where(lax.rem(row, 2) == 1, row < n_lat - 1, row > 0)


def split_tiles(x, odd):
    cut = x.reshape(TILE, 2, TILE, x.shape[-1])
    left = cut[:, 0].reshape(SPAN, x.shape[-1])
    right = cut[:, 1].reshape(SPAN, x.shape[-1])
    return jnp.where(odd, right, left), jnp.where(odd, left, right)


def split_kernel(q_hbm, kv_hbm, *refs):
    ke_ref, ve_ref, inner_ref, qi_ref, qe_ref, pool_ref, q_ref, kv_ref, sems = refs
    copies = [pltpu.make_async_copy(kv_hbm.at[i], kv_ref.at[i], sems.at[i]) for i in range(2)]
    copies.append(pltpu.make_async_copy(q_hbm, q_ref, sems.at[2]))
    for copy in copies:
        copy.start()
    odd = odd_column()
    pooled = []
    for half, edge_ref in enumerate((ke_ref, ve_ref)):
        copies[half].wait()
        edge, inner = split_tiles(kv_ref[half].astype(F32), odd)
        edge_ref[:SPAN] = edge.astype(BF16)
        inner_ref[half * SPAN : (half + 1) * SPAN] = inner.astype(BF16)
        for tile in (edge, inner):
            pooled.append(jnp.sum(tile, axis=0, keepdims=True) * (1.0 / SPAN))
    pooled = jnp.concatenate(pooled, axis=0).astype(BF16)
    pool_ref[...] = pooled
    ke_ref[SPAN:] = pooled
    copies[2].wait()
    edge, inner = split_tiles(q_ref[...].astype(F32), odd)
    qe_ref[...] = edge.astype(BF16)
    qi_ref[...] = inner.astype(BF16)


def logits(q, k):
    return lax.dot_general(q, k, (((1,), (1,)), ((), ())), preferred_element_type=F32) * SCALE


def heads():
    return [slice(h * HEAD_DIM, (h + 1) * HEAD_DIM) for h in range(HEADS)]


def stacked(places, cols):
    return jnp.concatenate([r[row : row + SPAN, cols] for r, row in places], axis=0)


def halves(refs, apart):
    if apart:
        return [(r, 0) for r in refs[0::2]], [(r, 0) for r in refs[1::2]]
    return [(r, 0) for r in refs], [(r, SPAN) for r in refs]


def partial_kernel(n_lat, apart, q_ref, *refs):
    keys, values = halves(refs[:-1], apart)
    out_ref = refs[-1]
    far = far_exists(n_lat)
    lane = lax.broadcasted_iota(jnp.int32, (SPAN, 3 * SPAN), 1)
    keep = jnp.logical_or(lane < 2 * SPAN, far)
    column = lax.broadcasted_iota(jnp.int32, (SPAN, HEAD_DIM), 1)
    scores = [
        jnp.where(keep, logits(q_ref[:, cols], stacked(keys, cols)), NEG) for cols in heads()
    ]
    tops = [jnp.max(s, axis=-1, keepdims=True) for s in scores]
    expos = [jnp.exp(s - top) for s, top in zip(scores, tops)]
    totals = [jnp.sum(e, axis=-1, keepdims=True) for e in expos]
    parts = [
        jnp.dot(e.astype(BF16), stacked(values, cols), preferred_element_type=F32)
        for e, cols in zip(expos, heads())
    ]
    stats = jnp.zeros((SPAN, HEAD_DIM), F32)
    for h in range(HEADS):
        lse = tops[h] + jnp.log(totals[h])
        high = lse.astype(BF16).astype(F32)
        mid = (lse - high).astype(BF16).astype(F32)
        low = lse - high - mid
        stats = jnp.where(column == h, high, stats)
        stats = jnp.where(column == HEADS + h, mid, stats)
        stats = jnp.where(column == 2 * HEADS + h, low, stats)
    for h, cols in enumerate(heads()):
        out_ref[:, cols] = (parts[h] * (1.0 / totals[h])).astype(BF16)
    out_ref[:, HEADS * HEAD_DIM :] = stats.astype(BF16)


def own_kernel(n_lat, count, *refs):
    edge_keys, edge_values = halves(refs[:6], True)
    inner_keys, inner_values = halves(refs[6:9], False)
    keys = [k for pair in zip(edge_keys, inner_keys) for k in pair]
    values = [v for pair in zip(edge_values, inner_values) for v in pair]
    qi_ref, qe_ref, coarse_ref, out_ref, lse_ref = refs[9:]
    rows = 2 * SPAN
    far = far_exists(n_lat)
    lane = lax.broadcasted_iota(jnp.int32, (rows, 6 * SPAN), 1)
    keep = jnp.logical_or(lane < 4 * SPAN, far)
    entry = lax.broadcasted_iota(jnp.int32, (rows, 2 * count), 1)
    bias = jnp.where(entry < count, math.log(SPAN), math.log(4 * SPAN)).astype(F32)
    column = lax.broadcasted_iota(jnp.int32, (rows, HEAD_DIM), 1)
    stats = jnp.zeros((rows, HEAD_DIM), F32)
    for group in range(0, HEADS, 4):
        near, coarse = [], []
        for cols in heads()[group : group + 4]:
            q = jnp.concatenate([qe_ref[:, cols], qi_ref[:, cols]], axis=0)
            near.append(jnp.where(keep, logits(q, stacked(keys, cols)), NEG))
            coarse.append(logits(q, coarse_ref[0, :, cols])[:, : 2 * count] + bias)
        tops = [
            jnp.maximum(jnp.max(n, axis=-1, keepdims=True), jnp.max(c, axis=-1, keepdims=True))
            for n, c in zip(near, coarse)
        ]
        near = [jnp.exp(n - top) for n, top in zip(near, tops)]
        coarse = [jnp.exp(c - top) for c, top in zip(coarse, tops)]
        totals = [
            jnp.sum(n, axis=-1, keepdims=True) + jnp.sum(c, axis=-1, keepdims=True)
            for n, c in zip(near, coarse)
        ]
        for i, cols in enumerate(heads()[group : group + 4]):
            part = jnp.dot(
                near[i].astype(BF16), stacked(values, cols), preferred_element_type=F32
            )
            part += jnp.dot(
                coarse[i].astype(BF16), coarse_ref[1, : 2 * count, cols], preferred_element_type=F32
            )
            out_ref[:, cols] = part * (1.0 / totals[i])
            stats = jnp.where(column == group + i, tops[i] + jnp.log(totals[i]), stats)
    lse_ref[...] = stats


def merge_kernel(own_ref, lse_ref, edge_ref, inner_ref, weight_ref, out_ref):
    width = HEADS * HEAD_DIM
    odd = odd_column()
    merged = []
    for index, back_ref in enumerate((edge_ref, inner_ref)):
        rows = slice(index * SPAN, (index + 1) * SPAN)
        stats = back_ref[:, width:].astype(F32)
        pieces = []
        for h in range(HEADS):
            cols = slice(h * HEAD_DIM, (h + 1) * HEAD_DIM)
            here = lse_ref[rows, h : h + 1]
            there = stats[:, h : h + 1] + stats[:, HEADS + h : HEADS + h + 1]
            there = there + stats[:, 2 * HEADS + h : 2 * HEADS + h + 1]
            share = 1.0 / (1.0 + jnp.exp(jnp.minimum(there - here, 80.0)))
            own = own_ref[rows, cols]
            pieces.append(own * share + back_ref[:, cols].astype(F32) * (1.0 - share))
        merged.append(jnp.concatenate(pieces, axis=1).reshape(TILE, TILE, width))
    edge, inner = merged
    left = jnp.where(odd, inner, edge)
    right = jnp.where(odd, edge, inner)
    attended = jnp.stack([left, right], axis=1).reshape(2 * SPAN, width).astype(BF16)
    mixed = jnp.dot(attended, weight_ref[...], preferred_element_type=F32)
    out_ref[...] = mixed.reshape(TILE, 2 * TILE, width).astype(BF16)


def swap(x, axis, distance):
    count = lax.axis_size(axis)
    return lax.ppermute(x, axis, [(i, i ^ distance) for i in range(count)])


def outward(x, axis):
    count = lax.axis_size(axis)
    return lax.ppermute(x, axis, [(i, (i + (1 if i % 2 else -1)) % count) for i in range(count)])


def stride(x, axis, step):
    count = lax.axis_size(axis)
    route = [(i, (i + (-step if i % 2 else step)) % count) for i in range(count)]
    return lax.ppermute(x, axis, route)


def after_kernel(*refs):
    pass


def after(x, *tokens, weight=0):
    return pl.pallas_call(
        after_kernel,
        out_shape=jax.ShapeDtypeStruct(x.shape, x.dtype),
        in_specs=[pl.BlockSpec(memory_space=pl.ANY)] * (1 + len(tokens)),
        out_specs=pl.BlockSpec(memory_space=pl.ANY),
        input_output_aliases={0: 0},
        name="after",
        compiler_params=pltpu.CompilerParams(vmem_limit_bytes=1024 * 1024),
        cost_estimate=pl.CostEstimate(flops=weight, bytes_accessed=0, transcendentals=0),
    )(x, *tokens)


def mean_entries(*entries):
    total = sum(e.astype(F32) for e in entries)
    return (total * (1.0 / len(entries))).astype(BF16)


def shards(queries, keys_values, out_weight):
    n_lat = lax.axis_size("lat")
    width = queries.shape[-1]
    def like(*shape):
        return jax.ShapeDtypeStruct(shape, BF16)

    tile = like(SPAN, width)
    ke_own, ve_own, inner_own, q_inner, q_edge, pooled = pl.pallas_call(
        split_kernel,
        out_shape=[
            like(SPAN + 4, width),
            tile,
            like(2 * SPAN, width),
            tile,
            tile,
            like(4, width),
        ],
        in_specs=[pl.BlockSpec(memory_space=pltpu.HBM)] * 2,
        out_specs=[VMEM] * 6,
        scratch_shapes=[
            pltpu.VMEM(queries.shape, BF16),
            pltpu.VMEM(keys_values.shape, BF16),
            pltpu.SemaphoreType.DMA((3,)),
        ],
        name="split",
        compiler_params=pltpu.CompilerParams(vmem_limit_bytes=LIMIT),
        cost_estimate=pl.CostEstimate(flops=0, bytes_accessed=2 << 20, transcendentals=0),
    )(*(pltpu.with_memory_space_constraint(x, pltpu.HBM) for x in (queries, keys_values)))
    ke_pair = swap(ke_own, "lat", 1)
    ve_pair = swap(ve_own, "lat", 1)
    inner_pair = swap(inner_own, "lat", 1)
    far_q_edge = outward(q_edge, "lon")
    far_q_inner = swap(q_inner, "lon", 1)
    pooled = after(pooled, weight=4 * WEIGHT)
    ke_pair = after(ke_pair, pooled, far_q_inner)
    ke_far = stride(ke_pair, "lat", 2)
    level0 = pooled.reshape(2, 2, width)
    level0_lat = ke_pair[SPAN:].reshape(2, 2, width)
    mine = mean_entries(level0[:, 0:1], level0[:, 1:2], level0_lat[:, 0:1], level0_lat[:, 1:2])
    three = jnp.concatenate([level0, level0_lat, mine], axis=1)
    beside = swap(three, "lon", 1)
    ve_pair = after(ve_pair, far_q_edge, beside)
    ve_far = stride(ve_pair, "lat", 2)
    group = jnp.concatenate([mine, beside[:, 4:5]], axis=1)
    group_lon = swap(group, "lon", 2)
    both = jnp.concatenate([group, group_lon], axis=1)
    inner_pair = after(inner_pair, ve_pair, ke_far)
    inner_far = stride(inner_pair, "lat", 2)
    back = like(SPAN, width + HEAD_DIM)
    flops = 4 * SPAN * 3 * SPAN * width
    ve_far = after(ve_far, weight=WEIGHT)
    edge = (ke_own, ve_own, ke_pair, ve_pair, ke_far, ve_far)
    part = functools.partial(partial_kernel, n_lat, True)
    edge_part = call(part, [back], "edge_part", flops, far_q_edge, *edge)[0]
    edge_back = outward(edge_part, "lon")
    both = after(both, edge_part)
    group_lat = swap(both, "lat", 2)
    coarse = jnp.concatenate([level0_lat, beside[:, 0:4], group_lon, group_lat], axis=1)
    count = coarse.shape[1] // 2
    coarse = jnp.pad(coarse, ((0, 0), (0, 16 - 2 * count), (0, 0)))
    inner_far = after(inner_far, edge_part)
    inner = (inner_own, inner_pair, inner_far)
    part = functools.partial(partial_kernel, n_lat, False)
    inner_part = call(part, [back], "inner_part", flops, far_q_inner, *inner)[0]
    inner_back = swap(inner_part, "lon", 1)
    coarse = after(coarse, inner_part)
    own, lse = call(
        functools.partial(own_kernel, n_lat, count),
        [
            jax.ShapeDtypeStruct((2 * SPAN, width), F32),
            jax.ShapeDtypeStruct((2 * SPAN, HEAD_DIM), F32),
        ],
        "own_part",
        4 * flops,
        *edge,
        *inner,
        q_inner,
        q_edge,
        coarse,
    )
    edge_back = after(edge_back, own, weight=WEIGHT)
    return call(
        merge_kernel,
        [jax.ShapeDtypeStruct(queries.shape, BF16)],
        "merge",
        4 * SPAN * width * width,
        own,
        lse,
        edge_back,
        inner_back,
        out_weight,
    )[0]


def solution(mesh):
    return jax.shard_map(
        shards,
        mesh=mesh,
        in_specs=(P("lat", "lon", None), P(None, "lat", "lon", None), P()),
        out_specs=P("lat", "lon", None),
        check_vma=False,
    )
```

```python
import functools
import math

import jax
import jax.numpy as jnp
from jax import lax
from jax.experimental import pallas as pl
from jax.experimental.pallas import tpu as pltpu
from jax.sharding import PartitionSpec as P

HEADS = 8
HEAD_DIM = 128
TILE = 8
SPAN = TILE * TILE
SCALE = 1.0 / math.sqrt(HEAD_DIM)
NEG = -1e30
WEIGHT = 2 * 10**8
LIMIT = 16 * 1024 * 1024
F32 = jnp.float32
BF16 = jnp.bfloat16
VMEM = pl.BlockSpec(memory_space=pltpu.VMEM)


def call(kernel, outs, name, flops, *args):
    moved = sum(a.size * a.dtype.itemsize for a in args)
    moved += sum(math.prod(o.shape) * o.dtype.itemsize for o in outs)
    return pl.pallas_call(
        kernel,
        out_shape=outs,
        in_specs=[VMEM] * len(args),
        out_specs=[VMEM] * len(outs),
        name=name,
        compiler_params=pltpu.CompilerParams(vmem_limit_bytes=LIMIT),
        cost_estimate=pl.CostEstimate(flops=flops, bytes_accessed=moved, transcendentals=0),
    )(*args)


def odd_column():
    return lax.rem(lax.axis_index("lon"), 2) == 1


def far_exists(n_lat):
    row = lax.axis_index("lat")
    return jnp.where(lax.rem(row, 2) == 1, row < n_lat - 1, row > 0)


def split_tiles(x, odd):
    cut = x.reshape(TILE, 2, TILE, x.shape[-1])
    left = cut[:, 0].reshape(SPAN, x.shape[-1])
    right = cut[:, 1].reshape(SPAN, x.shape[-1])
    return jnp.where(odd, right, left), jnp.where(odd, left, right)


def split_kernel(q_hbm, kv_hbm, qe_ref, qi_ref, edge_ref, inner_ref, pool_ref, q_ref, kv_ref, sems):
    copies = [pltpu.make_async_copy(kv_hbm.at[i], kv_ref.at[i], sems.at[i]) for i in range(2)]
    copies.append(pltpu.make_async_copy(q_hbm, q_ref, sems.at[2]))
    for copy in copies:
        copy.start()
    odd = odd_column()
    pooled = []
    for half in range(2):
        copies[half].wait()
        edge, inner = split_tiles(kv_ref[half].astype(F32), odd)
        rows = slice(half * SPAN, (half + 1) * SPAN)
        edge_ref[rows] = edge.astype(BF16)
        inner_ref[rows] = inner.astype(BF16)
        for tile in (edge, inner):
            pooled.append(jnp.sum(tile, axis=0, keepdims=True) * (1.0 / SPAN))
    pooled = jnp.concatenate(pooled, axis=0).astype(BF16)
    pool_ref[...] = pooled
    edge_ref[2 * SPAN :] = pooled
    copies[2].wait()
    edge, inner = split_tiles(q_ref[...].astype(F32), odd)
    qe_ref[...] = edge.astype(BF16)
    qi_ref[...] = inner.astype(BF16)


def logits(q, k):
    return lax.dot_general(q, k, (((1,), (1,)), ((), ())), preferred_element_type=F32) * SCALE


def heads():
    return [slice(h * HEAD_DIM, (h + 1) * HEAD_DIM) for h in range(HEADS)]


def stacked(refs, half, cols):
    return jnp.concatenate([r[half * SPAN : (half + 1) * SPAN, cols] for r in refs], axis=0)


def partial_kernel(n_lat, q_ref, own_ref, pair_ref, far_ref, out_ref):
    tiles = (own_ref, pair_ref, far_ref)
    far = far_exists(n_lat)
    lane = lax.broadcasted_iota(jnp.int32, (SPAN, 3 * SPAN), 1)
    keep = jnp.logical_or(lane < 2 * SPAN, far)
    column = lax.broadcasted_iota(jnp.int32, (SPAN, HEAD_DIM), 1)
    scores = [
        jnp.where(keep, logits(q_ref[:, cols], stacked(tiles, 0, cols)), NEG) for cols in heads()
    ]
    tops = [jnp.max(s, axis=-1, keepdims=True) for s in scores]
    expos = [jnp.exp(s - top) for s, top in zip(scores, tops)]
    totals = [jnp.sum(e, axis=-1, keepdims=True) for e in expos]
    parts = [
        jnp.dot(e.astype(BF16), stacked(tiles, 1, cols), preferred_element_type=F32)
        for e, cols in zip(expos, heads())
    ]
    stats = jnp.zeros((SPAN, HEAD_DIM), F32)
    for h in range(HEADS):
        lse = tops[h] + jnp.log(totals[h])
        high = lse.astype(BF16).astype(F32)
        mid = (lse - high).astype(BF16).astype(F32)
        low = lse - high - mid
        stats = jnp.where(column == h, high, stats)
        stats = jnp.where(column == HEADS + h, mid, stats)
        stats = jnp.where(column == 2 * HEADS + h, low, stats)
    for h, cols in enumerate(heads()):
        out_ref[:, cols] = (parts[h] * (1.0 / totals[h])).astype(BF16)
    out_ref[:, HEADS * HEAD_DIM :] = stats.astype(BF16)


def own_kernel(n_lat, count, *refs):
    tiles, (qi_ref, qe_ref, coarse_ref, out_ref, lse_ref) = refs[:6], refs[6:]
    rows = 2 * SPAN
    far = far_exists(n_lat)
    lane = lax.broadcasted_iota(jnp.int32, (rows, 6 * SPAN), 1)
    keep = jnp.logical_or(lane < 4 * SPAN, far)
    entry = lax.broadcasted_iota(jnp.int32, (rows, 2 * count), 1)
    bias = jnp.where(entry < count, math.log(SPAN), math.log(4 * SPAN)).astype(F32)
    column = lax.broadcasted_iota(jnp.int32, (rows, HEAD_DIM), 1)
    stats = jnp.zeros((rows, HEAD_DIM), F32)
    for group in range(0, HEADS, 4):
        near, coarse = [], []
        for cols in heads()[group : group + 4]:
            q = jnp.concatenate([qe_ref[:, cols], qi_ref[:, cols]], axis=0)
            near.append(jnp.where(keep, logits(q, stacked(tiles, 0, cols)), NEG))
            coarse.append(logits(q, coarse_ref[0, :, cols])[:, : 2 * count] + bias)
        tops = [
            jnp.maximum(jnp.max(n, axis=-1, keepdims=True), jnp.max(c, axis=-1, keepdims=True))
            for n, c in zip(near, coarse)
        ]
        near = [jnp.exp(n - top) for n, top in zip(near, tops)]
        coarse = [jnp.exp(c - top) for c, top in zip(coarse, tops)]
        totals = [
            jnp.sum(n, axis=-1, keepdims=True) + jnp.sum(c, axis=-1, keepdims=True)
            for n, c in zip(near, coarse)
        ]
        for i, cols in enumerate(heads()[group : group + 4]):
            part = jnp.dot(
                near[i].astype(BF16), stacked(tiles, 1, cols), preferred_element_type=F32
            )
            part += jnp.dot(
                coarse[i].astype(BF16), coarse_ref[1, : 2 * count, cols], preferred_element_type=F32
            )
            out_ref[:, cols] = part * (1.0 / totals[i])
            stats = jnp.where(column == group + i, tops[i] + jnp.log(totals[i]), stats)
    lse_ref[...] = stats


def merge_kernel(own_ref, lse_ref, edge_ref, inner_ref, weight_ref, out_ref):
    width = HEADS * HEAD_DIM
    odd = odd_column()
    merged = []
    for index, back_ref in enumerate((edge_ref, inner_ref)):
        rows = slice(index * SPAN, (index + 1) * SPAN)
        stats = back_ref[:, width:].astype(F32)
        pieces = []
        for h in range(HEADS):
            cols = slice(h * HEAD_DIM, (h + 1) * HEAD_DIM)
            here = lse_ref[rows, h : h + 1]
            there = stats[:, h : h + 1] + stats[:, HEADS + h : HEADS + h + 1]
            there = there + stats[:, 2 * HEADS + h : 2 * HEADS + h + 1]
            share = 1.0 / (1.0 + jnp.exp(jnp.minimum(there - here, 80.0)))
            own = own_ref[rows, cols]
            pieces.append(own * share + back_ref[:, cols].astype(F32) * (1.0 - share))
        merged.append(jnp.concatenate(pieces, axis=1).reshape(TILE, TILE, width))
    edge, inner = merged
    left = jnp.where(odd, inner, edge)
    right = jnp.where(odd, edge, inner)
    attended = jnp.stack([left, right], axis=1).reshape(2 * SPAN, width).astype(BF16)
    mixed = jnp.dot(attended, weight_ref[...], preferred_element_type=F32)
    out_ref[...] = mixed.reshape(TILE, 2 * TILE, width).astype(BF16)


def swap(x, axis, distance):
    count = lax.axis_size(axis)
    return lax.ppermute(x, axis, [(i, i ^ distance) for i in range(count)])


def outward(x, axis):
    count = lax.axis_size(axis)
    return lax.ppermute(x, axis, [(i, (i + (1 if i % 2 else -1)) % count) for i in range(count)])


def stride(x, axis, step):
    count = lax.axis_size(axis)
    route = [(i, (i + (-step if i % 2 else step)) % count) for i in range(count)]
    return lax.ppermute(x, axis, route)


def after_kernel(*refs):
    pass


def after(x, *tokens, weight=0):
    return pl.pallas_call(
        after_kernel,
        out_shape=jax.ShapeDtypeStruct(x.shape, x.dtype),
        in_specs=[pl.BlockSpec(memory_space=pl.ANY)] * (1 + len(tokens)),
        out_specs=pl.BlockSpec(memory_space=pl.ANY),
        input_output_aliases={0: 0},
        name="after",
        compiler_params=pltpu.CompilerParams(vmem_limit_bytes=1024 * 1024),
        cost_estimate=pl.CostEstimate(flops=weight, bytes_accessed=0, transcendentals=0),
    )(x, *tokens)


def mean_entries(*entries):
    total = sum(e.astype(F32) for e in entries)
    return (total * (1.0 / len(entries))).astype(BF16)


def shards(queries, keys_values, out_weight):
    n_lat = lax.axis_size("lat")
    width = queries.shape[-1]
    def like(*shape):
        return jax.ShapeDtypeStruct(shape, BF16)

    pack = 2 * SPAN + 4
    q_edge, q_inner, edge_own, inner_own, pooled = pl.pallas_call(
        split_kernel,
        out_shape=[
            like(SPAN, width),
            like(SPAN, width),
            like(pack, width),
            like(2 * SPAN, width),
            like(4, width),
        ],
        in_specs=[pl.BlockSpec(memory_space=pltpu.HBM)] * 2,
        out_specs=[VMEM] * 5,
        scratch_shapes=[
            pltpu.VMEM(queries.shape, BF16),
            pltpu.VMEM(keys_values.shape, BF16),
            pltpu.SemaphoreType.DMA((3,)),
        ],
        name="split",
        compiler_params=pltpu.CompilerParams(vmem_limit_bytes=LIMIT),
        cost_estimate=pl.CostEstimate(flops=0, bytes_accessed=2 << 20, transcendentals=0),
    )(*(pltpu.with_memory_space_constraint(x, pltpu.HBM) for x in (queries, keys_values)))
    edge_pair = swap(edge_own, "lat", 1)
    far_q_edge = outward(q_edge, "lon")
    far_q_inner = swap(q_inner, "lon", 1)
    inner_pair = swap(inner_own, "lat", 1)
    inner_hop = stride(inner_own, "lat", -2)
    pooled = after(pooled, weight=4 * WEIGHT)
    edge_pair = after(edge_pair, pooled, far_q_edge, far_q_inner, inner_hop)
    edge_far = stride(edge_pair, "lat", 2)
    inner_far = swap(inner_hop, "lat", 1)
    level0 = pooled.reshape(2, 2, width)
    level0_lat = edge_pair[2 * SPAN :].reshape(2, 2, width)
    mine = mean_entries(level0[:, 0:1], level0[:, 1:2], level0_lat[:, 0:1], level0_lat[:, 1:2])
    beside = swap(jnp.concatenate([level0, level0_lat, mine], axis=1), "lon", 1)
    group = jnp.concatenate([mine, beside[:, 4:5]], axis=1)
    group_lon = swap(group, "lon", 2)
    group_lat = swap(jnp.concatenate([group, group_lon], axis=1), "lat", 2)
    coarse = jnp.concatenate([level0_lat, beside[:, 0:4], group_lon, group_lat], axis=1)
    count = coarse.shape[1] // 2
    coarse = jnp.pad(coarse, ((0, 0), (0, 16 - 2 * count), (0, 0)))

    back = jax.ShapeDtypeStruct((SPAN, width + HEAD_DIM), BF16)
    flops = 4 * SPAN * 3 * SPAN * width
    edge_part = call(
        functools.partial(partial_kernel, n_lat),
        [back],
        "edge_part",
        flops,
        far_q_edge,
        edge_own,
        edge_pair,
        edge_far,
    )[0]
    edge_back = outward(edge_part, "lon")
    inner_far = after(inner_far, edge_part)
    inner_part = call(
        functools.partial(partial_kernel, n_lat),
        [back],
        "inner_part",
        flops,
        far_q_inner,
        inner_own,
        inner_pair,
        inner_far,
    )[0]
    inner_back = swap(inner_part, "lon", 1)
    coarse = after(coarse, inner_part)
    own, lse = call(
        functools.partial(own_kernel, n_lat, count),
        [
            jax.ShapeDtypeStruct((2 * SPAN, width), F32),
            jax.ShapeDtypeStruct((2 * SPAN, HEAD_DIM), F32),
        ],
        "own_part",
        4 * flops,
        edge_own,
        inner_own,
        edge_pair,
        inner_pair,
        edge_far,
        inner_far,
        q_inner,
        q_edge,
        coarse,
    )
    edge_back = after(edge_back, own, weight=WEIGHT)
    return call(
        merge_kernel,
        [jax.ShapeDtypeStruct(queries.shape, BF16)],
        "merge",
        4 * SPAN * width * width,
        own,
        lse,
        edge_back,
        inner_back,
        out_weight,
    )[0]


def solution(mesh):
    return jax.shard_map(
        shards,
        mesh=mesh,
        in_specs=(P("lat", "lon", None), P(None, "lat", "lon", None), P()),
        out_specs=P("lat", "lon", None),
        check_vma=False,
    )
```

```python
import functools
import math

import jax
import jax.numpy as jnp
from jax import lax
from jax.experimental import pallas as pl
from jax.experimental.pallas import tpu as pltpu
from jax.sharding import PartitionSpec as P

HEADS = 8
HEAD_DIM = 128
TILE = 8
SPAN = TILE * TILE
SCALE = 1.0 / math.sqrt(HEAD_DIM)
NEG = -1e30
WEIGHT = 2 * 10**8
LIMIT = 16 * 1024 * 1024
F32 = jnp.float32
BF16 = jnp.bfloat16
VMEM = pl.BlockSpec(memory_space=pltpu.VMEM)


def call(kernel, outs, name, flops, *args):
    moved = sum(a.size * a.dtype.itemsize for a in args)
    moved += sum(math.prod(o.shape) * o.dtype.itemsize for o in outs)
    return pl.pallas_call(
        kernel,
        out_shape=outs,
        in_specs=[VMEM] * len(args),
        out_specs=[VMEM] * len(outs),
        name=name,
        compiler_params=pltpu.CompilerParams(vmem_limit_bytes=LIMIT),
        cost_estimate=pl.CostEstimate(flops=flops, bytes_accessed=moved, transcendentals=0),
    )(*args)


def odd_column():
    return lax.rem(lax.axis_index("lon"), 2) == 1


def far_exists(n_lat):
    row = lax.axis_index("lat")
    return jnp.where(lax.rem(row, 2) == 1, row < n_lat - 1, row > 0)


def split_tiles(x, odd):
    cut = x.reshape(TILE, 2, TILE, x.shape[-1])
    left = cut[:, 0].reshape(SPAN, x.shape[-1])
    right = cut[:, 1].reshape(SPAN, x.shape[-1])
    return jnp.where(odd, right, left), jnp.where(odd, left, right)


def split_kernel(q_hbm, kv_hbm, qe_ref, qi_ref, edge_ref, inner_ref, pool_ref, q_ref, kv_ref, sems):
    copies = [pltpu.make_async_copy(kv_hbm.at[i], kv_ref.at[i], sems.at[i]) for i in range(2)]
    copies.append(pltpu.make_async_copy(q_hbm, q_ref, sems.at[2]))
    for copy in copies:
        copy.start()
    odd = odd_column()
    pooled = []
    for half in range(2):
        copies[half].wait()
        edge, inner = split_tiles(kv_ref[half].astype(F32), odd)
        rows = slice(half * SPAN, (half + 1) * SPAN)
        edge_ref[rows] = edge.astype(BF16)
        inner_ref[rows] = inner.astype(BF16)
        for tile in (edge, inner):
            pooled.append(jnp.sum(tile, axis=0, keepdims=True) * (1.0 / SPAN))
    pooled = jnp.concatenate(pooled, axis=0).astype(BF16)
    pool_ref[...] = pooled
    edge_ref[2 * SPAN :] = pooled
    copies[2].wait()
    edge, inner = split_tiles(q_ref[...].astype(F32), odd)
    qe_ref[...] = edge.astype(BF16)
    qi_ref[...] = inner.astype(BF16)


def logits(q, k):
    return lax.dot_general(q, k, (((1,), (1,)), ((), ())), preferred_element_type=F32) * SCALE


def heads():
    return [slice(h * HEAD_DIM, (h + 1) * HEAD_DIM) for h in range(HEADS)]


def stacked(refs, half, cols):
    return jnp.concatenate([r[half * SPAN : (half + 1) * SPAN, cols] for r in refs], axis=0)


def partial_kernel(n_lat, q_ref, own_ref, pair_ref, far_ref, out_ref):
    tiles = (own_ref, pair_ref, far_ref)
    far = far_exists(n_lat)
    lane = lax.broadcasted_iota(jnp.int32, (SPAN, 3 * SPAN), 1)
    keep = jnp.logical_or(lane < 2 * SPAN, far)
    column = lax.broadcasted_iota(jnp.int32, (SPAN, HEAD_DIM), 1)
    scores = [
        jnp.where(keep, logits(q_ref[:, cols], stacked(tiles, 0, cols)), NEG) for cols in heads()
    ]
    tops = [jnp.max(s, axis=-1, keepdims=True) for s in scores]
    expos = [jnp.exp(s - top) for s, top in zip(scores, tops)]
    totals = [jnp.sum(e, axis=-1, keepdims=True) for e in expos]
    parts = [
        jnp.dot(e.astype(BF16), stacked(tiles, 1, cols), preferred_element_type=F32)
        for e, cols in zip(expos, heads())
    ]
    stats = jnp.zeros((SPAN, HEAD_DIM), F32)
    for h in range(HEADS):
        lse = tops[h] + jnp.log(totals[h])
        high = lse.astype(BF16).astype(F32)
        mid = (lse - high).astype(BF16).astype(F32)
        low = lse - high - mid
        stats = jnp.where(column == h, high, stats)
        stats = jnp.where(column == HEADS + h, mid, stats)
        stats = jnp.where(column == 2 * HEADS + h, low, stats)
    for h, cols in enumerate(heads()):
        out_ref[:, cols] = (parts[h] * (1.0 / totals[h])).astype(BF16)
    out_ref[:, HEADS * HEAD_DIM :] = stats.astype(BF16)


def own_kernel(n_lat, count, *refs):
    tiles, (qi_ref, qe_ref, coarse_ref, out_ref, lse_ref) = refs[:6], refs[6:]
    rows = 2 * SPAN
    far = far_exists(n_lat)
    lane = lax.broadcasted_iota(jnp.int32, (rows, 6 * SPAN), 1)
    keep = jnp.logical_or(lane < 4 * SPAN, far)
    entry = lax.broadcasted_iota(jnp.int32, (rows, 2 * count), 1)
    bias = jnp.where(entry < count, math.log(SPAN), math.log(4 * SPAN)).astype(F32)
    column = lax.broadcasted_iota(jnp.int32, (rows, HEAD_DIM), 1)
    stats = jnp.zeros((rows, HEAD_DIM), F32)
    for group in range(0, HEADS, 4):
        near, coarse = [], []
        for cols in heads()[group : group + 4]:
            q = jnp.concatenate([qe_ref[:, cols], qi_ref[:, cols]], axis=0)
            near.append(jnp.where(keep, logits(q, stacked(tiles, 0, cols)), NEG))
            coarse.append(logits(q, coarse_ref[0, :, cols])[:, : 2 * count] + bias)
        tops = [
            jnp.maximum(jnp.max(n, axis=-1, keepdims=True), jnp.max(c, axis=-1, keepdims=True))
            for n, c in zip(near, coarse)
        ]
        near = [jnp.exp(n - top) for n, top in zip(near, tops)]
        coarse = [jnp.exp(c - top) for c, top in zip(coarse, tops)]
        totals = [
            jnp.sum(n, axis=-1, keepdims=True) + jnp.sum(c, axis=-1, keepdims=True)
            for n, c in zip(near, coarse)
        ]
        for i, cols in enumerate(heads()[group : group + 4]):
            part = jnp.dot(
                near[i].astype(BF16), stacked(tiles, 1, cols), preferred_element_type=F32
            )
            part += jnp.dot(
                coarse[i].astype(BF16), coarse_ref[1, : 2 * count, cols], preferred_element_type=F32
            )
            out_ref[:, cols] = part * (1.0 / totals[i])
            stats = jnp.where(column == group + i, tops[i] + jnp.log(totals[i]), stats)
    lse_ref[...] = stats


def merge_kernel(own_ref, lse_ref, edge_ref, inner_ref, weight_ref, out_ref):
    width = HEADS * HEAD_DIM
    odd = odd_column()
    merged = []
    for index, back_ref in enumerate((edge_ref, inner_ref)):
        rows = slice(index * SPAN, (index + 1) * SPAN)
        stats = back_ref[:, width:].astype(F32)
        pieces = []
        for h in range(HEADS):
            cols = slice(h * HEAD_DIM, (h + 1) * HEAD_DIM)
            here = lse_ref[rows, h : h + 1]
            there = stats[:, h : h + 1] + stats[:, HEADS + h : HEADS + h + 1]
            there = there + stats[:, 2 * HEADS + h : 2 * HEADS + h + 1]
            share = 1.0 / (1.0 + jnp.exp(jnp.minimum(there - here, 80.0)))
            own = own_ref[rows, cols]
            pieces.append(own * share + back_ref[:, cols].astype(F32) * (1.0 - share))
        merged.append(jnp.concatenate(pieces, axis=1).reshape(TILE, TILE, width))
    edge, inner = merged
    left = jnp.where(odd, inner, edge)
    right = jnp.where(odd, edge, inner)
    attended = jnp.stack([left, right], axis=1).reshape(2 * SPAN, width).astype(BF16)
    mixed = jnp.dot(attended, weight_ref[...], preferred_element_type=F32)
    out_ref[...] = mixed.reshape(TILE, 2 * TILE, width).astype(BF16)


def swap(x, axis, distance):
    count = lax.axis_size(axis)
    return lax.ppermute(x, axis, [(i, i ^ distance) for i in range(count)])


def outward(x, axis):
    count = lax.axis_size(axis)
    return lax.ppermute(x, axis, [(i, (i + (1 if i % 2 else -1)) % count) for i in range(count)])


def stride(x, axis, step):
    count = lax.axis_size(axis)
    route = [(i, (i + (-step if i % 2 else step)) % count) for i in range(count)]
    return lax.ppermute(x, axis, route)


def after_kernel(*refs):
    pass


def after(x, *tokens, weight=0):
    return pl.pallas_call(
        after_kernel,
        out_shape=jax.ShapeDtypeStruct(x.shape, x.dtype),
        in_specs=[pl.BlockSpec(memory_space=pl.ANY)] * (1 + len(tokens)),
        out_specs=pl.BlockSpec(memory_space=pl.ANY),
        input_output_aliases={0: 0},
        name="after",
        compiler_params=pltpu.CompilerParams(vmem_limit_bytes=1024 * 1024),
        cost_estimate=pl.CostEstimate(flops=weight, bytes_accessed=0, transcendentals=0),
    )(x, *tokens)


def mean_entries(*entries):
    total = sum(e.astype(F32) for e in entries)
    return (total * (1.0 / len(entries))).astype(BF16)


def shards(queries, keys_values, out_weight):
    n_lat = lax.axis_size("lat")
    width = queries.shape[-1]
    def like(*shape):
        return jax.ShapeDtypeStruct(shape, BF16)

    pack = 2 * SPAN + 4
    q_edge, q_inner, edge_own, inner_own, pooled = pl.pallas_call(
        split_kernel,
        out_shape=[
            like(SPAN, width),
            like(SPAN, width),
            like(pack, width),
            like(2 * SPAN, width),
            like(4, width),
        ],
        in_specs=[pl.BlockSpec(memory_space=pltpu.HBM)] * 2,
        out_specs=[VMEM] * 5,
        scratch_shapes=[
            pltpu.VMEM(queries.shape, BF16),
            pltpu.VMEM(keys_values.shape, BF16),
            pltpu.SemaphoreType.DMA((3,)),
        ],
        name="split",
        compiler_params=pltpu.CompilerParams(vmem_limit_bytes=LIMIT),
        cost_estimate=pl.CostEstimate(flops=0, bytes_accessed=2 << 20, transcendentals=0),
    )(*(pltpu.with_memory_space_constraint(x, pltpu.HBM) for x in (queries, keys_values)))
    edge_pair = swap(edge_own, "lat", 1)
    far_q_edge = outward(q_edge, "lon")
    far_q_inner = swap(q_inner, "lon", 1)
    inner_pair = swap(inner_own, "lat", 1)
    inner_hop = stride(inner_own, "lat", -2)
    pooled = after(pooled, weight=4 * WEIGHT)
    edge_pair = after(edge_pair, pooled, far_q_edge, inner_hop)
    edge_far = stride(edge_pair, "lat", 2)
    inner_far = swap(inner_hop, "lat", 1)
    level0 = pooled.reshape(2, 2, width)
    level0_lat = edge_pair[2 * SPAN :].reshape(2, 2, width)
    mine = mean_entries(level0[:, 0:1], level0[:, 1:2], level0_lat[:, 0:1], level0_lat[:, 1:2])
    beside = swap(jnp.concatenate([level0, level0_lat, mine], axis=1), "lon", 1)
    group = jnp.concatenate([mine, beside[:, 4:5]], axis=1)
    group_lon = swap(group, "lon", 2)
    group_both = jnp.concatenate([group, group_lon], axis=1)
    group_lat = swap(after(group_both, inner_pair, far_q_inner), "lat", 2)
    coarse = jnp.concatenate([level0_lat, beside[:, 0:4], group_lon, group_lat], axis=1)
    count = coarse.shape[1] // 2
    coarse = jnp.pad(coarse, ((0, 0), (0, 16 - 2 * count), (0, 0)))

    back = jax.ShapeDtypeStruct((SPAN, width + HEAD_DIM), BF16)
    flops = 4 * SPAN * 3 * SPAN * width
    edge_part = call(
        functools.partial(partial_kernel, n_lat),
        [back],
        "edge_part",
        flops,
        far_q_edge,
        edge_own,
        edge_pair,
        edge_far,
    )[0]
    edge_back = outward(edge_part, "lon")
    inner_far = after(inner_far, edge_part)
    inner_part = call(
        functools.partial(partial_kernel, n_lat),
        [back],
        "inner_part",
        flops,
        far_q_inner,
        inner_own,
        inner_pair,
        inner_far,
    )[0]
    inner_back = swap(inner_part, "lon", 1)
    coarse = after(coarse, inner_part)
    own, lse = call(
        functools.partial(own_kernel, n_lat, count),
        [
            jax.ShapeDtypeStruct((2 * SPAN, width), F32),
            jax.ShapeDtypeStruct((2 * SPAN, HEAD_DIM), F32),
        ],
        "own_part",
        4 * flops,
        edge_own,
        inner_own,
        edge_pair,
        inner_pair,
        edge_far,
        inner_far,
        q_inner,
        q_edge,
        coarse,
    )
    edge_back = after(edge_back, own, weight=WEIGHT)
    return call(
        merge_kernel,
        [jax.ShapeDtypeStruct(queries.shape, BF16)],
        "merge",
        4 * SPAN * width * width,
        own,
        lse,
        edge_back,
        inner_back,
        out_weight,
    )[0]


def solution(mesh):
    return jax.shard_map(
        shards,
        mesh=mesh,
        in_specs=(P("lat", "lon", None), P(None, "lat", "lon", None), P()),
        out_specs=P("lat", "lon", None),
        check_vma=False,
    )
```

```python
import functools
import math

import jax
import jax.numpy as jnp
from jax import lax
from jax.experimental import pallas as pl
from jax.experimental.pallas import tpu as pltpu
from jax.sharding import PartitionSpec as P

HEADS = 8
HEAD_DIM = 128
TILE = 8
SPAN = TILE * TILE
SCALE = 1.0 / math.sqrt(HEAD_DIM)
NEG = -1e30
WEIGHT = 2 * 10**8
LIMIT = 16 * 1024 * 1024
F32 = jnp.float32
BF16 = jnp.bfloat16
VMEM = pl.BlockSpec(memory_space=pltpu.VMEM)


def call(kernel, outs, name, flops, *args):
    moved = sum(a.size * a.dtype.itemsize for a in args)
    moved += sum(math.prod(o.shape) * o.dtype.itemsize for o in outs)
    return pl.pallas_call(
        kernel,
        out_shape=outs,
        in_specs=[VMEM] * len(args),
        out_specs=[VMEM] * len(outs),
        name=name,
        compiler_params=pltpu.CompilerParams(vmem_limit_bytes=LIMIT),
        cost_estimate=pl.CostEstimate(flops=flops, bytes_accessed=moved, transcendentals=0),
    )(*args)


def odd_column():
    return lax.rem(lax.axis_index("lon"), 2) == 1


def far_exists(n_lat):
    row = lax.axis_index("lat")
    return jnp.where(lax.rem(row, 2) == 1, row < n_lat - 1, row > 0)


def split_tiles(x, odd):
    cut = x.reshape(TILE, 2, TILE, x.shape[-1])
    left = cut[:, 0].reshape(SPAN, x.shape[-1])
    right = cut[:, 1].reshape(SPAN, x.shape[-1])
    return jnp.where(odd, right, left), jnp.where(odd, left, right)


def split_kernel(q_hbm, kv_hbm, qe_ref, qi_ref, edge_ref, inner_ref, pool_ref, q_ref, kv_ref, sems):
    copies = [pltpu.make_async_copy(kv_hbm.at[i], kv_ref.at[i], sems.at[i]) for i in range(2)]
    copies.append(pltpu.make_async_copy(q_hbm, q_ref, sems.at[2]))
    for copy in copies:
        copy.start()
    odd = odd_column()
    pooled = []
    for half in range(2):
        copies[half].wait()
        edge, inner = split_tiles(kv_ref[half].astype(F32), odd)
        rows = slice(half * SPAN, (half + 1) * SPAN)
        edge_ref[rows] = edge.astype(BF16)
        inner_ref[rows] = inner.astype(BF16)
        for tile in (edge, inner):
            pooled.append(jnp.sum(tile, axis=0, keepdims=True) * (1.0 / SPAN))
    pooled = jnp.concatenate(pooled, axis=0).astype(BF16)
    pool_ref[...] = pooled
    edge_ref[2 * SPAN :] = pooled
    copies[2].wait()
    edge, inner = split_tiles(q_ref[...].astype(F32), odd)
    qe_ref[...] = edge.astype(BF16)
    qi_ref[...] = inner.astype(BF16)


def logits(q, k):
    return lax.dot_general(q, k, (((1,), (1,)), ((), ())), preferred_element_type=F32) * SCALE


def heads():
    return [slice(h * HEAD_DIM, (h + 1) * HEAD_DIM) for h in range(HEADS)]


def stacked(refs, half, cols):
    return jnp.concatenate([r[half * SPAN : (half + 1) * SPAN, cols] for r in refs], axis=0)


def partial_kernel(n_lat, q_ref, own_ref, pair_ref, far_ref, out_ref):
    tiles = (own_ref, pair_ref, far_ref)
    far = far_exists(n_lat)
    lane = lax.broadcasted_iota(jnp.int32, (SPAN, 3 * SPAN), 1)
    keep = jnp.logical_or(lane < 2 * SPAN, far)
    column = lax.broadcasted_iota(jnp.int32, (SPAN, HEAD_DIM), 1)
    scores = [
        jnp.where(keep, logits(q_ref[:, cols], stacked(tiles, 0, cols)), NEG) for cols in heads()
    ]
    tops = [jnp.max(s, axis=-1, keepdims=True) for s in scores]
    expos = [jnp.exp(s - top) for s, top in zip(scores, tops)]
    totals = [jnp.sum(e, axis=-1, keepdims=True) for e in expos]
    parts = [
        jnp.dot(e.astype(BF16), stacked(tiles, 1, cols), preferred_element_type=F32)
        for e, cols in zip(expos, heads())
    ]
    stats = jnp.zeros((SPAN, HEAD_DIM), F32)
    for h in range(HEADS):
        lse = tops[h] + jnp.log(totals[h])
        high = lse.astype(BF16).astype(F32)
        mid = (lse - high).astype(BF16).astype(F32)
        low = lse - high - mid
        stats = jnp.where(column == h, high, stats)
        stats = jnp.where(column == HEADS + h, mid, stats)
        stats = jnp.where(column == 2 * HEADS + h, low, stats)
    for h, cols in enumerate(heads()):
        out_ref[:, cols] = (parts[h] * (1.0 / totals[h])).astype(BF16)
    out_ref[:, HEADS * HEAD_DIM :] = stats.astype(BF16)


def own_kernel(n_lat, count, *refs):
    tiles, (qi_ref, qe_ref, coarse_ref, out_ref, lse_ref) = refs[:6], refs[6:]
    rows = 2 * SPAN
    far = far_exists(n_lat)
    lane = lax.broadcasted_iota(jnp.int32, (rows, 6 * SPAN), 1)
    keep = jnp.logical_or(lane < 4 * SPAN, far)
    entry = lax.broadcasted_iota(jnp.int32, (rows, 2 * count), 1)
    bias = jnp.where(entry < count, math.log(SPAN), math.log(4 * SPAN)).astype(F32)
    column = lax.broadcasted_iota(jnp.int32, (rows, HEAD_DIM), 1)
    stats = jnp.zeros((rows, HEAD_DIM), F32)
    for group in range(0, HEADS, 4):
        near, coarse = [], []
        for cols in heads()[group : group + 4]:
            q = jnp.concatenate([qe_ref[:, cols], qi_ref[:, cols]], axis=0)
            near.append(jnp.where(keep, logits(q, stacked(tiles, 0, cols)), NEG))
            coarse.append(logits(q, coarse_ref[0, :, cols])[:, : 2 * count] + bias)
        tops = [
            jnp.maximum(jnp.max(n, axis=-1, keepdims=True), jnp.max(c, axis=-1, keepdims=True))
            for n, c in zip(near, coarse)
        ]
        near = [jnp.exp(n - top) for n, top in zip(near, tops)]
        coarse = [jnp.exp(c - top) for c, top in zip(coarse, tops)]
        totals = [
            jnp.sum(n, axis=-1, keepdims=True) + jnp.sum(c, axis=-1, keepdims=True)
            for n, c in zip(near, coarse)
        ]
        for i, cols in enumerate(heads()[group : group + 4]):
            part = jnp.dot(
                near[i].astype(BF16), stacked(tiles, 1, cols), preferred_element_type=F32
            )
            part += jnp.dot(
                coarse[i].astype(BF16), coarse_ref[1, : 2 * count, cols], preferred_element_type=F32
            )
            out_ref[:, cols] = part * (1.0 / totals[i])
            stats = jnp.where(column == group + i, tops[i] + jnp.log(totals[i]), stats)
    lse_ref[...] = stats


def merge_kernel(own_ref, lse_ref, edge_ref, inner_ref, weight_ref, out_ref):
    width = HEADS * HEAD_DIM
    odd = odd_column()
    merged = []
    for index, back_ref in enumerate((edge_ref, inner_ref)):
        rows = slice(index * SPAN, (index + 1) * SPAN)
        stats = back_ref[:, width:].astype(F32)
        pieces = []
        for h in range(HEADS):
            cols = slice(h * HEAD_DIM, (h + 1) * HEAD_DIM)
            here = lse_ref[rows, h : h + 1]
            there = stats[:, h : h + 1] + stats[:, HEADS + h : HEADS + h + 1]
            there = there + stats[:, 2 * HEADS + h : 2 * HEADS + h + 1]
            share = 1.0 / (1.0 + jnp.exp(jnp.minimum(there - here, 80.0)))
            own = own_ref[rows, cols]
            pieces.append(own * share + back_ref[:, cols].astype(F32) * (1.0 - share))
        merged.append(jnp.concatenate(pieces, axis=1).reshape(TILE, TILE, width))
    edge, inner = merged
    left = jnp.where(odd, inner, edge)
    right = jnp.where(odd, edge, inner)
    attended = jnp.stack([left, right], axis=1).reshape(2 * SPAN, width).astype(BF16)
    mixed = jnp.dot(attended, weight_ref[...], preferred_element_type=F32)
    out_ref[...] = mixed.reshape(TILE, 2 * TILE, width).astype(BF16)


def swap(x, axis, distance):
    count = lax.axis_size(axis)
    return lax.ppermute(x, axis, [(i, i ^ distance) for i in range(count)])


def outward(x, axis):
    count = lax.axis_size(axis)
    return lax.ppermute(x, axis, [(i, (i + (1 if i % 2 else -1)) % count) for i in range(count)])


def stride(x, axis, step):
    count = lax.axis_size(axis)
    route = [(i, (i + (-step if i % 2 else step)) % count) for i in range(count)]
    return lax.ppermute(x, axis, route)


def after_kernel(*refs):
    pass


def after(x, *tokens, weight=0):
    return pl.pallas_call(
        after_kernel,
        out_shape=jax.ShapeDtypeStruct(x.shape, x.dtype),
        in_specs=[pl.BlockSpec(memory_space=pl.ANY)] * (1 + len(tokens)),
        out_specs=pl.BlockSpec(memory_space=pl.ANY),
        input_output_aliases={0: 0},
        name="after",
        compiler_params=pltpu.CompilerParams(vmem_limit_bytes=1024 * 1024),
        cost_estimate=pl.CostEstimate(flops=weight, bytes_accessed=0, transcendentals=0),
    )(x, *tokens)


def mean_entries(*entries):
    total = sum(e.astype(F32) for e in entries)
    return (total * (1.0 / len(entries))).astype(BF16)


def shards(queries, keys_values, out_weight):
    n_lat = lax.axis_size("lat")
    width = queries.shape[-1]
    def like(*shape):
        return jax.ShapeDtypeStruct(shape, BF16)

    pack = 2 * SPAN + 4
    q_edge, q_inner, edge_own, inner_own, pooled = pl.pallas_call(
        split_kernel,
        out_shape=[
            like(SPAN, width),
            like(SPAN, width),
            like(pack, width),
            like(2 * SPAN, width),
            like(4, width),
        ],
        in_specs=[pl.BlockSpec(memory_space=pltpu.HBM)] * 2,
        out_specs=[VMEM] * 5,
        scratch_shapes=[
            pltpu.VMEM(queries.shape, BF16),
            pltpu.VMEM(keys_values.shape, BF16),
            pltpu.SemaphoreType.DMA((3,)),
        ],
        name="split",
        compiler_params=pltpu.CompilerParams(vmem_limit_bytes=LIMIT),
        cost_estimate=pl.CostEstimate(flops=0, bytes_accessed=2 << 20, transcendentals=0),
    )(*(pltpu.with_memory_space_constraint(x, pltpu.HBM) for x in (queries, keys_values)))
    edge_pair = swap(edge_own, "lat", 1)
    far_q_edge = outward(q_edge, "lon")
    far_q_inner = swap(q_inner, "lon", 1)
    inner_pair = swap(inner_own, "lat", 1)
    inner_hop = stride(inner_own, "lat", -2)
    pooled = after(pooled, weight=4 * WEIGHT)
    edge_pair = after(edge_pair, pooled, inner_hop)
    edge_far = stride(edge_pair, "lat", 2)
    inner_far = swap(inner_hop, "lat", 1)
    level0 = pooled.reshape(2, 2, width)
    level0_lat = edge_pair[2 * SPAN :].reshape(2, 2, width)
    mine = mean_entries(level0[:, 0:1], level0[:, 1:2], level0_lat[:, 0:1], level0_lat[:, 1:2])
    beside = swap(jnp.concatenate([level0, level0_lat, mine], axis=1), "lon", 1)
    group = jnp.concatenate([mine, beside[:, 4:5]], axis=1)
    group_lon = swap(group, "lon", 2)
    group_both = jnp.concatenate([group, group_lon], axis=1)
    group_lat = swap(after(group_both, inner_pair, far_q_edge, far_q_inner), "lat", 2)
    coarse = jnp.concatenate([level0_lat, beside[:, 0:4], group_lon, group_lat], axis=1)
    count = coarse.shape[1] // 2
    coarse = jnp.pad(coarse, ((0, 0), (0, 16 - 2 * count), (0, 0)))

    back = jax.ShapeDtypeStruct((SPAN, width + HEAD_DIM), BF16)
    flops = 4 * SPAN * 3 * SPAN * width
    edge_part = call(
        functools.partial(partial_kernel, n_lat),
        [back],
        "edge_part",
        flops,
        far_q_edge,
        edge_own,
        edge_pair,
        edge_far,
    )[0]
    edge_back = outward(edge_part, "lon")
    inner_far = after(inner_far, edge_part)
    inner_part = call(
        functools.partial(partial_kernel, n_lat),
        [back],
        "inner_part",
        flops,
        far_q_inner,
        inner_own,
        inner_pair,
        inner_far,
    )[0]
    inner_back = swap(inner_part, "lon", 1)
    coarse = after(coarse, inner_part)
    own, lse = call(
        functools.partial(own_kernel, n_lat, count),
        [
            jax.ShapeDtypeStruct((2 * SPAN, width), F32),
            jax.ShapeDtypeStruct((2 * SPAN, HEAD_DIM), F32),
        ],
        "own_part",
        4 * flops,
        edge_own,
        inner_own,
        edge_pair,
        inner_pair,
        edge_far,
        inner_far,
        q_inner,
        q_edge,
        coarse,
    )
    edge_back = after(edge_back, own, weight=WEIGHT)
    return call(
        merge_kernel,
        [jax.ShapeDtypeStruct(queries.shape, BF16)],
        "merge",
        4 * SPAN * width * width,
        own,
        lse,
        edge_back,
        inner_back,
        out_weight,
    )[0]


def solution(mesh):
    return jax.shard_map(
        shards,
        mesh=mesh,
        in_specs=(P("lat", "lon", None), P(None, "lat", "lon", None), P()),
        out_specs=P("lat", "lon", None),
        check_vma=False,
    )
```

```python
import functools
import math

import jax
import jax.numpy as jnp
from jax import lax
from jax.experimental import pallas as pl
from jax.experimental.pallas import tpu as pltpu
from jax.sharding import PartitionSpec as P

HEADS = 8
HEAD_DIM = 128
TILE = 8
SPAN = TILE * TILE
SCALE = 1.0 / math.sqrt(HEAD_DIM)
NEG = -1e30
WEIGHT = 2 * 10**8
LIMIT = 16 * 1024 * 1024
F32 = jnp.float32
BF16 = jnp.bfloat16
VMEM = pl.BlockSpec(memory_space=pltpu.VMEM)


def call(kernel, outs, name, flops, *args):
    moved = sum(a.size * a.dtype.itemsize for a in args)
    moved += sum(math.prod(o.shape) * o.dtype.itemsize for o in outs)
    return pl.pallas_call(
        kernel,
        out_shape=outs,
        in_specs=[VMEM] * len(args),
        out_specs=[VMEM] * len(outs),
        name=name,
        compiler_params=pltpu.CompilerParams(vmem_limit_bytes=LIMIT),
        cost_estimate=pl.CostEstimate(flops=flops, bytes_accessed=moved, transcendentals=0),
    )(*args)


def odd_column():
    return lax.rem(lax.axis_index("lon"), 2) == 1


def far_exists(n_lat):
    row = lax.axis_index("lat")
    return jnp.where(lax.rem(row, 2) == 1, row < n_lat - 1, row > 0)


def split_tiles(x, odd):
    cut = x.reshape(TILE, 2, TILE, x.shape[-1])
    left = cut[:, 0].reshape(SPAN, x.shape[-1])
    right = cut[:, 1].reshape(SPAN, x.shape[-1])
    return jnp.where(odd, right, left), jnp.where(odd, left, right)


def split_kernel(q_hbm, kv_hbm, qe_ref, qi_ref, edge_ref, inner_ref, pool_ref, q_ref, kv_ref, sems):
    copies = [pltpu.make_async_copy(kv_hbm.at[i], kv_ref.at[i], sems.at[i]) for i in range(2)]
    copies.append(pltpu.make_async_copy(q_hbm, q_ref, sems.at[2]))
    for copy in copies:
        copy.start()
    odd = odd_column()
    pooled = []
    for half in range(2):
        copies[half].wait()
        edge, inner = split_tiles(kv_ref[half].astype(F32), odd)
        rows = slice(half * SPAN, (half + 1) * SPAN)
        edge_ref[rows] = edge.astype(BF16)
        inner_ref[rows] = inner.astype(BF16)
        for tile in (edge, inner):
            pooled.append(jnp.sum(tile, axis=0, keepdims=True) * (1.0 / SPAN))
    pooled = jnp.concatenate(pooled, axis=0).astype(BF16)
    pool_ref[...] = pooled
    edge_ref[2 * SPAN :] = pooled
    copies[2].wait()
    edge, inner = split_tiles(q_ref[...].astype(F32), odd)
    qe_ref[...] = edge.astype(BF16)
    qi_ref[...] = inner.astype(BF16)


def logits(q, k):
    return lax.dot_general(q, k, (((1,), (1,)), ((), ())), preferred_element_type=F32) * SCALE


def heads():
    return [slice(h * HEAD_DIM, (h + 1) * HEAD_DIM) for h in range(HEADS)]


def stacked(refs, half, cols):
    return jnp.concatenate([r[half * SPAN : (half + 1) * SPAN, cols] for r in refs], axis=0)


def partial_kernel(n_lat, q_ref, own_ref, pair_ref, far_ref, out_ref):
    tiles = (own_ref, pair_ref, far_ref)
    far = far_exists(n_lat)
    lane = lax.broadcasted_iota(jnp.int32, (SPAN, 3 * SPAN), 1)
    keep = jnp.logical_or(lane < 2 * SPAN, far)
    column = lax.broadcasted_iota(jnp.int32, (SPAN, HEAD_DIM), 1)
    scores = [
        jnp.where(keep, logits(q_ref[:, cols], stacked(tiles, 0, cols)), NEG) for cols in heads()
    ]
    tops = [jnp.max(s, axis=-1, keepdims=True) for s in scores]
    expos = [jnp.exp(s - top) for s, top in zip(scores, tops)]
    totals = [jnp.sum(e, axis=-1, keepdims=True) for e in expos]
    parts = [
        jnp.dot(e.astype(BF16), stacked(tiles, 1, cols), preferred_element_type=F32)
        for e, cols in zip(expos, heads())
    ]
    stats = jnp.zeros((SPAN, HEAD_DIM), F32)
    for h in range(HEADS):
        lse = tops[h] + jnp.log(totals[h])
        high = lse.astype(BF16).astype(F32)
        mid = (lse - high).astype(BF16).astype(F32)
        low = lse - high - mid
        stats = jnp.where(column == h, high, stats)
        stats = jnp.where(column == HEADS + h, mid, stats)
        stats = jnp.where(column == 2 * HEADS + h, low, stats)
    for h, cols in enumerate(heads()):
        out_ref[:, cols] = (parts[h] * (1.0 / totals[h])).astype(BF16)
    out_ref[:, HEADS * HEAD_DIM :] = stats.astype(BF16)


def own_kernel(n_lat, count, *refs):
    tiles, (qi_ref, qe_ref, coarse_ref, out_ref, lse_ref) = refs[:6], refs[6:]
    rows = 2 * SPAN
    far = far_exists(n_lat)
    lane = lax.broadcasted_iota(jnp.int32, (rows, 6 * SPAN), 1)
    keep = jnp.logical_or(lane < 4 * SPAN, far)
    entry = lax.broadcasted_iota(jnp.int32, (rows, 2 * count), 1)
    bias = jnp.where(entry < count, math.log(SPAN), math.log(4 * SPAN)).astype(F32)
    column = lax.broadcasted_iota(jnp.int32, (rows, HEAD_DIM), 1)
    stats = jnp.zeros((rows, HEAD_DIM), F32)
    for group in range(0, HEADS, 4):
        near, coarse = [], []
        for cols in heads()[group : group + 4]:
            q = jnp.concatenate([qe_ref[:, cols], qi_ref[:, cols]], axis=0)
            near.append(jnp.where(keep, logits(q, stacked(tiles, 0, cols)), NEG))
            coarse.append(logits(q, coarse_ref[0, :, cols])[:, : 2 * count] + bias)
        tops = [
            jnp.maximum(jnp.max(n, axis=-1, keepdims=True), jnp.max(c, axis=-1, keepdims=True))
            for n, c in zip(near, coarse)
        ]
        near = [jnp.exp(n - top) for n, top in zip(near, tops)]
        coarse = [jnp.exp(c - top) for c, top in zip(coarse, tops)]
        totals = [
            jnp.sum(n, axis=-1, keepdims=True) + jnp.sum(c, axis=-1, keepdims=True)
            for n, c in zip(near, coarse)
        ]
        for i, cols in enumerate(heads()[group : group + 4]):
            part = jnp.dot(
                near[i].astype(BF16), stacked(tiles, 1, cols), preferred_element_type=F32
            )
            part += jnp.dot(
                coarse[i].astype(BF16), coarse_ref[1, : 2 * count, cols], preferred_element_type=F32
            )
            out_ref[:, cols] = part * (1.0 / totals[i])
            stats = jnp.where(column == group + i, tops[i] + jnp.log(totals[i]), stats)
    lse_ref[...] = stats


def merge_kernel(own_ref, lse_ref, edge_ref, inner_ref, weight_ref, out_ref, held_ref, sems):
    width = HEADS * HEAD_DIM
    odd = odd_column()
    merged = []
    for index, back_ref in enumerate((edge_ref, inner_ref)):
        rows = slice(index * SPAN, (index + 1) * SPAN)
        stats = back_ref[:, width:].astype(F32)
        pieces = []
        for h in range(HEADS):
            cols = slice(h * HEAD_DIM, (h + 1) * HEAD_DIM)
            here = lse_ref[rows, h : h + 1]
            there = stats[:, h : h + 1] + stats[:, HEADS + h : HEADS + h + 1]
            there = there + stats[:, 2 * HEADS + h : 2 * HEADS + h + 1]
            share = 1.0 / (1.0 + jnp.exp(jnp.minimum(there - here, 80.0)))
            own = own_ref[rows, cols]
            pieces.append(own * share + back_ref[:, cols].astype(F32) * (1.0 - share))
        merged.append(jnp.concatenate(pieces, axis=1).reshape(TILE, TILE, width))
    edge, inner = merged
    left = jnp.where(odd, inner, edge)
    right = jnp.where(odd, edge, inner)
    attended = jnp.stack([left, right], axis=1).reshape(2 * SPAN, width).astype(BF16)
    copies = []
    for part in range(4):
        cols = slice(part * width // 4, (part + 1) * width // 4)
        mixed = jnp.dot(attended, weight_ref[:, cols], preferred_element_type=F32)
        held_ref[:, :, cols] = mixed.reshape(TILE, 2 * TILE, width // 4).astype(BF16)
        copies.append(
            pltpu.make_async_copy(held_ref.at[:, :, cols], out_ref.at[:, :, cols], sems.at[part])
        )
        copies[-1].start()
    for copy in copies:
        copy.wait()


def swap(x, axis, distance):
    count = lax.axis_size(axis)
    return lax.ppermute(x, axis, [(i, i ^ distance) for i in range(count)])


def outward(x, axis):
    count = lax.axis_size(axis)
    return lax.ppermute(x, axis, [(i, (i + (1 if i % 2 else -1)) % count) for i in range(count)])


def stride(x, axis, step):
    count = lax.axis_size(axis)
    route = [(i, (i + (-step if i % 2 else step)) % count) for i in range(count)]
    return lax.ppermute(x, axis, route)


def after_kernel(*refs):
    pass


def after(x, *tokens, weight=0):
    return pl.pallas_call(
        after_kernel,
        out_shape=jax.ShapeDtypeStruct(x.shape, x.dtype),
        in_specs=[pl.BlockSpec(memory_space=pl.ANY)] * (1 + len(tokens)),
        out_specs=pl.BlockSpec(memory_space=pl.ANY),
        input_output_aliases={0: 0},
        name="after",
        compiler_params=pltpu.CompilerParams(vmem_limit_bytes=1024 * 1024),
        cost_estimate=pl.CostEstimate(flops=weight, bytes_accessed=0, transcendentals=0),
    )(x, *tokens)


def mean_entries(*entries):
    total = sum(e.astype(F32) for e in entries)
    return (total * (1.0 / len(entries))).astype(BF16)


def shards(queries, keys_values, out_weight):
    n_lat = lax.axis_size("lat")
    width = queries.shape[-1]
    def like(*shape):
        return jax.ShapeDtypeStruct(shape, BF16)

    pack = 2 * SPAN + 4
    q_edge, q_inner, edge_own, inner_own, pooled = pl.pallas_call(
        split_kernel,
        out_shape=[
            like(SPAN, width),
            like(SPAN, width),
            like(pack, width),
            like(2 * SPAN, width),
            like(4, width),
        ],
        in_specs=[pl.BlockSpec(memory_space=pltpu.HBM)] * 2,
        out_specs=[VMEM] * 5,
        scratch_shapes=[
            pltpu.VMEM(queries.shape, BF16),
            pltpu.VMEM(keys_values.shape, BF16),
            pltpu.SemaphoreType.DMA((3,)),
        ],
        name="split",
        compiler_params=pltpu.CompilerParams(vmem_limit_bytes=LIMIT),
        cost_estimate=pl.CostEstimate(flops=0, bytes_accessed=2 << 20, transcendentals=0),
    )(*(pltpu.with_memory_space_constraint(x, pltpu.HBM) for x in (queries, keys_values)))
    edge_pair = swap(edge_own, "lat", 1)
    far_q_edge = outward(q_edge, "lon")
    far_q_inner = swap(q_inner, "lon", 1)
    inner_pair = swap(inner_own, "lat", 1)
    inner_hop = stride(inner_own, "lat", -2)
    pooled = after(pooled, weight=4 * WEIGHT)
    edge_pair = after(edge_pair, pooled, far_q_edge, inner_hop)
    edge_far = stride(edge_pair, "lat", 2)
    inner_far = swap(inner_hop, "lat", 1)
    level0 = pooled.reshape(2, 2, width)
    level0_lat = edge_pair[2 * SPAN :].reshape(2, 2, width)
    mine = mean_entries(level0[:, 0:1], level0[:, 1:2], level0_lat[:, 0:1], level0_lat[:, 1:2])
    beside = swap(jnp.concatenate([level0, level0_lat, mine], axis=1), "lon", 1)
    group = jnp.concatenate([mine, beside[:, 4:5]], axis=1)
    group_lon = swap(group, "lon", 2)
    group_both = jnp.concatenate([group, group_lon], axis=1)
    group_lat = swap(after(group_both, inner_pair, far_q_inner), "lat", 2)
    coarse = jnp.concatenate([level0_lat, beside[:, 0:4], group_lon, group_lat], axis=1)
    count = coarse.shape[1] // 2
    coarse = jnp.pad(coarse, ((0, 0), (0, 16 - 2 * count), (0, 0)))

    back = jax.ShapeDtypeStruct((SPAN, width + HEAD_DIM), BF16)
    flops = 4 * SPAN * 3 * SPAN * width
    edge_part = call(
        functools.partial(partial_kernel, n_lat),
        [back],
        "edge_part",
        flops,
        far_q_edge,
        edge_own,
        edge_pair,
        edge_far,
    )[0]
    edge_back = outward(edge_part, "lon")
    inner_far = after(inner_far, edge_part)
    inner_part = call(
        functools.partial(partial_kernel, n_lat),
        [back],
        "inner_part",
        flops,
        far_q_inner,
        inner_own,
        inner_pair,
        inner_far,
    )[0]
    inner_back = swap(inner_part, "lon", 1)
    coarse = after(coarse, inner_part)
    own, lse = call(
        functools.partial(own_kernel, n_lat, count),
        [
            jax.ShapeDtypeStruct((2 * SPAN, width), F32),
            jax.ShapeDtypeStruct((2 * SPAN, HEAD_DIM), F32),
        ],
        "own_part",
        4 * flops,
        edge_own,
        inner_own,
        edge_pair,
        inner_pair,
        edge_far,
        inner_far,
        q_inner,
        q_edge,
        coarse,
    )
    edge_back = after(edge_back, own, weight=WEIGHT)
    return pl.pallas_call(
        merge_kernel,
        out_shape=jax.ShapeDtypeStruct(queries.shape, BF16),
        in_specs=[VMEM] * 5,
        out_specs=pl.BlockSpec(memory_space=pl.ANY),
        scratch_shapes=[pltpu.VMEM(queries.shape, BF16), pltpu.SemaphoreType.DMA((4,))],
        name="merge",
        compiler_params=pltpu.CompilerParams(vmem_limit_bytes=LIMIT),
        cost_estimate=pl.CostEstimate(
            flops=4 * SPAN * width * width, bytes_accessed=3 << 20, transcendentals=0
        ),
    )(own, lse, edge_back, inner_back, out_weight)


def solution(mesh):
    return jax.shard_map(
        shards,
        mesh=mesh,
        in_specs=(P("lat", "lon", None), P(None, "lat", "lon", None), P()),
        out_specs=P("lat", "lon", None),
        check_vma=False,
    )
```

```python
import functools
import math

import jax
import jax.numpy as jnp
from jax import lax
from jax.experimental import pallas as pl
from jax.experimental.pallas import tpu as pltpu
from jax.sharding import PartitionSpec as P

HEADS = 8
HEAD_DIM = 128
TILE = 8
SPAN = TILE * TILE
SCALE = 1.0 / math.sqrt(HEAD_DIM)
NEG = -1e30
WEIGHT = 2 * 10**8
LIMIT = 16 * 1024 * 1024
F32 = jnp.float32
BF16 = jnp.bfloat16
VMEM = pl.BlockSpec(memory_space=pltpu.VMEM)


def call(kernel, outs, name, flops, *args):
    moved = sum(a.size * a.dtype.itemsize for a in args)
    moved += sum(math.prod(o.shape) * o.dtype.itemsize for o in outs)
    return pl.pallas_call(
        kernel,
        out_shape=outs,
        in_specs=[VMEM] * len(args),
        out_specs=[VMEM] * len(outs),
        name=name,
        compiler_params=pltpu.CompilerParams(vmem_limit_bytes=LIMIT),
        cost_estimate=pl.CostEstimate(flops=flops, bytes_accessed=moved, transcendentals=0),
    )(*args)


def odd_column():
    return lax.rem(lax.axis_index("lon"), 2) == 1


def far_exists(n_lat):
    row = lax.axis_index("lat")
    return jnp.where(lax.rem(row, 2) == 1, row < n_lat - 1, row > 0)


def split_tiles(x, odd):
    cut = x.reshape(TILE, 2, TILE, x.shape[-1])
    left = cut[:, 0].reshape(SPAN, x.shape[-1])
    right = cut[:, 1].reshape(SPAN, x.shape[-1])
    return jnp.where(odd, right, left), jnp.where(odd, left, right)


def split_kernel(q_hbm, kv_hbm, qe_ref, qi_ref, edge_ref, inner_ref, pool_ref, q_ref, kv_ref, sems):
    copies = [pltpu.make_async_copy(kv_hbm.at[i], kv_ref.at[i], sems.at[i]) for i in range(2)]
    copies.append(pltpu.make_async_copy(q_hbm, q_ref, sems.at[2]))
    for copy in copies:
        copy.start()
    odd = odd_column()
    pooled = []
    for half in range(2):
        copies[half].wait()
        edge, inner = split_tiles(kv_ref[half].astype(F32), odd)
        rows = slice(half * SPAN, (half + 1) * SPAN)
        edge_ref[rows] = edge.astype(BF16)
        inner_ref[rows] = inner.astype(BF16)
        for tile in (edge, inner):
            pooled.append(jnp.sum(tile, axis=0, keepdims=True) * (1.0 / SPAN))
    pooled = jnp.concatenate(pooled, axis=0).astype(BF16)
    pool_ref[...] = pooled
    edge_ref[2 * SPAN :] = pooled
    copies[2].wait()
    edge, inner = split_tiles(q_ref[...].astype(F32), odd)
    qe_ref[...] = edge.astype(BF16)
    qi_ref[...] = inner.astype(BF16)


def logits(q, k):
    return lax.dot_general(q, k, (((1,), (1,)), ((), ())), preferred_element_type=F32) * SCALE


def heads():
    return [slice(h * HEAD_DIM, (h + 1) * HEAD_DIM) for h in range(HEADS)]


def stacked(refs, half, cols):
    return jnp.concatenate([r[half * SPAN : (half + 1) * SPAN, cols] for r in refs], axis=0)


def partial_kernel(n_lat, q_ref, own_ref, pair_ref, far_ref, out_ref):
    tiles = (own_ref, pair_ref, far_ref)
    far = far_exists(n_lat)
    lane = lax.broadcasted_iota(jnp.int32, (SPAN, 3 * SPAN), 1)
    keep = jnp.logical_or(lane < 2 * SPAN, far)
    column = lax.broadcasted_iota(jnp.int32, (SPAN, HEAD_DIM), 1)
    scores = [
        jnp.where(keep, logits(q_ref[:, cols], stacked(tiles, 0, cols)), NEG) for cols in heads()
    ]
    tops = [jnp.max(s, axis=-1, keepdims=True) for s in scores]
    expos = [jnp.exp(s - top) for s, top in zip(scores, tops)]
    totals = [jnp.sum(e, axis=-1, keepdims=True) for e in expos]
    parts = [
        jnp.dot(e.astype(BF16), stacked(tiles, 1, cols), preferred_element_type=F32)
        for e, cols in zip(expos, heads())
    ]
    stats = jnp.zeros((SPAN, HEAD_DIM), F32)
    for h in range(HEADS):
        lse = tops[h] + jnp.log(totals[h])
        high = lse.astype(BF16).astype(F32)
        mid = (lse - high).astype(BF16).astype(F32)
        low = lse - high - mid
        stats = jnp.where(column == h, high, stats)
        stats = jnp.where(column == HEADS + h, mid, stats)
        stats = jnp.where(column == 2 * HEADS + h, low, stats)
    for h, cols in enumerate(heads()):
        out_ref[:, cols] = (parts[h] * (1.0 / totals[h])).astype(BF16)
    out_ref[:, HEADS * HEAD_DIM :] = stats.astype(BF16)


def own_kernel(n_lat, count, *refs):
    tiles, (qi_ref, qe_ref, coarse_ref, out_ref, lse_ref) = refs[:6], refs[6:]
    rows = 2 * SPAN
    far = far_exists(n_lat)
    lane = lax.broadcasted_iota(jnp.int32, (rows, 6 * SPAN), 1)
    keep = jnp.logical_or(lane < 4 * SPAN, far)
    entry = lax.broadcasted_iota(jnp.int32, (rows, 2 * count), 1)
    bias = jnp.where(entry < count, math.log(SPAN), math.log(4 * SPAN)).astype(F32)
    column = lax.broadcasted_iota(jnp.int32, (rows, HEAD_DIM), 1)
    stats = jnp.zeros((rows, HEAD_DIM), F32)
    for group in range(0, HEADS, 4):
        near, coarse = [], []
        for cols in heads()[group : group + 4]:
            q = jnp.concatenate([qe_ref[:, cols], qi_ref[:, cols]], axis=0)
            near.append(jnp.where(keep, logits(q, stacked(tiles, 0, cols)), NEG))
            coarse.append(logits(q, coarse_ref[0, :, cols])[:, : 2 * count] + bias)
        tops = [
            jnp.maximum(jnp.max(n, axis=-1, keepdims=True), jnp.max(c, axis=-1, keepdims=True))
            for n, c in zip(near, coarse)
        ]
        near = [jnp.exp(n - top) for n, top in zip(near, tops)]
        coarse = [jnp.exp(c - top) for c, top in zip(coarse, tops)]
        totals = [
            jnp.sum(n, axis=-1, keepdims=True) + jnp.sum(c, axis=-1, keepdims=True)
            for n, c in zip(near, coarse)
        ]
        for i, cols in enumerate(heads()[group : group + 4]):
            part = jnp.dot(
                near[i].astype(BF16), stacked(tiles, 1, cols), preferred_element_type=F32
            )
            part += jnp.dot(
                coarse[i].astype(BF16), coarse_ref[1, : 2 * count, cols], preferred_element_type=F32
            )
            out_ref[:, cols] = part * (1.0 / totals[i])
            stats = jnp.where(column == group + i, tops[i] + jnp.log(totals[i]), stats)
    lse_ref[...] = stats


def merge_kernel(own_ref, lse_ref, edge_ref, inner_ref, weight_ref, out_ref):
    width = HEADS * HEAD_DIM
    odd = odd_column()
    merged = []
    for index, back_ref in enumerate((edge_ref, inner_ref)):
        rows = slice(index * SPAN, (index + 1) * SPAN)
        stats = back_ref[:, width:].astype(F32)
        pieces = []
        for h in range(HEADS):
            cols = slice(h * HEAD_DIM, (h + 1) * HEAD_DIM)
            here = lse_ref[rows, h : h + 1]
            there = stats[:, h : h + 1] + stats[:, HEADS + h : HEADS + h + 1]
            there = there + stats[:, 2 * HEADS + h : 2 * HEADS + h + 1]
            share = 1.0 / (1.0 + jnp.exp(jnp.minimum(there - here, 80.0)))
            own = own_ref[rows, cols]
            pieces.append(own * share + back_ref[:, cols].astype(F32) * (1.0 - share))
        merged.append(jnp.concatenate(pieces, axis=1).reshape(TILE, TILE, width))
    edge, inner = merged
    left = jnp.where(odd, inner, edge)
    right = jnp.where(odd, edge, inner)
    attended = jnp.stack([left, right], axis=1).reshape(2 * SPAN, width).astype(BF16)
    mixed = jnp.dot(attended, weight_ref[...], preferred_element_type=F32)
    out_ref[...] = mixed.reshape(TILE, 2 * TILE, width).astype(BF16)


def swap(x, axis, distance):
    count = lax.axis_size(axis)
    return lax.ppermute(x, axis, [(i, i ^ distance) for i in range(count)])


def outward(x, axis):
    count = lax.axis_size(axis)
    return lax.ppermute(x, axis, [(i, (i + (1 if i % 2 else -1)) % count) for i in range(count)])


def stride(x, axis, step):
    count = lax.axis_size(axis)
    route = [(i, (i + (-step if i % 2 else step)) % count) for i in range(count)]
    return lax.ppermute(x, axis, route)


def after_kernel(*refs):
    pass


def after(x, *tokens, weight=0):
    return pl.pallas_call(
        after_kernel,
        out_shape=jax.ShapeDtypeStruct(x.shape, x.dtype),
        in_specs=[pl.BlockSpec(memory_space=pl.ANY)] * (1 + len(tokens)),
        out_specs=pl.BlockSpec(memory_space=pl.ANY),
        input_output_aliases={0: 0},
        name="after",
        compiler_params=pltpu.CompilerParams(vmem_limit_bytes=1024 * 1024),
        cost_estimate=pl.CostEstimate(flops=weight, bytes_accessed=0, transcendentals=0),
    )(x, *tokens)


def mean_entries(*entries):
    total = sum(e.astype(F32) for e in entries)
    return (total * (1.0 / len(entries))).astype(BF16)


def shards(queries, keys_values, out_weight):
    n_lat = lax.axis_size("lat")
    width = queries.shape[-1]
    def like(*shape):
        return jax.ShapeDtypeStruct(shape, BF16)

    pack = 2 * SPAN + 4
    q_edge, q_inner, edge_own, inner_own, pooled = pl.pallas_call(
        split_kernel,
        out_shape=[
            like(SPAN, width),
            like(SPAN, width),
            like(pack, width),
            like(2 * SPAN, width),
            like(4, width),
        ],
        in_specs=[pl.BlockSpec(memory_space=pltpu.HBM)] * 2,
        out_specs=[VMEM] * 5,
        scratch_shapes=[
            pltpu.VMEM(queries.shape, BF16),
            pltpu.VMEM(keys_values.shape, BF16),
            pltpu.SemaphoreType.DMA((3,)),
        ],
        name="split",
        compiler_params=pltpu.CompilerParams(vmem_limit_bytes=LIMIT),
        cost_estimate=pl.CostEstimate(flops=0, bytes_accessed=2 << 20, transcendentals=0),
    )(*(pltpu.with_memory_space_constraint(x, pltpu.HBM) for x in (queries, keys_values)))
    edge_pair = swap(edge_own, "lat", 1)
    far_q_edge = outward(q_edge, "lon")
    far_q_inner = swap(q_inner, "lon", 1)
    inner_pair = swap(inner_own, "lat", 1)
    inner_hop = stride(inner_own, "lat", -2)
    pooled = after(pooled, weight=4 * WEIGHT)
    edge_pair = after(edge_pair, pooled, far_q_edge, inner_hop)
    edge_far = stride(edge_pair, "lat", 2)
    inner_far = swap(inner_hop, "lat", 1)
    level0 = pooled.reshape(2, 2, width)
    level0_lat = edge_pair[2 * SPAN :].reshape(2, 2, width)
    mine = mean_entries(level0[:, 0:1], level0[:, 1:2], level0_lat[:, 0:1], level0_lat[:, 1:2])
    beside = swap(jnp.concatenate([level0, level0_lat, mine], axis=1), "lon", 1)
    group = jnp.concatenate([mine, beside[:, 4:5]], axis=1)
    group_lon = swap(group, "lon", 2)
    group_both = jnp.concatenate([group, group_lon], axis=1)
    group_both = after(group_both, inner_pair, far_q_inner)
    edge_far = after(edge_far, group_both)

    back = jax.ShapeDtypeStruct((SPAN, width + HEAD_DIM), BF16)
    flops = 4 * SPAN * 3 * SPAN * width
    edge_part = call(
        functools.partial(partial_kernel, n_lat),
        [back],
        "edge_part",
        flops,
        far_q_edge,
        edge_own,
        edge_pair,
        edge_far,
    )[0]
    edge_back = outward(edge_part, "lon")
    group_lat = swap(after(group_both, edge_part), "lat", 2)
    coarse = jnp.concatenate([level0_lat, beside[:, 0:4], group_lon, group_lat], axis=1)
    count = coarse.shape[1] // 2
    coarse = jnp.pad(coarse, ((0, 0), (0, 16 - 2 * count), (0, 0)))
    inner_far = after(inner_far, edge_part)
    inner_part = call(
        functools.partial(partial_kernel, n_lat),
        [back],
        "inner_part",
        flops,
        far_q_inner,
        inner_own,
        inner_pair,
        inner_far,
    )[0]
    inner_back = swap(inner_part, "lon", 1)
    coarse = after(coarse, inner_part)
    own, lse = call(
        functools.partial(own_kernel, n_lat, count),
        [
            jax.ShapeDtypeStruct((2 * SPAN, width), F32),
            jax.ShapeDtypeStruct((2 * SPAN, HEAD_DIM), F32),
        ],
        "own_part",
        4 * flops,
        edge_own,
        inner_own,
        edge_pair,
        inner_pair,
        edge_far,
        inner_far,
        q_inner,
        q_edge,
        coarse,
    )
    edge_back = after(edge_back, own, weight=4 * WEIGHT)
    return call(
        merge_kernel,
        [jax.ShapeDtypeStruct(queries.shape, BF16)],
        "merge",
        4 * SPAN * width * width,
        own,
        lse,
        edge_back,
        inner_back,
        out_weight,
    )[0]


def solution(mesh):
    return jax.shard_map(
        shards,
        mesh=mesh,
        in_specs=(P("lat", "lon", None), P(None, "lat", "lon", None), P()),
        out_specs=P("lat", "lon", None),
        check_vma=False,
    )
```
